32 devices in a mesh: dp: 16 (over z, y, core), mp: 2 (over x).
Axes of the slice: x: 2, y: 2, z: 4, core: 2. Of those that a mesh axis runs over, the one named last changes fastest.
Arguments:
- tokens: bfloat16 [65536, 512], P(('dp', 'mp')), may hold values from -6 to 6
- out_grad: bfloat16 [65536, 512], P(('dp', 'mp')), may hold values from -6 to 6
- patch_valid: int32 [64, 256], P('dp'), may hold values 0 or 1
- clip_ids: int32 [64, 4], P('dp'), may hold values from 0 to 3, as said below
- ln_gain: float32 [2, 2, 512], replicated, may hold values from 0.1 to 1.9
- ln_bias: float32 [2, 2, 512], replicated, may hold values from -2 to 2
- w_qkv: bfloat16 [2, 512, 1536], P(None, None, 'mp'), may hold values from -0.25 to 0.25
- w_out: bfloat16 [2, 512, 512], P(None, 'mp'), may hold values from -0.5 to 0.5
- w_up: bfloat16 [2, 512, 2048], P(None, None, 'mp'), may hold values from -0.25 to 0.25
- w_down: bfloat16 [2, 2048, 512], P(None, 'mp'), may hold values from -0.125 to 0.125
Outputs:
- layer_out: bfloat16 [65536, 512], P(('dp', 'mp'))
- input_grad: float32 [65536, 512], P(('dp', 'mp'))
- grad_ln_gain: float32 [2, 2, 512], replicated
- grad_ln_bias: float32 [2, 2, 512], replicated
- grad_w_qkv: float32 [2, 512, 1536], P(None, None, 'mp')
- grad_w_out: float32 [2, 512, 512], P(None, 'mp')
- grad_w_up: float32 [2, 512, 2048], P(None, None, 'mp')
- grad_w_down: float32 [2, 2048, 512], P(None, 'mp')
The draws below stay inside these ranges and needn't reach their ends.
Inputs may be any that keep to these rules, and one draw needn't show every extreme that they name: `clip_ids`: each stream's clip numbers start at 0 and rise by 0 or 1 from one frame slot to the next.
All inputs are finite; a program needn't handle non-finite values. No bound on the sum of `patch_valid` on one device may be relied on, other than what follows from the above.
Results may differ from the reference program's by a relative error of at most 0.025.
Values may be sent and summed in bfloat16 or wider, within the bound.
No kernel may reach another device: no remote copies, remote signals or barrier semaphores. Data moves between devices by JAX's collectives and lax.ppermute only.
A program may use at most 384 MiB of HBM per device.

```python
import jax
import jax.numpy as jnp
from jax import lax

D = 512
HEADS = 8
HEAD_DIM = 64
FF = 2048
FRAMES = 4
PATCHES = 256
STREAMS_DEV = 4
STREAMS = 64
TOKENS = 65536
N_DP = 16


def draw_clip_ids(key, part):
    rises = jax.random.randint(jax.random.fold_in(key, 11), (STREAMS, FRAMES), 0, 2)
    chosen = jax.random.randint(jax.random.fold_in(key, 12), (), 0, STREAMS)
    column = jnp.arange(FRAMES)[None, :]
    row_index = jnp.arange(STREAMS)[:, None]
    rises = jnp.where((row_index == chosen) & (column > 0), 1, rises)
    rises = jnp.where(column == 0, 0, rises)
    return jnp.cumsum(rises, axis=1).astype(jnp.int32)


def with_ends(entries, key, low, high):
    longest = entries.shape.index(max(entries.shape))
    spots = []
    for shift in (0, 1):
        where = [jax.random.randint(jax.random.fold_in(key, axis), (), 0, length) for axis, length in enumerate(entries.shape)]
        where[longest] = (where[longest] + shift) % entries.shape[longest]
        spots.append(tuple(where))
    return entries.at[spots[0]].set(low).at[spots[1]].set(high)


def shard_levels(key, extent, split, least, largest):
    def one(dim, shards_of):
        draws = jax.random.uniform(jax.random.fold_in(jax.random.fold_in(key, 6), dim), (shards_of,), jnp.float32, least / len(split), largest / len(split))
        return jnp.repeat(jnp.exp(draws), extent[dim] // shards_of).reshape((-1,) + (1,) * (len(extent) - dim - 1))

    gain = one(*split[0])
    for cut in split[1:]:
        gain = gain * one(*cut)
    return gain


def gaussian(own_key, extent, width, reach, cuts=(), held_as=jnp.bfloat16):
    array = jax.random.normal(own_key, extent, jnp.float32) * width
    if len(cuts) > 0:
        array = shard_levels(own_key, extent, cuts, -0.22, 0.18) * array
    return jnp.clip(array, min=-reach, max=reach).astype(held_as)


def setup_inputs(seed: int = 0) -> dict:
    key_of = jax.random.split(jax.random.key(seed), 11)
    tokens = gaussian(key_of[0], (TOKENS, D), 1.0, 6.0, ((0, 32),))
    out_grad = gaussian(key_of[1], (TOKENS, D), 1.0, 6.0, ((0, 32),))
    patch_valid = with_ends((jax.random.randint(key_of[2], (STREAMS, PATCHES), 0, 8) < 7).astype(jnp.int32), jax.random.fold_in(key_of[2], 1), 0, 1)
    clip_ids = draw_clip_ids(jax.random.fold_in(key_of[10], 71), 0)
    ln_gain = jnp.clip(1.0 + 0.18 * jax.random.normal(key_of[4], (2, 2, D), jnp.float32), 0.1, 1.9)
    ln_bias = gaussian(key_of[5], (2, 2, D), 0.3, 2.0, (), jnp.float32)
    w_qkv = gaussian(key_of[6], (2, D, 3 * D), D ** -0.5, 0.25, ((2, 2),))
    w_out = gaussian(key_of[7], (2, D, D), (D // 4) ** -0.5, 0.5, ((1, 2),))
    w_up = gaussian(key_of[8], (2, D, FF), D ** -0.5, 0.25, ((2, 2),))
    w_down = gaussian(key_of[9], (2, FF, D), FF ** -0.5, 0.125, ((1, 2),))
    return {"tokens": tokens, "out_grad": out_grad, "patch_valid": patch_valid, "clip_ids": clip_ids, "ln_gain": ln_gain, "ln_bias": ln_bias, "w_qkv": w_qkv, "w_out": w_out, "w_up": w_up, "w_down": w_down}


@jax.custom_vjp
def low(v):
    return lax.optimization_barrier(v.astype(jnp.bfloat16)).astype(jnp.float32)

@jax.custom_vjp
def low_back(v):
    return v

def low_keep(v):
    return (low(v), None)

def low_pass(kept, grad):
    return (grad,)

def back_keep(v):
    return (v, None)

def back_low(kept, grad):
    return (low(grad),)
low.defvjp(low_keep, low_pass)
low_back.defvjp(back_keep, back_low)
HIGHEST = lax.Precision.HIGHEST
SPATIAL_FORMS = ('sfphe,sfqhe->sfhpq', 'sfhpq,sfqhe->sfphe')
TEMPORAL_FORMS = ('sfphe,sgphe->sphfg', 'sphfg,sgphe->sfphe')

def layer_norm(values, ln_gain, ln_bias):
    centre = values - lax.optimization_barrier(jnp.mean(values, axis=-1, keepdims=True))
    spread = lax.optimization_barrier(jnp.mean(centre * centre, axis=-1, keepdims=True))
    return centre * lax.rsqrt(spread + 1e-05) * ln_gain + ln_bias

def mask_biases(patch_valid, clip_ids):
    space_bias = jnp.where(patch_valid == 1, 0.0, -1000000000.0).astype(jnp.float32)[:, None, None, None, :]
    frame_row = jnp.arange(FRAMES)[:, None]
    frame_col = jnp.arange(FRAMES)[None, :]
    allowed = (clip_ids[:, :, None] == clip_ids[:, None, :]) & (frame_col <= frame_row)
    time_bias = jnp.where(allowed, 0.0, -1000000000.0).astype(jnp.float32)[:, None, None, :, :]
    return (space_bias, time_bias)

def attend(normed, w_qkv, w_out, mask_bias, einsum_forms):
    streams = mask_bias.shape[0]
    projected = low_back(low(jnp.dot(normed, w_qkv, precision=HIGHEST, preferred_element_type=jnp.float32)))
    projected = projected.reshape(streams, FRAMES, PATCHES, HEADS, 3, HEAD_DIM)
    queries = projected[..., 0, :]
    key_rows = projected[..., 1, :]
    value_rows = projected[..., 2, :]
    scores = jnp.einsum(einsum_forms[0], queries, key_rows, precision=HIGHEST) * HEAD_DIM ** (-0.5) + mask_bias
    scores = low_back(scores)
    top_score = lax.optimization_barrier(jnp.max(scores, axis=-1, keepdims=True))
    exponent = jnp.exp(scores - top_score)
    weights = low(exponent / lax.optimization_barrier(jnp.sum(exponent, axis=-1, keepdims=True)))
    mixed_heads = jnp.einsum(einsum_forms[1], weights, value_rows, precision=HIGHEST)
    mixed_heads = low_back(low(mixed_heads)).reshape(-1, HEADS * HEAD_DIM)
    return jnp.dot(mixed_heads, w_out, precision=HIGHEST, preferred_element_type=jnp.float32)

def block(stream_in, ln_gain, ln_bias, w_qkv, w_out, w_up, w_down, mask_bias, einsum_forms):
    normed = low(layer_norm(stream_in, ln_gain[0], ln_bias[0]))
    middle = stream_in + low_back(attend(normed, w_qkv, w_out, mask_bias, einsum_forms))
    second = low(layer_norm(middle, ln_gain[1], ln_bias[1]))
    hidden_pre = low_back(jnp.dot(second, w_up, precision=HIGHEST, preferred_element_type=jnp.float32))
    activated = low(jax.nn.gelu(hidden_pre))
    return middle + low_back(jnp.dot(activated, w_down, precision=HIGHEST, preferred_element_type=jnp.float32))

def whole_layer(tokens, ln_gain, ln_bias, w_qkv, w_out, w_up, w_down, space_bias, time_bias):
    first = block(tokens, ln_gain[0], ln_bias[0], w_qkv[0], w_out[0], w_up[0], w_down[0], space_bias, SPATIAL_FORMS)
    return block(first, ln_gain[1], ln_bias[1], w_qkv[1], w_out[1], w_up[1], w_down[1], time_bias, TEMPORAL_FORMS)

def reference(tokens, out_grad, patch_valid, clip_ids, ln_gain, ln_bias, w_qkv, w_out, w_up, w_down):
    params = (ln_gain.astype(jnp.float32), ln_bias.astype(jnp.float32), w_qkv.astype(jnp.float32), w_out.astype(jnp.float32), w_up.astype(jnp.float32), w_down.astype(jnp.float32))
    group_tokens = STREAMS_DEV * FRAMES * PATCHES
    token_groups = tokens.astype(jnp.float32).reshape(N_DP, group_tokens, D)
    grad_groups = out_grad.astype(jnp.float32).reshape(N_DP, group_tokens, D)
    space_bias, time_bias = mask_biases(patch_valid, clip_ids)
    space_groups = space_bias.reshape((N_DP, STREAMS_DEV) + space_bias.shape[1:])
    time_groups = time_bias.reshape((N_DP, STREAMS_DEV) + time_bias.shape[1:])

    def one_group(totals, inputs):
        group_in, cotangent, space_part, time_part = inputs

        def forward(group_values, gains, shifts, qkv_weight, out_weight, up_weight, down_weight):
            return whole_layer(group_values, gains, shifts, qkv_weight, out_weight, up_weight, down_weight, space_part, time_part)
        result, pull = jax.vjp(forward, group_in, *params)
        grads = pull(cotangent)
        totals = tuple((total + grad for total, grad in zip(totals, grads[1:])))
        return (totals, (result.astype(jnp.bfloat16), grads[0]))
    zeros = tuple((jnp.zeros_like(param) for param in params))
    totals, outputs = lax.scan(one_group, zeros, (token_groups, grad_groups, space_groups, time_groups))
    layer_out = outputs[0].reshape(TOKENS, D)
    input_grad = outputs[1].reshape(TOKENS, D)
    return (layer_out, input_grad, totals[0], totals[1], totals[2], totals[3], totals[4], totals[5])
```

```python
import functools

import jax
import jax.numpy as jnp
from jax import lax
from jax.experimental import pallas as pl
from jax.experimental.pallas import tpu as pltpu
from jax.sharding import Mesh
from jax.sharding import PartitionSpec as P

HEAD_DIM = 64
FRAMES = 4
EPS = 1e-05
SCALE = HEAD_DIM ** (-0.5)
F32 = jnp.float32
BF = jnp.bfloat16
VMEM_BYTES = 56 * 2**20
SWAP = [(0, 1), (1, 0)]


def nn(a, b):
    return lax.dot_general(a, b, (((1,), (0,)), ((), ())), preferred_element_type=F32)


def nt(a, b):
    return lax.dot_general(a, b, (((1,), (1,)), ((), ())), preferred_element_type=F32)


def tn(a, b):
    return lax.dot_general(a, b, (((0,), (0,)), ((), ())), preferred_element_type=F32)


def cat(ref):
    return jnp.concatenate([ref[i] for i in range(ref.shape[0])], axis=1)


def put(ref, values):
    width = ref.shape[-1]
    for i in range(ref.shape[0]):
        ref[i] = values[:, i * width : (i + 1) * width].astype(ref.dtype)


def centred(values):
    centre = values - jnp.mean(values, axis=0, keepdims=True)
    rstd = lax.rsqrt(jnp.mean(centre * centre, axis=0, keepdims=True) + EPS)
    return centre * rstd, rstd


def norm_back(values, gain, grad, sums):
    hat, rstd = centred(values)
    scaled = grad * hat
    for k in range(values.shape[1] // 128):
        sums[0] += scaled[:, k * 128 : (k + 1) * 128]
        sums[1] += grad[:, k * 128 : (k + 1) * 128]
    inner = grad * gain
    return rstd * (
        inner
        - jnp.mean(inner, axis=0, keepdims=True)
        - hat * jnp.mean(inner * hat, axis=0, keepdims=True)
    )


def put_sums(ref, sums):
    ref[0:1, :] = jnp.sum(sums[0].T, axis=0, keepdims=True)
    ref[1:2, :] = jnp.sum(sums[1].T, axis=0, keepdims=True)


def gelu_pair(u):
    c0, c1 = 0.7978845608028654, 0.044715
    square = u * u
    tanh = jnp.tanh(u * (c0 + (c0 * c1) * square))
    half = 0.5 + 0.5 * tanh
    slope = half + (0.5 * u) * (1.0 - tanh * tanh) * (c0 + (3 * c0 * c1) * square)
    return u * half, slope


def quarter(place, index):
    return (place[0] ^ (index // 2)) * 2 + (place[1] ^ (index % 2))


def weight_copies(place, layer, by_rows, mine, pieces, held, sem):
    rows, cols = mine.shape[1], mine.shape[2]
    part = rows // 4
    if by_rows:
        copies = [pltpu.make_async_copy(mine.at[layer], held.at[0:rows, :], sem.at[0])]
    else:
        copies = [pltpu.make_async_copy(mine.at[layer], held.at[:, 0:cols], sem.at[0])]
    for index, piece in enumerate(pieces):
        if by_rows:
            start = pl.multiple_of(rows + quarter(place, index) * part, part)
            target = held.at[pl.ds(start, part), :]
        else:
            start = pl.multiple_of(quarter(place, index) * part, part)
            target = held.at[pl.ds(start, part), cols : 2 * cols]
        copies.append(pltpu.make_async_copy(piece, target, sem.at[1 + index]))
    return copies


def put_grads(place, by_rows, total, keep, send):
    part, cols = keep.shape[2], keep.shape[3]
    for dx in range(2):
        for index in range(4):
            start = quarter(place, index) * part
            if by_rows:
                start = pl.multiple_of(dx * 4 * part + start, part)
                values = total[pl.ds(start, part), :]
            else:
                start = pl.multiple_of(start, part)
                values = total[pl.ds(start, part), dx * cols : (dx + 1) * cols]
            target = send if index % 2 else keep
            target[dx, index // 2] = values.astype(BF)


def spatial_forward_kernel(
    layer, place, x_ref, bias_ref, norm_ref, wq, q0, q1, q2, q3, wo, o0, o1, o2, o3,
    p_ref, o_ref, r_ref, a2_ref, stat_ref, wq_v, wo_v, sem_q, sem_o,
):
    @pl.when(pl.program_id(0) == 0)
    def _():
        copies = weight_copies(place, layer, False, wq, (q0, q1, q2, q3), wq_v, sem_q)
        copies += weight_copies(place, layer, True, wo, (o0, o1, o2, o3), wo_v, sem_o)
        for copy in copies:
            copy.start()
        for copy in copies:
            copy.wait()

    x = x_ref[...].astype(F32).T
    hat, _ = centred(x)
    a = (hat * norm_ref[:, 0:1] + norm_ref[:, 1:2]).astype(BF)
    put(p_ref, tn(wq_v[...], a))
    heads = wq_v.shape[1] // (3 * HEAD_DIM)
    for frame in range(p_ref.shape[0]):
        bias = bias_ref[0]

        def one_head(h, _):
            base = pl.multiple_of(h * 3 * HEAD_DIM, HEAD_DIM)
            q = p_ref[frame, pl.ds(base, HEAD_DIM), :] * SCALE
            k = p_ref[frame, pl.ds(base + HEAD_DIM, HEAD_DIM), :]
            v = p_ref[frame, pl.ds(base + 2 * HEAD_DIM, HEAD_DIM), :]
            s = tn(k, q.astype(BF)) + bias
            top = jnp.max(s, axis=0, keepdims=True)
            e = jnp.exp(s - top)
            inverse = 1.0 / jnp.sum(e, axis=0, keepdims=True)
            stat_ref[frame, pl.ds(h, 1), :] = top
            stat_ref[frame, pl.ds(heads + h, 1), :] = inverse
            o = nn(v, (e * inverse).astype(BF))
            o_ref[frame, pl.ds(pl.multiple_of(h * HEAD_DIM, HEAD_DIM), HEAD_DIM), :] = (
                o.astype(BF)
            )
            return 0

        lax.fori_loop(0, heads, one_head, 0, unroll=2)
    r = x + tn(wo_v[...], cat(o_ref))
    put(r_ref, r)
    hat, _ = centred(r)
    put(a2_ref, hat * norm_ref[:, 2:3] + norm_ref[:, 3:4])


def mlp_forward_kernel(
    layer, chunk, place, r_ref, a2_ref, wu, u0, u1, u2, u3, wd, d0, d1, d2, d3,
    x_ref, g_ref, slope_ref, total, wu_v, wd_v, sem_u, sem_d,
):
    @pl.when(pl.program_id(0) == 0)
    def _():
        copies = weight_copies(place, layer, False, wu, (u0, u1, u2, u3), wu_v, sem_u)
        copies += weight_copies(place, layer, True, wd, (d0, d1, d2, d3), wd_v, sem_d)
        for copy in copies:
            copy.start()
        for copy in copies:
            copy.wait()

    a2 = cat(a2_ref)
    total[...] = cat(r_ref)

    def step(j, _):
        for part in range(2):
            here = pl.ds(pl.multiple_of((2 * j + part) * chunk, chunk), chunk)
            g, slope = gelu_pair(tn(wu_v[:, here], a2))
            g = g.astype(BF)
            g_ref[0, here, :] = g
            slope_ref[0, here, :] = slope.astype(BF)
            total[...] += tn(wd_v[here, :], g)
        return 0

    lax.fori_loop(0, wu_v.shape[1] // (2 * chunk), step, 0)
    put(x_ref, total[...])


def temporal_weights(p_ref, h, clip_ref, stream):
    base = pl.multiple_of(h * 3 * HEAD_DIM, HEAD_DIM)
    take = lambda f, c: p_ref[f, pl.ds(base + c * HEAD_DIM, HEAD_DIM), :].astype(F32)
    q = [take(f, 0) for f in range(FRAMES)]
    k = [take(f, 1) for f in range(FRAMES)]
    v = [take(f, 2) for f in range(FRAMES)]
    weights = []
    for f in range(FRAMES):
        scores = []
        for g in range(f + 1):
            bias = jnp.where(clip_ref[stream, g] == clip_ref[stream, f], 0.0, -1000000000.0)
            scores.append(jnp.sum(q[f] * k[g], axis=0, keepdims=True) * SCALE + bias)
        top = functools.reduce(jnp.maximum, scores)
        e = [jnp.exp(s - top) for s in scores]
        inverse = 1.0 / functools.reduce(jnp.add, e)
        weights.append([x * inverse for x in e])
    return q, k, v, weights


def low(v):
    return v.astype(BF).astype(F32)


def temporal_forward_kernel(
    layer, place, clip_ref, x_ref, norm_ref, wq, q0, q1, q2, q3, wo, o0, o1, o2, o3,
    p_ref, o_ref, r_ref, a2_ref, wq_v, wo_v, sem_q, sem_o,
):
    @pl.when((pl.program_id(0) == 0) & (pl.program_id(1) == 0))
    def _():
        copies = weight_copies(place, layer, False, wq, (q0, q1, q2, q3), wq_v, sem_q)
        copies += weight_copies(place, layer, True, wo, (o0, o1, o2, o3), wo_v, sem_o)
        for copy in copies:
            copy.start()
        for copy in copies:
            copy.wait()

    stream = pl.program_id(0)
    x = cat(x_ref)
    hat, _ = centred(x)
    a = (hat * norm_ref[:, 4:5] + norm_ref[:, 5:6]).astype(BF)
    put(p_ref, tn(wq_v[...], a))
    heads = wq_v.shape[1] // (3 * HEAD_DIM)

    def one_head(h, _):
        _, _, v, weights = temporal_weights(p_ref, h, clip_ref, stream)
        rows = pl.ds(pl.multiple_of(h * HEAD_DIM, HEAD_DIM), HEAD_DIM)
        for f in range(FRAMES):
            o = functools.reduce(jnp.add, [low(w) * v[g] for g, w in enumerate(weights[f])])
            o_ref[f, rows, :] = o.astype(BF)
        return 0

    lax.fori_loop(0, heads, one_head, 0)
    r = x + tn(wo_v[...], cat(o_ref))
    put(r_ref, r)
    hat, _ = centred(r)
    put(a2_ref, hat * norm_ref[:, 6:7] + norm_ref[:, 7:8])


def mlp_both_kernel(
    layer, chunk, place, r_ref, a2_ref, y_ref, norm_ref, wu, u0, u1, u2, u3, wd, d0, d1, d2, d3,
    out_ref, dr_ref, ku_ref, su_ref, kd_ref, sd_ref, ln_ref,
    total, back, gu, gd, sums, wu_v, wd_v, sem_u, sem_d,
):
    @pl.when(pl.program_id(0) == 0)
    def _():
        copies = weight_copies(place, layer, False, wu, (u0, u1, u2, u3), wu_v, sem_u)
        copies += weight_copies(place, layer, True, wd, (d0, d1, d2, d3), wd_v, sem_d)
        for copy in copies:
            copy.start()
        gu[...] = jnp.zeros_like(gu)
        gd[...] = jnp.zeros_like(gd)
        sums[...] = jnp.zeros_like(sums)
        for copy in copies:
            copy.wait()

    a2 = cat(a2_ref)
    dm = y_ref[...].T
    total[...] = cat(r_ref)
    back[...] = jnp.zeros_like(back)

    def step(j, _):
        for part in range(2):
            here = pl.ds(pl.multiple_of((2 * j + part) * chunk, chunk), chunk)
            g, slope = gelu_pair(tn(wu_v[:, here], a2))
            g = g.astype(BF)
            du = (nn(wd_v[here, :], dm) * slope).astype(BF)
            total[...] += tn(wd_v[here, :], g)
            gd[here, :] += nt(g, dm)
            gu[:, here] += nt(a2, du)
            back[...] += nn(wu_v[:, here], du)
        return 0

    lax.fori_loop(0, wu_v.shape[1] // (2 * chunk), step, 0)
    out_ref[...] = total[...].astype(BF).T
    put(dr_ref, dm.astype(F32) + norm_back(cat(r_ref), norm_ref[:, 6:7], back[...], sums))

    @pl.when(pl.program_id(0) == pl.num_programs(0) - 1)
    def _():
        put_grads(place, False, gu, ku_ref, su_ref)
        put_grads(place, True, gd, kd_ref, sd_ref)
        put_sums(ln_ref, sums)


def mlp_back_kernel(
    layer, chunk, place, r_ref, a2_ref, y_ref, g_ref, slope_ref, norm_ref,
    wu, u0, u1, u2, u3, wd, d0, d1, d2, d3,
    dr_ref, ku_ref, su_ref, kd_ref, sd_ref, ln_ref,
    back, gu, gd, sums, wu_v, wd_v, sem_u, sem_d,
):
    @pl.when(pl.program_id(0) == 0)
    def _():
        copies = weight_copies(place, layer, False, wu, (u0, u1, u2, u3), wu_v, sem_u)
        copies += weight_copies(place, layer, True, wd, (d0, d1, d2, d3), wd_v, sem_d)
        for copy in copies:
            copy.start()
        gu[...] = jnp.zeros_like(gu)
        gd[...] = jnp.zeros_like(gd)
        sums[...] = jnp.zeros_like(sums)
        for copy in copies:
            copy.wait()

    a2 = cat(a2_ref)
    dm = cat(y_ref).astype(BF)
    back[...] = jnp.zeros_like(back)

    def step(j, _):
        for part in range(2):
            here = pl.ds(pl.multiple_of((2 * j + part) * chunk, chunk), chunk)
            du = (nn(wd_v[here, :], dm) * slope_ref[0, here, :].astype(F32)).astype(BF)
            gd[here, :] += nt(g_ref[0, here, :], dm)
            gu[:, here] += nt(a2, du)
            back[...] += nn(wu_v[:, here], du)
        return 0

    lax.fori_loop(0, wu_v.shape[1] // (2 * chunk), step, 0)
    put(dr_ref, cat(y_ref) + norm_back(cat(r_ref), norm_ref[:, 2:3], back[...], sums))

    @pl.when(pl.program_id(0) == pl.num_programs(0) - 1)
    def _():
        put_grads(place, False, gu, ku_ref, su_ref)
        put_grads(place, True, gd, kd_ref, sd_ref)
        put_sums(ln_ref, sums)


def temporal_back_kernel(
    layer, place, clip_ref, x_ref, y_ref, p_ref, o_ref, norm_ref,
    wq, q0, q1, q2, q3, wo, o0, o1, o2, o3,
    dx_ref, kq_ref, sq_ref, ko_ref, so_ref, ln_ref,
    gq, go, sums, do_v, dp_v, wq_v, wo_v, sem_q, sem_o,
):
    first = (pl.program_id(0) == 0) & (pl.program_id(1) == 0)
    last = (pl.program_id(0) == pl.num_programs(0) - 1) & (
        pl.program_id(1) == pl.num_programs(1) - 1
    )

    @pl.when(first)
    def _():
        copies = weight_copies(place, layer, False, wq, (q0, q1, q2, q3), wq_v, sem_q)
        copies += weight_copies(place, layer, True, wo, (o0, o1, o2, o3), wo_v, sem_o)
        for copy in copies:
            copy.start()
        gq[...] = jnp.zeros_like(gq)
        go[...] = jnp.zeros_like(go)
        sums[...] = jnp.zeros_like(sums)
        for copy in copies:
            copy.wait()

    stream = pl.program_id(0)
    da = cat(y_ref).astype(BF)
    go[...] += nt(cat(o_ref), da)
    put(do_v, nn(wo_v[...], da))
    heads = wq_v.shape[1] // (3 * HEAD_DIM)

    def one_head(h, _):
        q, k, v, weights = temporal_weights(p_ref, h, clip_ref, stream)
        base = pl.multiple_of(h * 3 * HEAD_DIM, HEAD_DIM)
        rows = pl.ds(pl.multiple_of(h * HEAD_DIM, HEAD_DIM), HEAD_DIM)
        do = [do_v[f, rows, :].astype(F32) for f in range(FRAMES)]
        dk = [0.0] * FRAMES
        dv = [0.0] * FRAMES
        for f in range(FRAMES):
            dw = [jnp.sum(do[f] * v[g], axis=0, keepdims=True) for g in range(f + 1)]
            inner = functools.reduce(jnp.add, [w * d for w, d in zip(weights[f], dw)])
            dq = 0.0
            for g in range(f + 1):
                ds = low(weights[f][g] * (dw[g] - inner)) * SCALE
                dq = dq + ds * k[g]
                dk[g] = dk[g] + ds * q[f]
                dv[g] = dv[g] + low(weights[f][g]) * do[f]
            dp_v[f, pl.ds(base, HEAD_DIM), :] = dq.astype(BF)
        for g in range(FRAMES):
            dp_v[g, pl.ds(base + HEAD_DIM, HEAD_DIM), :] = dk[g].astype(BF)
            dp_v[g, pl.ds(base + 2 * HEAD_DIM, HEAD_DIM), :] = dv[g].astype(BF)
        return 0

    lax.fori_loop(0, heads, one_head, 0)
    x = cat(x_ref)
    hat, _ = centred(x)
    a = (hat * norm_ref[:, 4:5] + norm_ref[:, 5:6]).astype(BF)
    dp = cat(dp_v)
    gq[...] += nt(a, dp)
    put(dx_ref, cat(y_ref) + norm_back(x, norm_ref[:, 4:5], nn(wq_v[...], dp), sums))

    @pl.when(last)
    def _():
        put_grads(place, False, gq, kq_ref, sq_ref)
        put_grads(place, True, go, ko_ref, so_ref)
        put_sums(ln_ref, sums)


def spatial_back_kernel(
    layer, place, x_ref, bias_ref, y_ref, p_ref, o_ref, stat_ref, norm_ref,
    wq, q0, q1, q2, q3, wo, o0, o1, o2, o3,
    dx_ref, kq_ref, sq_ref, ko_ref, so_ref, ln_ref,
    gq, go, sums, do_v, dp_v, wq_v, wo_v, sem_q, sem_o,
):
    @pl.when(pl.program_id(0) == 0)
    def _():
        copies = weight_copies(place, layer, False, wq, (q0, q1, q2, q3), wq_v, sem_q)
        copies += weight_copies(place, layer, True, wo, (o0, o1, o2, o3), wo_v, sem_o)
        for copy in copies:
            copy.start()
        gq[...] = jnp.zeros_like(gq)
        go[...] = jnp.zeros_like(go)
        sums[...] = jnp.zeros_like(sums)
        for copy in copies:
            copy.wait()

    da = cat(y_ref).astype(BF)
    go[...] += nt(cat(o_ref), da)
    put(do_v, nn(wo_v[...], da))
    heads = wq_v.shape[1] // (3 * HEAD_DIM)
    for frame in range(p_ref.shape[0]):
        bias = bias_ref[0]

        def one_head(h, _):
            base = pl.multiple_of(h * 3 * HEAD_DIM, HEAD_DIM)
            q = (p_ref[frame, pl.ds(base, HEAD_DIM), :] * SCALE).astype(BF)
            k = p_ref[frame, pl.ds(base + HEAD_DIM, HEAD_DIM), :]
            v = p_ref[frame, pl.ds(base + 2 * HEAD_DIM, HEAD_DIM), :]
            do = do_v[frame, pl.ds(pl.multiple_of(h * HEAD_DIM, HEAD_DIM), HEAD_DIM), :]
            top = stat_ref[frame, pl.ds(h, 1), :]
            inverse = stat_ref[frame, pl.ds(heads + h, 1), :]
            w = jnp.exp(tn(k, q) + bias - top) * inverse
            dw = tn(v, do)
            inner = jnp.sum(w * dw, axis=0, keepdims=True)
            ds = (w * (dw - inner)).astype(BF)
            dq = nn(k, ds) * SCALE
            dp_v[frame, pl.ds(base, HEAD_DIM), :] = dq.astype(BF)
            dp_v[frame, pl.ds(base + HEAD_DIM, HEAD_DIM), :] = nt(q, ds).astype(BF)
            dp_v[frame, pl.ds(base + 2 * HEAD_DIM, HEAD_DIM), :] = nt(do, w.astype(BF)).astype(BF)
            return 0

        lax.fori_loop(0, heads, one_head, 0, unroll=2)
    x = x_ref[...].astype(F32).T
    hat, _ = centred(x)
    a = (hat * norm_ref[:, 0:1] + norm_ref[:, 1:2]).astype(BF)
    dp = cat(dp_v)
    gq[...] += nt(a, dp)
    dx = cat(y_ref) + norm_back(x, norm_ref[:, 0:1], nn(wq_v[...], dp), sums)
    dx_ref[...] = dx.T

    @pl.when(pl.program_id(0) == pl.num_programs(0) - 1)
    def _():
        put_grads(place, False, gq, kq_ref, sq_ref)
        put_grads(place, True, go, ko_ref, so_ref)
        put_sums(ln_ref, sums)


ANY = pl.BlockSpec(memory_space=pl.ANY)
SMEM = pl.BlockSpec(memory_space=pltpu.SMEM)


def whole(shape):
    zeros = (0,) * len(shape)
    return pl.BlockSpec(shape, lambda *_: zeros, pipeline_mode=pl.Buffered(1))


def call(body, name, grid, ins, outs, scratch, cost):
    flops, exps = cost
    moved = sum(a.size * a.dtype.itemsize for a, _ in ins)
    shapes = [jax.ShapeDtypeStruct(shape, dtype) for shape, dtype, _ in outs]
    moved += sum(s.size * s.dtype.itemsize for s in shapes)
    return pl.pallas_call(
        body,
        grid=grid,
        in_specs=[spec for _, spec in ins],
        out_specs=[spec for _, _, spec in outs],
        out_shape=shapes,
        scratch_shapes=scratch,
        compiler_params=pltpu.CompilerParams(
            vmem_limit_bytes=VMEM_BYTES, dimension_semantics=("arbitrary",) * len(grid)
        ),
        cost_estimate=pl.CostEstimate(
            flops=int(flops), transcendentals=int(exps), bytes_accessed=int(moved)
        ),
        name=name,
    )(*[a for a, _ in ins])


def weight_ins(mine, pieces):
    return [(mine, ANY)] + [(piece, ANY) for piece in pieces]


def held(mine, by_rows):
    rows, cols = mine.shape[1:]
    return pltpu.VMEM((2 * rows, cols) if by_rows else (rows, 2 * cols), BF)


def held_grad(mine, by_rows):
    rows, cols = mine.shape[1:]
    return pltpu.VMEM((2 * rows, cols) if by_rows else (rows, 2 * cols), F32)


def grad_outs(mine):
    shape = (2, 2, mine.shape[1] // 4, mine.shape[2])
    return [(shape, BF, whole(shape))] * 2


SEMS = pltpu.SemaphoreType.DMA((5,))


def fetch(weight, layer, place):
    part = weight.shape[1] // 4
    start = (place[0] * 2 + place[1]) * part
    own = lax.dynamic_slice(weight, (layer, start, 0), (1, part, weight.shape[2]))[0]
    near = lax.ppermute(own, "mp", SWAP)
    side = lax.ppermute(near, "y", SWAP)
    return (
        near,
        lax.ppermute(near, "core", SWAP),
        side,
        lax.ppermute(side, "core", SWAP),
    )


def add(a, b):
    return (a.astype(F32) + b.astype(F32)).astype(a.dtype)


def over_z(value, z):
    inward = add(value, lax.ppermute(value, "z", [(0, 1), (3, 2)]))
    middle = add(inward, lax.ppermute(inward, "z", [(1, 2), (2, 1)]))
    outward = lax.ppermute(middle, "z", [(1, 0), (2, 3)])
    return jnp.where((z == 1) | (z == 2), middle, outward)


def reduce(keep, send, z):
    got = lax.ppermute(send, "core", SWAP)
    far = add(keep[1], got[1])
    near = (keep[0].astype(F32) + got[0].astype(F32)).astype(BF)
    near = add(near, lax.ppermute(far, "mp", SWAP))
    mine = over_z(add(near[0], lax.ppermute(near[1], "y", SWAP)), z)
    side = lax.ppermute(mine, "y", SWAP)
    return (mine, lax.ppermute(mine, "core", SWAP), side, lax.ppermute(side, "core", SWAP))


def reduce_small(value, z):
    for axis in ("core", "mp", "y"):
        value = value + lax.ppermute(value, axis, SWAP)
    return over_z(value, z)


def finish_kernel(place, *refs):
    pieces, outs = refs[:-2], refs[-2:]
    for t, out in enumerate(outs):
        part = out.shape[1] // 4
        for layer in range(2):
            for index in range(4):
                start = pl.multiple_of(quarter(place, index) * part, part)
                piece = pieces[t * 8 + layer * 4 + index]
                out[layer, pl.ds(start, part), :] = piece[...].astype(F32)


def finish(place, first, second, shapes):
    pieces = [p for pair in (first, second) for layer in pair for p in layer]
    ins = [(place, SMEM)] + [(p, whole(p.shape)) for p in pieces]
    outs = [(s, F32, whole(s)) for s in shapes]
    return call(finish_kernel, "finish", (1,), ins, outs, [], (0, 0))


def shards(tokens, out_grad, patch_valid, clip_ids, ln_gain, ln_bias, w_qkv, w_out, w_up, w_down):
    z, y, core, mp = (lax.axis_index(a) for a in ("z", "y", "core", "mp"))
    place = jnp.stack([y, core]).astype(jnp.int32)
    n, width = tokens.shape
    patches = patch_valid.shape[1]
    frames = n // patches
    streams = frames // FRAMES
    hidden = 2 * w_up.shape[2]
    heads = 2 * w_qkv.shape[2] // (3 * HEAD_DIM)
    qkv = 2 * w_qkv.shape[2]
    inner = 2 * w_out.shape[1]

    valid = lax.dynamic_slice(patch_valid, (mp * streams, 0), (streams, patches))
    bias = jnp.where(valid == 1, 0.0, -1000000000.0).astype(F32)[:, :, None]
    clips = lax.dynamic_slice(clip_ids, (mp * streams, 0), (streams, FRAMES))
    norms = jnp.stack([ln_gain, ln_bias], axis=2).reshape(8, width).T

    got = {}
    for layer in range(2):
        for name, weight in (("qkv", w_qkv), ("out", w_out), ("up", w_up), ("down", w_down)):
            got[name, layer] = fetch(weight, layer, (y, core))

    def attn_ins(layer):
        return weight_ins(w_qkv, got["qkv", layer]) + weight_ins(w_out, got["out", layer])

    def mlp_ins(layer):
        return weight_ins(w_up, got["up", layer]) + weight_ins(w_down, got["down", layer])

    attn_held = [held(w_qkv, False), held(w_out, True), SEMS, SEMS]
    mlp_held = [held(w_up, False), held(w_down, True), SEMS, SEMS]
    norm_in = (norms, whole(norms.shape))
    place_in = (place, SMEM)
    both = 2 if frames % 2 == 0 else 1
    span = both * patches
    tiles = frames // both
    chunk = min(512, hidden // 2)

    def rows(count, features):
        return pl.BlockSpec((count, features, patches), lambda i: (i, 0, 0))

    def columns(width_):
        return pl.BlockSpec((FRAMES, width_, 128), lambda i, j: (i, 0, j))

    token_rows = lambda count: pl.BlockSpec((count * patches, width), lambda i: (i, 0))
    act = lambda features: (frames, features, patches)
    bias_of = lambda count: pl.BlockSpec(
        (1, patches, 1), lambda i: (i * count // FRAMES, 0, 0)
    )
    ln_out = ((8, width), F32, whole((8, width)))
    spatial_flops = 4 * n * patches * inner
    attn_flops = 2 * n * width * (qkv + inner)
    mlp_flops = 4 * n * width * hidden

    p0, o0, r0, a0, stat0 = call(
        functools.partial(spatial_forward_kernel, 0), "spatial_forward", (tiles,),
        [place_in, (tokens, token_rows(both)), (bias, bias_of(both)), norm_in] + attn_ins(0),
        [(act(qkv), BF, rows(both, qkv)), (act(inner), BF, rows(both, inner)),
         (act(width), F32, rows(both, width)), (act(width), BF, rows(both, width)),
         (act(2 * heads), F32, rows(both, 2 * heads))],
        attn_held, (attn_flops + spatial_flops, n * patches * heads),
    )
    saved = (tiles, hidden, span)
    saved_spec = pl.BlockSpec((1, hidden, span), lambda i: (i, 0, 0))
    x1, g0, slope0 = call(
        functools.partial(mlp_forward_kernel, 0, chunk), "mlp_forward", (tiles,),
        [place_in, (r0, rows(both, width)), (a0, rows(both, width))] + mlp_ins(0),
        [(act(width), F32, rows(both, width)), (saved, BF, saved_spec), (saved, BF, saved_spec)],
        [pltpu.VMEM((width, span), F32)] + mlp_held, (mlp_flops, n * hidden),
    )

    clip_in = (clips, SMEM)
    grid1 = (streams, patches // 128)
    p1, o1, r1, a1 = call(
        functools.partial(temporal_forward_kernel, 1), "temporal_forward", grid1,
        [place_in, clip_in, (x1, columns(width)), norm_in] + attn_ins(1),
        [(act(qkv), BF, columns(qkv)), (act(inner), BF, columns(inner)),
         (act(width), F32, columns(width)), (act(width), BF, columns(width))],
        attn_held, (attn_flops * 1.2, 0),
    )
    layer_out, dr1, ku1, su1, kd1, sd1, ln11 = call(
        functools.partial(mlp_both_kernel, 1, chunk), "mlp_both", (tiles,),
        [place_in, (r1, rows(both, width)), (a1, rows(both, width)),
         (out_grad, token_rows(both)), norm_in] + mlp_ins(1),
        [((n, width), BF, token_rows(both)), (act(width), F32, rows(both, width))]
        + grad_outs(w_up) + grad_outs(w_down) + [ln_out],
        [pltpu.VMEM((width, span), F32), pltpu.VMEM((width, span), F32),
         held_grad(w_up, False), held_grad(w_down, True), pltpu.VMEM((2, width, 128), F32)]
        + mlp_held,
        (3 * mlp_flops, n * hidden),
    )
    up1 = reduce(ku1, su1, z)
    down1 = reduce(kd1, sd1, z)
    dx1, kq1, sq1, ko1, so1, ln10 = call(
        functools.partial(temporal_back_kernel, 1), "temporal_back", grid1,
        [place_in, clip_in, (x1, columns(width)), (dr1, columns(width)), (p1, columns(qkv)),
         (o1, columns(inner)), norm_in] + attn_ins(1),
        [(act(width), F32, columns(width))] + grad_outs(w_qkv) + grad_outs(w_out) + [ln_out],
        [held_grad(w_qkv, False), held_grad(w_out, True), pltpu.VMEM((2, width, 128), F32),
         pltpu.VMEM((FRAMES, inner, 128), BF), pltpu.VMEM((FRAMES, qkv, 128), BF)] + attn_held,
        (2.4 * attn_flops, 0),
    )
    qkv1 = reduce(kq1, sq1, z)
    out1 = reduce(ko1, so1, z)

    dr0, ku0, su0, kd0, sd0, ln01 = call(
        functools.partial(mlp_back_kernel, 0, chunk), "mlp_back", (tiles,),
        [place_in, (r0, rows(both, width)), (a0, rows(both, width)), (dx1, rows(both, width)),
         (g0, saved_spec), (slope0, saved_spec), norm_in] + mlp_ins(0),
        [(act(width), F32, rows(both, width))] + grad_outs(w_up) + grad_outs(w_down) + [ln_out],
        [pltpu.VMEM((width, span), F32), held_grad(w_up, False), held_grad(w_down, True),
         pltpu.VMEM((2, width, 128), F32)] + mlp_held,
        (2 * mlp_flops, 0),
    )
    up0 = reduce(ku0, su0, z)
    down0 = reduce(kd0, sd0, z)
    input_grad, kq0, sq0, ko0, so0, ln00 = call(
        functools.partial(spatial_back_kernel, 0), "spatial_back", (tiles,),
        [place_in, (tokens, token_rows(both)), (bias, bias_of(both)), (dr0, rows(both, width)),
         (p0, rows(both, qkv)), (o0, rows(both, inner)), (stat0, rows(both, 2 * heads)),
         norm_in] + attn_ins(0),
        [((n, width), F32, token_rows(both))] + grad_outs(w_qkv) + grad_outs(w_out) + [ln_out],
        [held_grad(w_qkv, False), held_grad(w_out, True), pltpu.VMEM((2, width, 128), F32),
         pltpu.VMEM((both, inner, patches), BF), pltpu.VMEM((both, qkv, patches), BF)]
        + attn_held,
        (2 * attn_flops + 2.5 * spatial_flops, n * patches * heads),
    )
    qkv0 = reduce(kq0, sq0, z)
    out0 = reduce(ko0, so0, z)

    small = reduce_small(jnp.stack([ln00[:2], ln01[:2], ln10[:2], ln11[:2]]), z)
    small = small.reshape(2, 2, 2, width)
    grad_up, grad_down = finish(place, (up0, up1), (down0, down1), (w_up.shape, w_down.shape))
    grad_qkv, grad_out = finish(place, (qkv0, qkv1), (out0, out1), (w_qkv.shape, w_out.shape))
    return (
        layer_out,
        input_grad,
        small[:, :, 0],
        small[:, :, 1],
        grad_qkv,
        grad_out,
        grad_up,
        grad_down,
    )


SPATIAL_FORMS = ("sfphe,sfqhe->sfhpq", "sfhpq,sfqhe->sfphe", "sfhpq,sfphe->sfqhe")
TEMPORAL_FORMS = ("sfphe,sgphe->sphfg", "sphfg,sgphe->sfphe", "sphfg,sfphe->sgphe")
ROWS_ONLY = (((0,), (0,)), ((), ()))
COLS_ONLY = (((1,), (1,)), ((), ()))


def layer_norm(values, ln_gain, ln_bias):
    centre = values - jnp.mean(values, axis=-1, keepdims=True)
    spread = jnp.mean(centre * centre, axis=-1, keepdims=True)
    return centre * lax.rsqrt(spread + 1e-05) * ln_gain + ln_bias


def mask_biases(patch_valid, clip_ids):
    space_bias = jnp.where(patch_valid == 1, 0.0, -1000000000.0).astype(jnp.float32)[
        :, None, None, None, :
    ]
    frame_row = jnp.arange(FRAMES)[:, None]
    frame_col = jnp.arange(FRAMES)[None, :]
    allowed = (clip_ids[:, :, None] == clip_ids[:, None, :]) & (frame_col <= frame_row)
    time_bias = jnp.where(allowed, 0.0, -1000000000.0).astype(jnp.float32)[:, None, None, :, :]
    return (space_bias, time_bias)


def norm_gather(normed):
    return lax.all_gather(normed, "mp", axis=0, tiled=True)


def grad_gather(grad_rows):
    return lax.all_gather(grad_rows, "mp", axis=0, tiled=True)


def branch_scatter(values_bf, weight):
    return lax.psum_scatter(
        jnp.dot(values_bf, weight, preferred_element_type=jnp.float32).astype(jnp.bfloat16),
        "mp",
        scatter_dimension=0,
        tiled=True,
    ).astype(jnp.float32)


def input_scatter(grads_bf, weight):
    return lax.psum_scatter(
        lax.dot_general(grads_bf, weight, COLS_ONLY, preferred_element_type=jnp.float32).astype(
            jnp.bfloat16
        ),
        "mp",
        scatter_dimension=0,
        tiled=True,
    ).astype(jnp.float32)


def weight_grad(stored, grads_bf):
    return lax.dot_general(stored, grads_bf, ROWS_ONLY, preferred_element_type=jnp.float32)


def split_heads(projected, streams, frames):
    heads_dev = projected.shape[1] // (3 * HEAD_DIM)
    split = projected.reshape(streams, frames, -1, heads_dev, 3, HEAD_DIM)
    return (split[..., 0, :], split[..., 1, :], split[..., 2, :], heads_dev)


def attend_forward(projected, mask_bias, einsum_forms, streams, frames):
    queries, key_rows, value_rows, heads_dev = split_heads(projected, streams, frames)
    scores = (
        jnp.einsum(einsum_forms[0], queries, key_rows, preferred_element_type=jnp.float32)
        * HEAD_DIM ** (-0.5)
        + mask_bias
    )
    top_score = jnp.max(scores, axis=-1, keepdims=True)
    exponent = jnp.exp(scores - top_score)
    total = jnp.sum(exponent, axis=-1, keepdims=True)
    weights = exponent / total
    log_total = top_score + jnp.log(total)
    mixed_heads = jnp.einsum(
        einsum_forms[1],
        weights.astype(jnp.bfloat16),
        value_rows,
        preferred_element_type=jnp.float32,
    )
    return (mixed_heads.astype(jnp.bfloat16).reshape(-1, heads_dev * HEAD_DIM), log_total)


def attend_backward(projected, log_total, heads_grad, mask_bias, einsum_forms, streams, frames):
    queries, key_rows, value_rows, heads_dev = split_heads(projected, streams, frames)
    grad_heads = heads_grad.reshape(streams, frames, -1, heads_dev, HEAD_DIM)
    scale = HEAD_DIM ** (-0.5)
    scores = (
        jnp.einsum(einsum_forms[0], queries, key_rows, preferred_element_type=jnp.float32) * scale
        + mask_bias
    )
    weights = jnp.exp(scores - log_total)
    weights_grad = jnp.einsum(
        einsum_forms[0], grad_heads, value_rows, preferred_element_type=jnp.float32
    )
    inner = jnp.sum(weights * weights_grad, axis=-1, keepdims=True)
    score_grad = (weights * (weights_grad - inner)).astype(jnp.bfloat16)
    query_grad = (
        jnp.einsum(einsum_forms[1], score_grad, key_rows, preferred_element_type=jnp.float32)
        * scale
    ).astype(jnp.bfloat16)
    key_grad = (
        jnp.einsum(einsum_forms[2], score_grad, queries, preferred_element_type=jnp.float32) * scale
    ).astype(jnp.bfloat16)
    value_grad = jnp.einsum(
        einsum_forms[2],
        weights.astype(jnp.bfloat16),
        grad_heads,
        preferred_element_type=jnp.float32,
    ).astype(jnp.bfloat16)
    return jnp.stack([query_grad, key_grad, value_grad], axis=-2).reshape(projected.shape)


def block_forward(
    stream_in,
    ln_gain,
    ln_bias,
    w_qkv,
    w_out,
    w_up,
    w_down,
    mask_bias,
    einsum_forms,
    streams,
    frames,
):
    normed = layer_norm(stream_in, ln_gain[0], ln_bias[0]).astype(jnp.bfloat16)
    full_rows = norm_gather(normed)
    projected = jnp.dot(full_rows, w_qkv, preferred_element_type=jnp.float32).astype(jnp.bfloat16)
    mixed_heads, log_total = attend_forward(projected, mask_bias, einsum_forms, streams, frames)
    middle = stream_in + branch_scatter(mixed_heads, w_out)
    second = layer_norm(middle, ln_gain[1], ln_bias[1]).astype(jnp.bfloat16)
    second_full = norm_gather(second)
    hidden_pre = jnp.dot(second_full, w_up, preferred_element_type=jnp.float32)
    activated = jax.nn.gelu(hidden_pre).astype(jnp.bfloat16)
    result = middle + branch_scatter(activated, w_down)
    kept = (
        stream_in,
        full_rows,
        projected,
        mixed_heads,
        log_total,
        middle,
        second_full,
        hidden_pre,
        activated,
    )
    return (result, kept)


def block_backward(
    result_grad,
    kept,
    ln_gain,
    ln_bias,
    w_qkv,
    w_out,
    w_up,
    w_down,
    mask_bias,
    einsum_forms,
    streams,
    frames,
):
    (
        stream_in,
        first_store,
        projected,
        mixed_heads,
        log_total,
        middle,
        second_store,
        hidden_pre,
        activated,
    ) = kept
    result_low = result_grad.astype(jnp.bfloat16)
    gelu_pull = jax.vjp(jax.nn.gelu, hidden_pre)[1]
    down_in = grad_gather(result_low)
    grad_down = lax.dot_general(activated, down_in, ROWS_ONLY, preferred_element_type=jnp.float32)
    act_grad = lax.dot_general(down_in, w_down, COLS_ONLY, preferred_element_type=jnp.float32)
    hidden_grad = gelu_pull(act_grad)[0].astype(jnp.bfloat16)
    grad_up = weight_grad(second_store, hidden_grad)
    second_grad = input_scatter(hidden_grad, w_up)
    second_pull = jax.vjp(layer_norm, middle, ln_gain[1], ln_bias[1])[1]
    middle_part, gain_two, shift_two = second_pull(second_grad)
    middle_grad = result_grad + middle_part
    middle_low = middle_grad.astype(jnp.bfloat16)
    out_in = grad_gather(middle_low)
    grad_out = lax.dot_general(mixed_heads, out_in, ROWS_ONLY, preferred_element_type=jnp.float32)
    heads_grad = lax.dot_general(
        out_in, w_out, COLS_ONLY, preferred_element_type=jnp.float32
    ).astype(jnp.bfloat16)
    proj_grad = attend_backward(
        projected, log_total, heads_grad, mask_bias, einsum_forms, streams, frames
    )
    grad_qkv = weight_grad(first_store, proj_grad)
    first_grad = input_scatter(proj_grad, w_qkv)
    first_pull = jax.vjp(layer_norm, stream_in, ln_gain[0], ln_bias[0])[1]
    input_part, gain_one, shift_one = first_pull(first_grad)
    matrices = (grad_qkv, grad_out, grad_up, grad_down)
    return (
        middle_grad + input_part,
        matrices,
        jnp.stack([gain_one, gain_two]),
        jnp.stack([shift_one, shift_two]),
    )


def split_shards(tokens, out_grad, patch_valid, clip_ids, ln_gain, ln_bias, w_qkv, w_out, w_up, w_down):
    streams = patch_valid.shape[0]
    space_bias, time_bias = mask_biases(patch_valid, clip_ids)
    up_use, down_use = (w_up, w_down)
    weights = (w_qkv, w_out, up_use, down_use)
    layouts = ((streams, FRAMES, space_bias), (streams, FRAMES, time_bias))
    form_pair = (SPATIAL_FORMS, TEMPORAL_FORMS)
    state = tokens.astype(jnp.float32)
    kept_blocks = []
    for layer_index in range(2):
        group_count, frame_count, mask_bias = layouts[layer_index]
        state, kept = block_forward(
            state,
            ln_gain[layer_index],
            ln_bias[layer_index],
            weights[0][layer_index],
            weights[1][layer_index],
            weights[2][layer_index],
            weights[3][layer_index],
            mask_bias,
            form_pair[layer_index],
            group_count,
            frame_count,
        )
        kept_blocks.append(kept)
    layer_out = state.astype(jnp.bfloat16)
    grad_state = out_grad.astype(jnp.float32)
    matrix_grads = [None, None]
    gain_grads = [None, None]
    shift_grads = [None, None]
    for layer_index in (1, 0):
        group_count, frame_count, mask_bias = layouts[layer_index]
        grad_state, matrices, gain_part, shift_part = block_backward(
            grad_state,
            kept_blocks[layer_index],
            ln_gain[layer_index],
            ln_bias[layer_index],
            weights[0][layer_index],
            weights[1][layer_index],
            weights[2][layer_index],
            weights[3][layer_index],
            mask_bias,
            form_pair[layer_index],
            group_count,
            frame_count,
        )
        matrix_grads[layer_index] = matrices
        gain_grads[layer_index] = gain_part
        shift_grads[layer_index] = shift_part
    stacked = tuple(
        (jnp.stack([matrix_grads[0][item], matrix_grads[1][item]]) for item in range(4))
    )
    stacked = (
        lax.psum(stacked[0].astype(jnp.bfloat16), "dp").astype(jnp.float32),
        lax.psum(stacked[1].astype(jnp.bfloat16), "dp").astype(jnp.float32),
        lax.psum(stacked[2].astype(jnp.bfloat16), "dp").astype(jnp.float32),
        lax.psum(stacked[3].astype(jnp.bfloat16), "dp").astype(jnp.float32),
    )
    norm_sums = lax.psum((jnp.stack(gain_grads), jnp.stack(shift_grads)), ("dp", "mp"))
    return (
        layer_out,
        grad_state,
        norm_sums[0],
        norm_sums[1],
        stacked[0],
        stacked[1],
        stacked[2],
        stacked[3],
    )


def solution(mesh):
    dp, mp = mesh.shape["dp"], mesh.shape["mp"]
    if (dp, mp) != (16, 2):
        return on_mesh(split_shards, mesh, ("dp",), "mp")
    fine = Mesh(mesh.devices.reshape(4, 2, 2, 2), ("z", "y", "core", "mp"))
    return on_mesh(shards, fine, ("z", "y", "core"), "mp")


def on_mesh(body, mesh, dp, mp):
    both = dp + (mp,)
    return jax.shard_map(
        body,
        mesh=mesh,
        in_specs=(
            P(both, None),
            P(both, None),
            P(dp, None),
            P(dp, None),
            P(),
            P(),
            P(None, None, mp),
            P(None, mp, None),
            P(None, None, mp),
            P(None, mp, None),
        ),
        out_specs=(
            P(both, None),
            P(both, None),
            P(),
            P(),
            P(None, None, mp),
            P(None, mp, None),
            P(None, None, mp),
            P(None, mp, None),
        ),
        check_vma=False,
    )
```

```python
import functools

import jax
import jax.numpy as jnp
from jax import lax
from jax.experimental import pallas as pl
from jax.experimental.pallas import tpu as pltpu
from jax.sharding import Mesh
from jax.sharding import PartitionSpec as P

HEAD_DIM = 64
FRAMES = 4
EPS = 1e-05
SCALE = HEAD_DIM ** (-0.5)
F32 = jnp.float32
BF = jnp.bfloat16
VMEM_BYTES = 40 * 2**20
SWAP = [(0, 1), (1, 0)]


def nn(a, b):
    return lax.dot_general(a, b, (((1,), (0,)), ((), ())), preferred_element_type=F32)


def nt(a, b):
    return lax.dot_general(a, b, (((1,), (1,)), ((), ())), preferred_element_type=F32)


def tn(a, b):
    return lax.dot_general(a, b, (((0,), (0,)), ((), ())), preferred_element_type=F32)


def cat(ref):
    return jnp.concatenate([ref[i] for i in range(ref.shape[0])], axis=1)


def put(ref, values):
    width = ref.shape[-1]
    for i in range(ref.shape[0]):
        ref[i] = values[:, i * width : (i + 1) * width].astype(ref.dtype)


def centred(values):
    centre = values - jnp.mean(values, axis=0, keepdims=True)
    rstd = lax.rsqrt(jnp.mean(centre * centre, axis=0, keepdims=True) + EPS)
    return centre * rstd, rstd


def norm_back(values, gain, grad, sums):
    hat, rstd = centred(values)
    scaled = grad * hat
    for k in range(values.shape[1] // 128):
        sums[0] += scaled[:, k * 128 : (k + 1) * 128]
        sums[1] += grad[:, k * 128 : (k + 1) * 128]
    inner = grad * gain
    return rstd * (
        inner
        - jnp.mean(inner, axis=0, keepdims=True)
        - hat * jnp.mean(inner * hat, axis=0, keepdims=True)
    )


def put_sums(ref, sums):
    ref[0:1, :] = jnp.sum(sums[0].T, axis=0, keepdims=True)
    ref[1:2, :] = jnp.sum(sums[1].T, axis=0, keepdims=True)


def gelu_pair(u):
    c0, c1 = 2 * 0.7978845608028654, 2 * 0.7978845608028654 * 0.044715
    square = u * u
    half = jax.nn.sigmoid(u * (c0 + c1 * square))
    g = u * half
    return g, half + (g * (1.0 - half)) * (c0 + (3 * c1) * square)


def spots(part, cols, width):
    found = []
    done = row = 0
    while cols - done >= width:
        found.append(((0, done), (part, width), (row, 0)))
        done += width
        row += part
    if done < cols:
        half, rest = part // 2, cols - done
        found.append(((0, done), (half, rest), (row, 0)))
        found.append(((half, done), (half, rest), (row, rest)))
    return found


def packed_rows(part, cols, width):
    return part * cols // width


def pack(block, width):
    part, cols = block.shape
    pieces = [block[:, c : c + width] for c in range(0, cols - width + 1, width)]
    rest = block[:, cols - cols % width :]
    if rest.shape[1]:
        pieces.append(jnp.concatenate([rest[: part // 2], rest[part // 2 :]], axis=1))
    return jnp.concatenate(pieces, axis=0)


def weight_copies(place, layer, first, second, near, far, first_v, second_v, sem):
    rows, width = first.shape[1], first.shape[2]
    part, cols = second.shape[1] // 4, second.shape[2]
    copies = [
        (first.at[layer], first_v.at[0:rows, :]),
        (second.at[layer], second_v.at[:, 0:cols]),
    ]
    for dc, pieces in enumerate((near, far)):
        for y in range(2):
            index = 2 * y + (place[1] ^ dc)
            start = pl.multiple_of(rows + index * (rows // 4), rows // 4)
            target = first_v.at[pl.ds(start, rows // 4), :]
            if len(pieces) == 2:
                copies.append((pieces[0].at[y], target))
                start = pl.multiple_of(index * part, part)
                copies.append(
                    (pieces[1].at[y], second_v.at[pl.ds(start, part), cols : 2 * cols])
                )
                continue
            (piece,) = pieces
            copies.append((piece.at[y, 0 : rows // 4, :], target))
            for (r, c), (h, w), (pr, pc) in spots(part, cols, width):
                start = pl.multiple_of(index * part + r, part // 2)
                pr += rows // 4
                copies.append(
                    (
                        piece.at[y, pr : pr + h, pc : pc + w],
                        second_v.at[pl.ds(start, h), cols + c : cols + c + w],
                    )
                )
    return [pltpu.make_async_copy(a, b, sem.at[i]) for i, (a, b) in enumerate(copies)]


def load_weights(*args):
    copies = weight_copies(*args)
    for copy in copies:
        copy.start()
    for copy in copies:
        copy.wait()


def put_blocks(place, keep, send, blocks, x_first):
    for core in range(2):

        @pl.when(place[1] == core)
        def _(core=core):
            for kind, dx, quarter, z, values, rows in blocks:
                dy, dz = place[0] ^ (quarter // 2), place[2] ^ z
                lead = (dx, dy) if x_first else (dy, dx)
                target = keep if quarter % 2 == core else send
                target[(kind, *lead, dz, rows)] = values.astype(BF)


def spatial_forward_kernel(
    layer, place, x_ref, bias_ref, norm_ref, wq, wo, near_o, near_q, far_o, far_q,
    p_ref, w_ref, inv_ref, o_ref, r_ref, a_ref, a2_ref, bias_v, wq_v, wo_v, sem,
):
    @pl.when(pl.program_id(0) == 0)
    def _():
        near, far = (near_o, near_q), (far_o, far_q)
        load_weights(place, layer, wo, wq, near, far, wo_v, wq_v, sem)

    patches = p_ref.shape[2]
    heads = wq_v.shape[1] // (3 * HEAD_DIM)
    bias_v[...] = jnp.broadcast_to(bias_ref[0], bias_v.shape)
    frames = range(p_ref.shape[0])
    xs = []
    for f in frames:
        x = x_ref[f * patches : (f + 1) * patches, :].astype(F32).T
        hat, _ = centred(x)
        a = (hat * norm_ref[:, 0:1] + norm_ref[:, 1:2]).astype(BF)
        a_ref[f] = a
        p_ref[f] = tn(wq_v[...], a).astype(BF)
        xs.append(x)

    def scores(f, h):
        base = h * 3 * HEAD_DIM
        q = (p_ref[f, base : base + HEAD_DIM, :] * SCALE).astype(BF)
        return tn(p_ref[f, base + HEAD_DIM : base + 2 * HEAD_DIM, :], q)

    def softmax(f, h, s):
        inverse = []
        for c in range(0, patches, 128):
            part = s[:, c : c + 128] + bias_v[...]
            e = jnp.exp(part - jnp.max(part, axis=0, keepdims=True))
            inverse.append(1.0 / jnp.sum(e, axis=0, keepdims=True))
            w_ref[f, h, :, c : c + 128] = e.astype(BF)
        inv_ref[f, h : h + 1, :] = jnp.concatenate(inverse, axis=1)

    def mix(f, h):
        base = h * 3 * HEAD_DIM
        v = p_ref[f, base + 2 * HEAD_DIM : base + 3 * HEAD_DIM, :]
        o = nn(v, w_ref[f, h]) * inv_ref[f, h : h + 1, :]
        o_ref[f, h * HEAD_DIM : (h + 1) * HEAD_DIM, :] = o.astype(BF)

    order = [(f, h) for f in frames for h in range(heads)]
    ahead = scores(*order[0])
    for i, at in enumerate(order):
        s = ahead
        if i + 1 < len(order):
            ahead = scores(*order[i + 1])
        if i:
            mix(*order[i - 1])
        softmax(*at, s)
    mix(*order[-1])
    for f in frames:
        r = xs[f] + tn(wo_v[...], o_ref[f])
        r_ref[f] = r.astype(r_ref.dtype)
        hat, _ = centred(r)
        a2_ref[f] = (hat * norm_ref[:, 2:3] + norm_ref[:, 3:4]).astype(BF)


def mlp_forward_kernel(
    layer, chunk, place, r_ref, a2_ref, wu, wd, near, far,
    x_ref, g_ref, slope_ref, wu_v, wd_v, sem,
):
    @pl.when(pl.program_id(0) == 0)
    def _():
        load_weights(place, layer, wd, wu, (near,), (far,), wd_v, wu_v, sem)

    a2 = cat(a2_ref)
    hidden = wu_v.shape[1]
    half = chunk // 2
    ahead = tn(wu_v[:, 0:half], a2)
    for j in range(0, hidden, half):
        u = ahead
        if j + half < hidden:
            ahead = tn(wu_v[:, j + half : j + 2 * half], a2)
        g, slope = gelu_pair(u)
        g_ref[j : j + half, :] = g.astype(BF)
        slope_ref[j : j + half, :] = slope.astype(BF)
    put(x_ref, cat(r_ref).astype(F32) + tn(wd_v[...], g_ref[...]))


def temporal_weights(p_ref, h, cols, clip_ref, stream):
    base = h * 3 * HEAD_DIM
    take = lambda f, c: p_ref[
        f, base + c * HEAD_DIM : base + (c + 1) * HEAD_DIM, cols
    ].astype(F32)
    q = [take(f, 0) for f in range(FRAMES)]
    k = [take(f, 1) for f in range(FRAMES)]
    v = [take(f, 2) for f in range(FRAMES)]
    weights = []
    for f in range(FRAMES):
        scores = []
        for g in range(f + 1):
            bias = jnp.where(clip_ref[stream, g] == clip_ref[stream, f], 0.0, -1000000000.0)
            scores.append(jnp.sum(q[f] * k[g], axis=0, keepdims=True) * SCALE + bias)
        top = functools.reduce(jnp.maximum, scores)
        e = [jnp.exp(s - top) for s in scores]
        inverse = 1.0 / functools.reduce(jnp.add, e)
        weights.append([x * inverse for x in e])
    return q, k, v, weights


def low(v):
    return v.astype(BF).astype(F32)


def temporal_forward_kernel(
    layer, place, clip_ref, x_ref, norm_ref, wq, wo, near, far,
    p_ref, o_ref, r_ref, a_ref, a2_ref, wq_v, wo_v, sem,
):
    @pl.when(pl.program_id(0) == 0)
    def _():
        load_weights(place, layer, wo, wq, (near,), (far,), wo_v, wq_v, sem)

    stream = pl.program_id(0)
    heads = wq_v.shape[1] // (3 * HEAD_DIM)
    patches = x_ref.shape[2]
    halves = [slice(c, c + 128) for c in range(0, patches, 128)]

    def project(cols):
        x = jnp.concatenate([x_ref[f, :, cols] for f in range(FRAMES)], axis=1).astype(F32)
        hat, _ = centred(x)
        a = (hat * norm_ref[:, 4:5] + norm_ref[:, 5:6]).astype(BF)
        p = tn(wq_v[...], a).astype(BF)
        for f in range(FRAMES):
            a_ref[f, :, cols] = a[:, f * 128 : (f + 1) * 128]
            p_ref[f, :, cols] = p[:, f * 128 : (f + 1) * 128]

    def mix(cols, h):
        _, _, v, weights = temporal_weights(p_ref, h, cols, clip_ref, stream)
        for f in range(FRAMES):
            o = functools.reduce(jnp.add, [low(w) * v[g] for g, w in enumerate(weights[f])])
            o_ref[f, h * HEAD_DIM : (h + 1) * HEAD_DIM, cols] = o.astype(BF)

    def finish(cols):
        o = jnp.concatenate([o_ref[f, :, cols] for f in range(FRAMES)], axis=1)
        x = jnp.concatenate([x_ref[f, :, cols] for f in range(FRAMES)], axis=1).astype(F32)
        r = x + tn(wo_v[...], o)
        hat, _ = centred(r)
        a2 = (hat * norm_ref[:, 6:7] + norm_ref[:, 7:8]).astype(BF)
        r = r.astype(BF)
        for f in range(FRAMES):
            r_ref[f, :, cols] = r[:, f * 128 : (f + 1) * 128]
            a2_ref[f, :, cols] = a2[:, f * 128 : (f + 1) * 128]

    project(halves[0])
    for i, cols in enumerate(halves):
        if i + 1 < len(halves):
            project(halves[i + 1])
        for h in range(heads):
            mix(cols, h)
        finish(cols)


def mlp_turn_kernel(
    layer, chunk, place, r_ref, a2_ref, y_ref, norm_ref, wu, wd, near, far,
    out_ref, dr_ref, dm_ref, g_ref, du_ref, ln_ref, sums, wu_v, wd_v, sem,
):
    @pl.when(pl.program_id(0) == 0)
    def _():
        load_weights(place, layer, wd, wu, (near,), (far,), wd_v, wu_v, sem)
        sums[...] = jnp.zeros_like(sums)

    a2 = cat(a2_ref)
    dm = y_ref[...].T
    put(dm_ref, dm)
    hidden = wu_v.shape[1]
    half = chunk // 2
    ahead = lambda j: (tn(wu_v[:, j : j + half], a2), nn(wd_v[j : j + half, :], dm))
    after = ahead(0)
    for j in range(0, hidden, half):
        u, dg = after
        if j + half < hidden:
            after = ahead(j + half)
        g, slope = gelu_pair(u)
        g_ref[j : j + half, :] = g.astype(BF)
        du_ref[j : j + half, :] = (dg * slope).astype(BF)
    r = cat(r_ref).astype(F32)
    back = nn(wu_v[...], du_ref[...])
    out = tn(wd_v[...], g_ref[...])
    put(dr_ref, dm.astype(F32) + norm_back(r, norm_ref[:, 6:7], back, sums))
    out_ref[...] = (r + out).astype(BF).T

    @pl.when(pl.program_id(0) == pl.num_programs(0) - 1)
    def _():
        put_sums(ln_ref, sums)


def mlp_back_kernel(
    layer, chunk, place, r_ref, y_ref, slope_ref, norm_ref, wu, wd, near, far,
    dr_ref, du_ref, ln_ref, sums, wu_v, wd_v, sem,
):
    @pl.when(pl.program_id(0) == 0)
    def _():
        load_weights(place, layer, wd, wu, (near,), (far,), wd_v, wu_v, sem)
        sums[...] = jnp.zeros_like(sums)

    dm = cat(y_ref)
    hidden = wu_v.shape[1]
    half = chunk // 2
    after = nn(wd_v[0:half, :], dm)
    for j in range(0, hidden, half):
        dg = after
        if j + half < hidden:
            after = nn(wd_v[j + half : j + 2 * half, :], dm)
        slope = slope_ref[j : j + half, :].astype(F32)
        du_ref[j : j + half, :] = (dg * slope).astype(BF)
    back = nn(wu_v[...], du_ref[...])
    r = cat(r_ref).astype(F32)
    put(dr_ref, dm.astype(F32) + norm_back(r, norm_ref[:, 2:3], back, sums))

    @pl.when(pl.program_id(0) == pl.num_programs(0) - 1)
    def _():
        put_sums(ln_ref, sums)


def mlp_grad_kernel(place, a2_ref, dm_ref, g_ref, du_ref, keep, send):
    step, steps = pl.program_id(0), pl.num_programs(0)
    dx, part = step // (steps // 2), lax.rem(step, steps // 2)
    chunk, width = g_ref.shape[0], dm_ref.shape[1]
    rows = keep.shape[4]
    quarters = chunk // (4 * rows)
    down = nt(g_ref[...], cat(dm_ref))
    up = nt(cat(a2_ref), du_ref[...])
    unit = width // 16
    spot = pl.ds(pl.multiple_of(part * unit, unit), unit)
    for core in range(2):

        @pl.when(place[1] == core)
        def _(core=core):
            for i in range(quarters):
                for z in range(4):
                    at = (4 * i + z) * rows
                    dy = place[0] ^ (part * (quarters // 2) + i // 2)
                    target = keep if i % 2 == core else send
                    target[0, dx, dy, place[2] ^ z] = down[at : at + rows].astype(BF)
            for quarter in range(4):
                for z in range(4):
                    at = (4 * quarter + z) * unit
                    dy = place[0] ^ (quarter // 2)
                    target = keep if quarter % 2 == core else send
                    target[1, dy, dx, place[2] ^ z, spot] = up[at : at + unit].astype(BF)


def temporal_back_kernel(
    layer, place, clip_ref, x_ref, y_ref, p_ref, norm_ref, wq, wo, near, far,
    dx_ref, dp_ref, ln_ref, sums, do_v, wq_v, wo_v, sem,
):
    @pl.when(pl.program_id(0) == 0)
    def _():
        load_weights(place, layer, wo, wq, (near,), (far,), wo_v, wq_v, sem)
        sums[...] = jnp.zeros_like(sums)

    stream = pl.program_id(0)
    heads = wq_v.shape[1] // (3 * HEAD_DIM)
    patches = x_ref.shape[2]
    halves = [slice(c, c + 128) for c in range(0, patches, 128)]
    gather = lambda ref, cols: jnp.concatenate([ref[f, :, cols] for f in range(FRAMES)], axis=1)

    def grad_heads(cols):
        do = nn(wo_v[...], gather(y_ref, cols)).astype(BF)
        for f in range(FRAMES):
            do_v[f, :, cols] = do[:, f * 128 : (f + 1) * 128]

    def one_head(cols, h):
        q, k, v, weights = temporal_weights(p_ref, h, cols, clip_ref, stream)
        base = h * 3 * HEAD_DIM
        rows = slice(h * HEAD_DIM, (h + 1) * HEAD_DIM)
        do = [do_v[f, rows, cols].astype(F32) for f in range(FRAMES)]
        dk = [0.0] * FRAMES
        dv = [0.0] * FRAMES
        for f in range(FRAMES):
            dw = [jnp.sum(do[f] * v[g], axis=0, keepdims=True) for g in range(f + 1)]
            inner = functools.reduce(jnp.add, [w * d for w, d in zip(weights[f], dw)])
            dq = 0.0
            for g in range(f + 1):
                ds = low(weights[f][g] * (dw[g] - inner)) * SCALE
                dq = dq + ds * k[g]
                dk[g] = dk[g] + ds * q[f]
                dv[g] = dv[g] + low(weights[f][g]) * do[f]
            dp_ref[f, base : base + HEAD_DIM, cols] = dq.astype(BF)
        for g in range(FRAMES):
            dp_ref[g, base + HEAD_DIM : base + 2 * HEAD_DIM, cols] = dk[g].astype(BF)
            dp_ref[g, base + 2 * HEAD_DIM : base + 3 * HEAD_DIM, cols] = dv[g].astype(BF)

    def finish(cols):
        inner = nn(wq_v[...], gather(dp_ref, cols))
        x, y = gather(x_ref, cols).astype(F32), gather(y_ref, cols).astype(F32)
        dx = (y + norm_back(x, norm_ref[:, 4:5], inner, sums)).astype(BF)
        for f in range(FRAMES):
            dx_ref[f, :, cols] = dx[:, f * 128 : (f + 1) * 128]

    grad_heads(halves[0])
    for i, cols in enumerate(halves):
        if i + 1 < len(halves):
            grad_heads(halves[i + 1])
        for h in range(heads):
            one_head(cols, h)
        finish(cols)

    @pl.when(pl.program_id(0) == pl.num_programs(0) - 1)
    def _():
        put_sums(ln_ref, sums)


def spatial_back_kernel(
    layer, place, y_ref, p_ref, w_ref, inv_ref, o_ref, wq, wo, near_o, near_q, far_o, far_q,
    dp_ref, do_v, inner_v, ds_v, wq_v, wo_v, sem,
):
    @pl.when(pl.program_id(0) == 0)
    def _():
        near, far = (near_o, near_q), (far_o, far_q)
        load_weights(place, layer, wo, wq, near, far, wo_v, wq_v, sem)

    heads = wq_v.shape[1] // (3 * HEAD_DIM)
    frames = range(p_ref.shape[0])
    for f in frames:
        do = nn(wo_v[...], y_ref[f]).astype(BF).astype(F32)
        for h in range(heads):
            rows = slice(h * HEAD_DIM, (h + 1) * HEAD_DIM)
            scaled = do[rows] * inv_ref[f, h : h + 1, :]
            inner = jnp.sum(scaled * o_ref[f, rows, :].astype(F32), axis=0, keepdims=True)
            inner_v[f, h : h + 1, :] = inner
            do_v[f, rows, :] = scaled.astype(BF)

    def grad_w(f, h):
        v = p_ref[f, (3 * h + 2) * HEAD_DIM : (3 * h + 3) * HEAD_DIM, :]
        return tn(v, do_v[f, h * HEAD_DIM : (h + 1) * HEAD_DIM, :])

    def grad_s(f, h, slot, dw):
        for c in range(0, dw.shape[1], 128):
            cols = slice(c, c + 128)
            w = w_ref[f, h, :, cols].astype(F32)
            ds_v[slot, :, cols] = (w * (dw[:, cols] - inner_v[f, h : h + 1, cols])).astype(BF)

    def grad_qkv(f, h, slot):
        base = h * 3 * HEAD_DIM
        q = (p_ref[f, base : base + HEAD_DIM, :] * SCALE).astype(BF)
        k = p_ref[f, base + HEAD_DIM : base + 2 * HEAD_DIM, :]
        ds = ds_v[slot]
        do = do_v[f, h * HEAD_DIM : (h + 1) * HEAD_DIM, :]
        dp_ref[f, base : base + HEAD_DIM, :] = (nn(k, ds) * SCALE).astype(BF)
        dp_ref[f, base + HEAD_DIM : base + 2 * HEAD_DIM, :] = nt(q, ds).astype(BF)
        dp_ref[f, base + 2 * HEAD_DIM : base + 3 * HEAD_DIM, :] = nt(do, w_ref[f, h]).astype(BF)

    order = [(f, h) for f in frames for h in range(heads)]
    ahead = grad_w(*order[0])
    for i, at in enumerate(order):
        dw = ahead
        if i + 1 < len(order):
            ahead = grad_w(*order[i + 1])
        if i:
            grad_qkv(*order[i - 1], (i - 1) % 2)
        grad_s(*at, i % 2, dw)
    grad_qkv(*order[-1], (len(order) - 1) % 2)


def input_grad_kernel(
    layer, place, x_ref, y_ref, dp_ref, norm_ref, wq, wo, near_o, near_q, far_o, far_q,
    dx_ref, ln_ref, sums, wq_v, wo_v, sem,
):
    @pl.when(pl.program_id(0) == 0)
    def _():
        near, far = (near_o, near_q), (far_o, far_q)
        load_weights(place, layer, wo, wq, near, far, wo_v, wq_v, sem)
        sums[...] = jnp.zeros_like(sums)

    patches = dp_ref.shape[2]
    inner = [nn(wq_v[...], dp_ref[f]) for f in range(dp_ref.shape[0])]
    for f in range(dp_ref.shape[0]):
        tokens = slice(f * patches, (f + 1) * patches)
        x = x_ref[tokens, :].astype(F32).T
        dx = y_ref[f].astype(F32) + norm_back(x, norm_ref[:, 0:1], inner[f], sums)
        dx_ref[tokens, :] = dx.T

    @pl.when(pl.program_id(0) == pl.num_programs(0) - 1)
    def _():
        put_sums(ln_ref, sums)


def attn_grad_kernel(place, a_ref, da_ref, o_ref, dp_ref, keep, send):
    dx = pl.program_id(0)
    width = da_ref.shape[1]
    out = nt(cat(o_ref), cat(da_ref))
    rows = out.shape[0] // 16
    blocks = []
    for quarter in range(4):
        for z in range(4):
            at = (4 * quarter + z) * rows
            blocks.append((0, dx, quarter, z, out[at : at + rows], slice(0, rows)))
    qkv = nt(cat(a_ref), cat(dp_ref))
    unit = qkv.shape[0] // 16
    for quarter in range(4):
        for z in range(4):
            at = (4 * quarter + z) * unit
            rows_of = {}
            for (r, c), (h, w), (pr, pc) in spots(unit, qkv.shape[1], width):
                rows_of.setdefault(pr, []).append(qkv[at + r : at + r + h, c : c + w])
            block = jnp.concatenate(
                [jnp.concatenate(rows_of[pr], axis=1) for pr in sorted(rows_of)], axis=0
            )
            spot = slice(rows, rows + block.shape[0])
            blocks.append((0, dx, quarter, z, block, spot))
    put_blocks(place, keep, send, blocks, True)


ANY = pl.BlockSpec(memory_space=pl.ANY)
SMEM = pl.BlockSpec(memory_space=pltpu.SMEM)
SEMS = pltpu.SemaphoreType.DMA((32,))


def whole(shape):
    zeros = (0,) * len(shape)
    return pl.BlockSpec(shape, lambda *_: zeros, pipeline_mode=pl.Buffered(1))


def call(body, name, grid, ins, outs, scratch, cost, after=()):
    flops, exps = cost
    count, inner = len(ins), body
    if after:
        body = lambda *refs: inner(*refs[:count], *refs[count + len(after) :])
    moved = sum(a.size * a.dtype.itemsize for a, _ in ins)
    shapes = [jax.ShapeDtypeStruct(shape, dtype) for shape, dtype, _ in outs]
    moved += sum(s.size * s.dtype.itemsize for s in shapes)
    return pl.pallas_call(
        body,
        grid=grid,
        in_specs=[spec for _, spec in ins] + [ANY] * len(after),
        out_specs=[spec for _, _, spec in outs],
        out_shape=shapes,
        scratch_shapes=scratch,
        compiler_params=pltpu.CompilerParams(
            vmem_limit_bytes=VMEM_BYTES, dimension_semantics=("arbitrary",) * len(grid)
        ),
        cost_estimate=pl.CostEstimate(
            flops=int(flops), transcendentals=int(exps), bytes_accessed=int(moved)
        ),
        name=name,
    )(*[a for a, _ in ins], *after)


def held(mine, by_rows):
    rows, cols = mine.shape[1:]
    return pltpu.VMEM((2 * rows, cols) if by_rows else (rows, 2 * cols), BF)


def later(value, *others):
    return lax.optimization_barrier((value,) + others)[0]


def own_rows(weight, layer, core):
    part, cols = weight.shape[1] // 4, weight.shape[2]
    split = weight.reshape(weight.shape[0], 2, 2, part, cols)
    return lax.dynamic_slice(split, (layer, 0, core, 0, 0), (1, 2, 1, part, cols))[0, :, 0]


def own_quarters(first, second, layer, core):
    own = []
    for y in range(2):
        index = 2 * y + core
        parts = []
        for weight in (first, second):
            part = weight.shape[1] // 4
            spot = (layer, index * part, 0)
            block = lax.dynamic_slice(weight, spot, (1, part, weight.shape[2]))[0]
            parts.append(pack(block, first.shape[2]))
        own.append(jnp.concatenate(parts, axis=0))
    return jnp.stack(own)


def swap(value, axis):
    return lax.ppermute(value, axis, SWAP)


def swap_z(value, dz):
    return lax.ppermute(value, "z", [(i, i ^ dz) for i in range(4)])


def glue_kernel(jobs, count, *refs):
    ins, outs = refs[:count], refs[count:]
    for out, stack in zip(outs, jobs):
        for i, terms in enumerate(stack):
            total = functools.reduce(
                jnp.add, [ins[a][at].astype(F32) for a, at in terms]
            )
            spot = (i,) if len(stack) > 1 else (...,)
            out[spot] = total.astype(out.dtype)


def glue(name, arrays, jobs, after=()):
    outs = []
    for stack in jobs:
        a, at = stack[0][0]
        shape = arrays[a].shape[len(at) :] if at != (...,) else arrays[a].shape
        outs.append(((len(stack),) + shape if len(stack) > 1 else shape, arrays[a].dtype))
    return call(
        functools.partial(glue_kernel, jobs, len(arrays)), name, (1,),
        [(a, whole(a.shape)) for a in arrays],
        [(shape, dtype, whole(shape)) for shape, dtype in outs], [], (0, 0), after,
    )


class Sum:
    def __init__(self, name, keep, send):
        self.name, self.keep = name, keep
        self.kinds = keep.shape[0]
        self.out = send

    def start(self, *wait):
        self.got = swap(later(self.out, *wait), "core")

    def over_core(self, *wait):
        jobs = [[[(0, (k, side)), (1, (k, side))]] for side in (0, 1) for k in range(self.kinds)]
        outs = glue(self.name + "_core", [self.keep, self.got], jobs, wait)
        self.near, far = outs[: self.kinds], outs[self.kinds :]
        self.sent = far
        self.got = [swap(f, axis) for f, axis in zip(far, ("mp", "y"))]

    def over_first(self, *wait):
        kinds = self.kinds
        jobs = [
            [[(k, (side,)), (kinds + k, (side,))]] for side in (0, 1) for k in range(kinds)
        ]
        outs = glue(self.name + "_first", list(self.near) + self.got, jobs, wait)
        self.near, far = outs[:kinds], outs[kinds:]
        self.sent = far
        self.got = [swap(f, axis) for f, axis in zip(far, ("y", "mp"))]

    def over_second(self, *wait):
        kinds = self.kinds
        jobs = [
            [[(k, (dz,)), (kinds + k, (dz,))] for k in range(kinds)] for dz in range(4)
        ]
        outs = glue(self.name + "_second", list(self.near) + self.got, jobs, wait)
        self.near, self.sent = outs[0], outs[1:]
        self.got = [swap_z(outs[dz], dz) for dz in (1, 2, 3)]

    def line(self, pairs, wait, first=False, last=False):
        kinds = self.kinds
        if first:
            jobs = [[[(k, (...,)), (kinds + k, (...,))] for k in range(kinds)]]
            arrays = list(self.near) + self.got
        else:
            jobs = [[[(0, (...,)), (1, (...,))]]]
            arrays = [self.near, self.got]
        (self.near,) = glue(self.name + "_line", arrays, jobs, wait)
        self.sent = [self.near]
        self.got = lax.ppermute(self.near, "z", pairs)

    def inward(self, *wait):
        self.line([(0, 1), (3, 2)], wait, True)

    def middle(self, *wait):
        self.line([(1, 2), (2, 1)], wait)

    def outward(self, *wait):
        self.line([(1, 0), (2, 3)], wait)

    def turn_y(self, z, *wait):
        got = later(self.got, *wait)
        self.near = jnp.where((z == 1) | (z == 2), self.near, got)
        self.sent = [self.near]
        self.got = swap(self.near, "y")

    def over_z(self, *wait):
        jobs = [[[(i, (...,)) for i in range(4)]]]
        (self.near,) = glue(self.name + "_z", [self.near] + self.got, jobs, wait)
        self.sent = [self.near]
        self.got = [swap_z(self.near, dz) for dz in (1, 2, 3)]

    def back_z(self, *wait):
        jobs = [[[(i, (...,))] for i in range(4)]]
        (self.near,) = glue(self.name + "_back", [self.near] + self.got, jobs, wait)
        self.sent = [self.near]
        self.got = swap(self.near, "y")

    def back_y(self, *wait):
        side = later(self.got, *wait)
        self.pieces = [self.near, swap(self.near, "core"), side, swap(side, "core")]


def sum_small(value, waits):
    hops = [lambda v, a=axis: swap(v, a) for axis in ("core", "mp", "y")]
    hops += [lambda v, d=dz: swap_z(v, d) for dz in (1, 2)]
    for hop, wait in zip(hops, waits):
        value = value + later(hop(value), *wait)
    return value


def finish_kernel(lines, place, *refs):
    pieces, (first, second) = refs[:-2], refs[-2:]
    width = first.shape[2]
    rows, unit, cols = first.shape[1] // 16, second.shape[1] // 16, second.shape[2]
    for layer in range(2):
        for dy in range(2):
            for dc in range(2):
                piece = pieces[4 * layer + 2 * dy + dc]
                for dz in range(4):
                    z = dz if lines[layer] else place[2] ^ dz
                    index = ((place[0] ^ dy) * 2 + (place[1] ^ dc)) * 4 + z
                    pair = len(piece.shape) == 4
                    at = lambda kind: ((kind, dz) if lines[layer] else (dz, kind)) if pair else (dz,)
                    lead = at(0)
                    start = pl.multiple_of(index * rows, rows)
                    first[layer, pl.ds(start, rows), :] = piece[
                        (*lead, slice(0, rows))
                    ].astype(F32)
                    lead, base = (at(1), 0) if pair else (at(0), rows)
                    for (r, c), (h, w), (pr, pc) in spots(unit, cols, width):
                        start = pl.multiple_of(index * unit + r, unit // 2)
                        pr += base
                        second[layer, pl.ds(start, h), c : c + w] = piece[
                            (*lead, slice(pr, pr + h), slice(pc, pc + w))
                        ].astype(F32)


def finish(name, place, layers, shapes):
    pieces = [p for layer in layers for p in layer.pieces]
    ins = [(place, SMEM)] + [(p, whole(p.shape)) for p in pieces]
    outs = [(s, F32, whole(s)) for s in shapes]
    lines = (False, True)
    return call(functools.partial(finish_kernel, lines), name, (1,), ins, outs, [], (0, 0))


def shards(tokens, out_grad, patch_valid, clip_ids, ln_gain, ln_bias, w_qkv, w_out, w_up, w_down):
    z, y, core, mp = (lax.axis_index(a) for a in ("z", "y", "core", "mp"))
    place = jnp.stack([y, core, z]).astype(jnp.int32)
    flat_place = jnp.stack([y, core, jnp.zeros_like(z)]).astype(jnp.int32)
    n, width = tokens.shape
    patches = patch_valid.shape[1]
    frames = n // patches
    streams = frames // FRAMES
    hidden = 2 * w_up.shape[2]
    heads = 2 * w_qkv.shape[2] // (3 * HEAD_DIM)
    qkv = 2 * w_qkv.shape[2]
    inner = 2 * w_out.shape[1]

    attn, mlp = (w_out, w_qkv), (w_down, w_up)
    near_a0 = [swap(own_rows(w, 0, core), "mp") for w in attn]
    own_m0, own_a1, own_m1 = (
        own_quarters(*mlp, 0, core), own_quarters(*attn, 1, core), own_quarters(*mlp, 1, core)
    )
    near_m0 = swap(later(own_m0, *near_a0), "mp")
    got_a0 = near_a0 + [swap(near, "core") for near in near_a0]

    def attn_ins(got):
        return [(array, ANY) for array in (w_qkv, w_out, *got)]

    def mlp_ins(got):
        return [(array, ANY) for array in (w_up, w_down, *got)]

    valid = lax.dynamic_slice(patch_valid, (mp * streams, 0), (streams, patches))
    bias = jnp.where(valid == 1, 0.0, -1000000000.0).astype(F32)[:, :, None]
    clips = lax.dynamic_slice(clip_ids, (mp * streams, 0), (streams, FRAMES))
    norms = jnp.stack([ln_gain, ln_bias], axis=2).reshape(8, width).T

    attn_held = [held(w_qkv, False), held(w_out, True), SEMS]
    mlp_held = [held(w_up, False), held(w_down, True), SEMS]
    norm_in = (norms, whole(norms.shape))
    place_in = (place, SMEM)
    both = 2
    span = both * patches
    tiles = frames // both
    chunk = hidden // 4

    def rows(features):
        return pl.BlockSpec((both, features, patches), lambda i: (i, 0, 0))

    def columns(features):
        return pl.BlockSpec((FRAMES, features, patches), lambda i: (i, 0, 0))

    def flat(features):
        return pl.BlockSpec((features, span), lambda i: (0, i))

    act = lambda features: (frames, features, patches)
    full = lambda features: whole(act(features))
    token_rows = pl.BlockSpec((span, width), lambda i: (i, 0))
    bias_rows = pl.BlockSpec((1, patches, 1), lambda i: (i * both // FRAMES, 0, 0))
    ln_out = ((8, width), F32, whole((8, width)))
    sums = pltpu.VMEM((2, width, 128), F32)
    spatial_flops = 4 * n * patches * inner
    attn_flops = 2 * n * width * (qkv + inner)
    mlp_flops = 4 * n * width * hidden
    grad_shape = lambda kinds, size: (kinds, 2, 2, 4, size, width)
    mlp_grad = grad_shape(2, w_down.shape[1] // 16)
    attn_grad = grad_shape(1, w_out.shape[1] // 16 + w_qkv.shape[1] * w_qkv.shape[2] // width // 16)

    p0, w0, inv0, o0, r0, a0, b0 = call(
        functools.partial(spatial_forward_kernel, 0), "spatial_forward", (tiles,),
        [place_in, (tokens, token_rows), (bias, bias_rows), norm_in] + attn_ins(got_a0),
        [(act(qkv), BF, rows(qkv)),
         ((frames, heads, patches, patches), BF,
          pl.BlockSpec((both, heads, patches, patches), lambda i: (i, 0, 0, 0))),
         (act(heads), F32, rows(heads)),
         (act(inner), BF, rows(inner)), (act(width), BF, rows(width)),
         (act(width), BF, rows(width)), (act(width), BF, rows(width))],
        [pltpu.VMEM((patches, 128), F32)] + attn_held,
        (attn_flops + spatial_flops, n * patches * heads),
    )
    near_m0 = later(near_m0, r0)
    got_m0 = [near_m0, swap(near_m0, "core")]
    near_a1 = swap(later(own_a1, near_m0), "mp")
    near_m1 = swap(later(own_m1, near_m0), "mp")
    hid = (hidden, n)
    x1, g0, slope0 = call(
        functools.partial(mlp_forward_kernel, 0, chunk), "mlp_forward", (tiles,),
        [place_in, (r0, rows(width)), (b0, rows(width))] + mlp_ins(got_m0),
        [(act(width), BF, rows(width)), (hid, BF, flat(hidden)), (hid, BF, flat(hidden))],
        mlp_held, (mlp_flops, n * hidden),
    )

    near_a1 = later(near_a1, x1)
    got_a1 = [near_a1, swap(near_a1, "core")]
    clip_in = (clips, SMEM)
    grid1 = (streams,)
    p1, o1, r1, a1, b1 = call(
        functools.partial(temporal_forward_kernel, 1), "temporal_forward", grid1,
        [place_in, clip_in, (x1, columns(width)), norm_in] + attn_ins(got_a1),
        [(act(qkv), BF, columns(qkv)), (act(inner), BF, columns(inner)),
         (act(width), BF, columns(width)), (act(width), BF, columns(width)),
         (act(width), BF, columns(width))],
        attn_held, (attn_flops * 1.2, 0),
    )
    near_m1 = later(near_m1, r1)
    got_m1 = [near_m1, swap(near_m1, "core")]
    layer_out, dr1, dm1, g1, du1, ln11 = call(
        functools.partial(mlp_turn_kernel, 1, chunk), "mlp_turn", (tiles,),
        [place_in, (r1, rows(width)), (b1, rows(width)), (out_grad, token_rows), norm_in]
        + mlp_ins(got_m1),
        [((n, width), BF, token_rows), (act(width), BF, rows(width)),
         (act(width), BF, rows(width)), (hid, BF, flat(hidden)), (hid, BF, flat(hidden)), ln_out],
        [sums] + mlp_held, (2 * mlp_flops, n * hidden),
    )

    def mlp_grads(name, place, b, dm, g, du, after=()):
        block = pl.BlockSpec((chunk, n), lambda i: (i, 0))
        keep, send = call(
            mlp_grad_kernel, name, (hidden // chunk,),
            [(place, SMEM), (b, full(width)), (dm, full(width)), (g, block), (du, block)],
            [(mlp_grad, BF, whole(mlp_grad))] * 2, [], (mlp_flops, 0), after,
        )
        return Sum(name, keep, send)

    def attn_grads(name, place, a, da, o, dp, after=()):
        half = lambda f: pl.BlockSpec((frames, f // 2, patches), lambda i: (0, i, 0))
        keep, send = call(
            attn_grad_kernel, name, (2,),
            [(place, SMEM), (a, full(width)), (da, full(width)), (o, half(inner)), (dp, half(qkv))],
            [(attn_grad, BF, whole(attn_grad))] * 2, [], (attn_flops, 0), after,
        )
        return Sum(name, keep, send)

    mlp1 = mlp_grads("mlp1", flat_place, b1, dm1, g1, du1)
    mlp1.start()
    dx1, dp1, ln10 = call(
        functools.partial(temporal_back_kernel, 1), "temporal_back", grid1,
        [place_in, clip_in, (x1, columns(width)), (dr1, columns(width)), (p1, columns(qkv)),
         norm_in] + attn_ins(got_a1),
        [(act(width), BF, columns(width)), (act(qkv), BF, columns(qkv)), ln_out],
        [sums, pltpu.VMEM((FRAMES, inner, patches), BF)] + attn_held, (1.4 * attn_flops, 0),
        [mlp1.keep],
    )
    mlp1.over_core(dx1)
    attn1 = attn_grads("attn1", flat_place, a1, dr1, o1, dp1, mlp1.sent)
    attn1.start()
    dr0, du0, ln01 = call(
        functools.partial(mlp_back_kernel, 0, chunk), "mlp_back", (tiles,),
        [place_in, (r0, rows(width)), (dx1, rows(width)), (slope0, flat(hidden)), norm_in]
        + mlp_ins(got_m0),
        [(act(width), BF, rows(width)), (hid, BF, flat(hidden)), ln_out],
        [sums] + mlp_held, (mlp_flops, 0), [attn1.keep],
    )
    mlp1.over_first(dr0)
    attn1.over_core(*mlp1.sent)
    mlp0 = mlp_grads("mlp0", place, b0, dx1, g0, du0, [*mlp1.sent, *attn1.sent])
    mlp1.inward(mlp0.keep)
    attn1.over_first(*mlp1.sent)
    mlp0.start(*attn1.sent)
    (dp0,) = call(
        functools.partial(spatial_back_kernel, 0), "spatial_back", (tiles,),
        [place_in, (dr0, rows(width)), (p0, rows(qkv)),
         (w0, pl.BlockSpec((both, heads, patches, patches), lambda i: (i, 0, 0, 0))),
         (inv0, rows(heads)), (o0, rows(inner))] + attn_ins(got_a0),
        [(act(qkv), BF, rows(qkv))],
        [pltpu.VMEM((both, inner, patches), BF), pltpu.VMEM((both, heads, patches), F32),
         pltpu.VMEM((2, patches, patches), BF)] + attn_held,
        (attn_flops + 2.5 * spatial_flops, 0), [*mlp1.sent, *attn1.sent],
    )
    mlp0.over_core(dp0)
    mlp1.middle(*mlp0.sent)
    attn1.inward(*mlp1.sent)
    attn0 = attn_grads("attn0", place, a0, dr0, o0, dp0, [*mlp0.sent, *mlp1.sent, *attn1.sent])
    attn0.start()
    attn0.over_core()
    input_grad, ln00 = call(
        functools.partial(input_grad_kernel, 0), "input_grad", (tiles,),
        [place_in, (tokens, token_rows), (dr0, rows(width)), (dp0, rows(qkv)), norm_in]
        + attn_ins(got_a0),
        [((n, width), F32, token_rows), ln_out],
        [sums] + attn_held, (attn_flops, 0), [*attn0.sent],
    )
    mlp0.over_first(input_grad)
    mlp1.outward(*mlp0.sent)
    attn1.middle(*mlp1.sent)
    waits = []
    attn0.over_first(*attn1.sent)
    waits.append(attn0.sent)
    mlp0.over_second(*attn0.sent)
    mlp1.turn_y(z, *mlp0.sent)
    attn1.outward(*mlp1.sent)
    waits.append(attn1.sent)
    attn0.over_second(*attn1.sent)
    mlp0.over_z(*attn0.sent)
    waits.append(mlp0.sent)
    attn1.turn_y(z, *mlp0.sent)
    attn0.over_z(*attn1.sent)
    waits.append(attn0.sent)
    mlp0.back_z(*attn0.sent)
    waits.append(mlp0.sent)
    mlp1.back_y(*mlp0.sent)
    attn0.back_z(*mlp0.sent)
    attn1.back_y(*attn0.sent)
    mlp0.back_y(*attn0.sent)
    attn0.back_y()

    small = sum_small(jnp.stack([ln00[:2], ln01[:2], ln10[:2], ln11[:2]]), waits)
    small = small.reshape(2, 2, 2, width)
    grad_down, grad_up = finish("finish_mlp", place, (mlp0, mlp1), (w_down.shape, w_up.shape))
    grad_out, grad_qkv = finish("finish_attn", place, (attn0, attn1), (w_out.shape, w_qkv.shape))
    return (
        layer_out,
        input_grad,
        small[:, :, 0],
        small[:, :, 1],
        grad_qkv,
        grad_out,
        grad_up,
        grad_down,
    )


SPATIAL_FORMS = ("sfphe,sfqhe->sfhpq", "sfhpq,sfqhe->sfphe", "sfhpq,sfphe->sfqhe")
TEMPORAL_FORMS = ("sfphe,sgphe->sphfg", "sphfg,sgphe->sfphe", "sphfg,sfphe->sgphe")
ROWS_ONLY = (((0,), (0,)), ((), ()))
COLS_ONLY = (((1,), (1,)), ((), ()))


def layer_norm(values, ln_gain, ln_bias):
    centre = values - jnp.mean(values, axis=-1, keepdims=True)
    spread = jnp.mean(centre * centre, axis=-1, keepdims=True)
    return centre * lax.rsqrt(spread + 1e-05) * ln_gain + ln_bias


def mask_biases(patch_valid, clip_ids):
    space_bias = jnp.where(patch_valid == 1, 0.0, -1000000000.0).astype(jnp.float32)[
        :, None, None, None, :
    ]
    frame_row = jnp.arange(FRAMES)[:, None]
    frame_col = jnp.arange(FRAMES)[None, :]
    allowed = (clip_ids[:, :, None] == clip_ids[:, None, :]) & (frame_col <= frame_row)
    time_bias = jnp.where(allowed, 0.0, -1000000000.0).astype(jnp.float32)[:, None, None, :, :]
    return (space_bias, time_bias)


def norm_gather(normed):
    return lax.all_gather(normed, "mp", axis=0, tiled=True)


def grad_gather(grad_rows):
    return lax.all_gather(grad_rows, "mp", axis=0, tiled=True)


def branch_scatter(values_bf, weight):
    return lax.psum_scatter(
        jnp.dot(values_bf, weight, preferred_element_type=jnp.float32).astype(jnp.bfloat16),
        "mp",
        scatter_dimension=0,
        tiled=True,
    ).astype(jnp.float32)


def input_scatter(grads_bf, weight):
    return lax.psum_scatter(
        lax.dot_general(grads_bf, weight, COLS_ONLY, preferred_element_type=jnp.float32).astype(
            jnp.bfloat16
        ),
        "mp",
        scatter_dimension=0,
        tiled=True,
    ).astype(jnp.float32)


def weight_grad(stored, grads_bf):
    return lax.dot_general(stored, grads_bf, ROWS_ONLY, preferred_element_type=jnp.float32)


def split_heads(projected, streams, frames):
    heads_dev = projected.shape[1] // (3 * HEAD_DIM)
    split = projected.reshape(streams, frames, -1, heads_dev, 3, HEAD_DIM)
    return (split[..., 0, :], split[..., 1, :], split[..., 2, :], heads_dev)


def attend_forward(projected, mask_bias, einsum_forms, streams, frames):
    queries, key_rows, value_rows, heads_dev = split_heads(projected, streams, frames)
    scores = (
        jnp.einsum(einsum_forms[0], queries, key_rows, preferred_element_type=jnp.float32)
        * HEAD_DIM ** (-0.5)
        + mask_bias
    )
    top_score = jnp.max(scores, axis=-1, keepdims=True)
    exponent = jnp.exp(scores - top_score)
    total = jnp.sum(exponent, axis=-1, keepdims=True)
    weights = exponent / total
    log_total = top_score + jnp.log(total)
    mixed_heads = jnp.einsum(
        einsum_forms[1],
        weights.astype(jnp.bfloat16),
        value_rows,
        preferred_element_type=jnp.float32,
    )
    return (mixed_heads.astype(jnp.bfloat16).reshape(-1, heads_dev * HEAD_DIM), log_total)


def attend_backward(projected, log_total, heads_grad, mask_bias, einsum_forms, streams, frames):
    queries, key_rows, value_rows, heads_dev = split_heads(projected, streams, frames)
    grad_heads = heads_grad.reshape(streams, frames, -1, heads_dev, HEAD_DIM)
    scale = HEAD_DIM ** (-0.5)
    scores = (
        jnp.einsum(einsum_forms[0], queries, key_rows, preferred_element_type=jnp.float32) * scale
        + mask_bias
    )
    weights = jnp.exp(scores - log_total)
    weights_grad = jnp.einsum(
        einsum_forms[0], grad_heads, value_rows, preferred_element_type=jnp.float32
    )
    inner = jnp.sum(weights * weights_grad, axis=-1, keepdims=True)
    score_grad = (weights * (weights_grad - inner)).astype(jnp.bfloat16)
    query_grad = (
        jnp.einsum(einsum_forms[1], score_grad, key_rows, preferred_element_type=jnp.float32)
        * scale
    ).astype(jnp.bfloat16)
    key_grad = (
        jnp.einsum(einsum_forms[2], score_grad, queries, preferred_element_type=jnp.float32) * scale
    ).astype(jnp.bfloat16)
    value_grad = jnp.einsum(
        einsum_forms[2],
        weights.astype(jnp.bfloat16),
        grad_heads,
        preferred_element_type=jnp.float32,
    ).astype(jnp.bfloat16)
    return jnp.stack([query_grad, key_grad, value_grad], axis=-2).reshape(projected.shape)


def block_forward(
    stream_in,
    ln_gain,
    ln_bias,
    w_qkv,
    w_out,
    w_up,
    w_down,
    mask_bias,
    einsum_forms,
    streams,
    frames,
):
    normed = layer_norm(stream_in, ln_gain[0], ln_bias[0]).astype(jnp.bfloat16)
    full_rows = norm_gather(normed)
    projected = jnp.dot(full_rows, w_qkv, preferred_element_type=jnp.float32).astype(jnp.bfloat16)
    mixed_heads, log_total = attend_forward(projected, mask_bias, einsum_forms, streams, frames)
    middle = stream_in + branch_scatter(mixed_heads, w_out)
    second = layer_norm(middle, ln_gain[1], ln_bias[1]).astype(jnp.bfloat16)
    second_full = norm_gather(second)
    hidden_pre = jnp.dot(second_full, w_up, preferred_element_type=jnp.float32)
    activated = jax.nn.gelu(hidden_pre).astype(jnp.bfloat16)
    result = middle + branch_scatter(activated, w_down)
    kept = (
        stream_in,
        full_rows,
        projected,
        mixed_heads,
        log_total,
        middle,
        second_full,
        hidden_pre,
        activated,
    )
    return (result, kept)


def block_backward(
    result_grad,
    kept,
    ln_gain,
    ln_bias,
    w_qkv,
    w_out,
    w_up,
    w_down,
    mask_bias,
    einsum_forms,
    streams,
    frames,
):
    (
        stream_in,
        first_store,
        projected,
        mixed_heads,
        log_total,
        middle,
        second_store,
        hidden_pre,
        activated,
    ) = kept
    result_low = result_grad.astype(jnp.bfloat16)
    gelu_pull = jax.vjp(jax.nn.gelu, hidden_pre)[1]
    down_in = grad_gather(result_low)
    grad_down = lax.dot_general(activated, down_in, ROWS_ONLY, preferred_element_type=jnp.float32)
    act_grad = lax.dot_general(down_in, w_down, COLS_ONLY, preferred_element_type=jnp.float32)
    hidden_grad = gelu_pull(act_grad)[0].astype(jnp.bfloat16)
    grad_up = weight_grad(second_store, hidden_grad)
    second_grad = input_scatter(hidden_grad, w_up)
    second_pull = jax.vjp(layer_norm, middle, ln_gain[1], ln_bias[1])[1]
    middle_part, gain_two, shift_two = second_pull(second_grad)
    middle_grad = result_grad + middle_part
    middle_low = middle_grad.astype(jnp.bfloat16)
    out_in = grad_gather(middle_low)
    grad_out = lax.dot_general(mixed_heads, out_in, ROWS_ONLY, preferred_element_type=jnp.float32)
    heads_grad = lax.dot_general(
        out_in, w_out, COLS_ONLY, preferred_element_type=jnp.float32
    ).astype(jnp.bfloat16)
    proj_grad = attend_backward(
        projected, log_total, heads_grad, mask_bias, einsum_forms, streams, frames
    )
    grad_qkv = weight_grad(first_store, proj_grad)
    first_grad = input_scatter(proj_grad, w_qkv)
    first_pull = jax.vjp(layer_norm, stream_in, ln_gain[0], ln_bias[0])[1]
    input_part, gain_one, shift_one = first_pull(first_grad)
    matrices = (grad_qkv, grad_out, grad_up, grad_down)
    return (
        middle_grad + input_part,
        matrices,
        jnp.stack([gain_one, gain_two]),
        jnp.stack([shift_one, shift_two]),
    )


def split_shards(tokens, out_grad, patch_valid, clip_ids, ln_gain, ln_bias, w_qkv, w_out, w_up, w_down):
    streams = patch_valid.shape[0]
    space_bias, time_bias = mask_biases(patch_valid, clip_ids)
    up_use, down_use = (w_up, w_down)
    weights = (w_qkv, w_out, up_use, down_use)
    layouts = ((streams, FRAMES, space_bias), (streams, FRAMES, time_bias))
    form_pair = (SPATIAL_FORMS, TEMPORAL_FORMS)
    state = tokens.astype(jnp.float32)
    kept_blocks = []
    for layer_index in range(2):
        group_count, frame_count, mask_bias = layouts[layer_index]
        state, kept = block_forward(
            state,
            ln_gain[layer_index],
            ln_bias[layer_index],
            weights[0][layer_index],
            weights[1][layer_index],
            weights[2][layer_index],
            weights[3][layer_index],
            mask_bias,
            form_pair[layer_index],
            group_count,
            frame_count,
        )
        kept_blocks.append(kept)
    layer_out = state.astype(jnp.bfloat16)
    grad_state = out_grad.astype(jnp.float32)
    matrix_grads = [None, None]
    gain_grads = [None, None]
    shift_grads = [None, None]
    for layer_index in (1, 0):
        group_count, frame_count, mask_bias = layouts[layer_index]
        grad_state, matrices, gain_part, shift_part = block_backward(
            grad_state,
            kept_blocks[layer_index],
            ln_gain[layer_index],
            ln_bias[layer_index],
            weights[0][layer_index],
            weights[1][layer_index],
            weights[2][layer_index],
            weights[3][layer_index],
            mask_bias,
            form_pair[layer_index],
            group_count,
            frame_count,
        )
        matrix_grads[layer_index] = matrices
        gain_grads[layer_index] = gain_part
        shift_grads[layer_index] = shift_part
    stacked = tuple(
        (jnp.stack([matrix_grads[0][item], matrix_grads[1][item]]) for item in range(4))
    )
    stacked = (
        lax.psum(stacked[0].astype(jnp.bfloat16), "dp").astype(jnp.float32),
        lax.psum(stacked[1].astype(jnp.bfloat16), "dp").astype(jnp.float32),
        lax.psum(stacked[2].astype(jnp.bfloat16), "dp").astype(jnp.float32),
        lax.psum(stacked[3].astype(jnp.bfloat16), "dp").astype(jnp.float32),
    )
    norm_sums = lax.psum((jnp.stack(gain_grads), jnp.stack(shift_grads)), ("dp", "mp"))
    return (
        layer_out,
        grad_state,
        norm_sums[0],
        norm_sums[1],
        stacked[0],
        stacked[1],
        stacked[2],
        stacked[3],
    )


def solution(mesh):
    dp, mp = mesh.shape["dp"], mesh.shape["mp"]
    if (dp, mp) != (16, 2):
        return on_mesh(split_shards, mesh, ("dp",), "mp")
    fine = Mesh(mesh.devices.reshape(4, 2, 2, 2), ("z", "y", "core", "mp"))
    return on_mesh(shards, fine, ("z", "y", "core"), "mp")


def on_mesh(body, mesh, dp, mp):
    both = dp + (mp,)
    return jax.shard_map(
        body,
        mesh=mesh,
        in_specs=(
            P(both, None),
            P(both, None),
            P(dp, None),
            P(dp, None),
            P(),
            P(),
            P(None, None, mp),
            P(None, mp, None),
            P(None, None, mp),
            P(None, mp, None),
        ),
        out_specs=(
            P(both, None),
            P(both, None),
            P(),
            P(),
            P(None, None, mp),
            P(None, mp, None),
            P(None, None, mp),
            P(None, mp, None),
        ),
        check_vma=False,
    )
```

```python
import functools

import jax
import jax.numpy as jnp
from jax import lax
from jax.experimental import pallas as pl
from jax.experimental.pallas import tpu as pltpu
from jax.sharding import Mesh
from jax.sharding import PartitionSpec as P

HEAD_DIM = 64
FRAMES = 4
EPS = 1e-05
SCALE = HEAD_DIM ** (-0.5)
F32 = jnp.float32
BF = jnp.bfloat16
VMEM_BYTES = 40 * 2**20
SWAP = [(0, 1), (1, 0)]


def nn(a, b):
    return lax.dot_general(a, b, (((1,), (0,)), ((), ())), preferred_element_type=F32)


def nt(a, b):
    return lax.dot_general(a, b, (((1,), (1,)), ((), ())), preferred_element_type=F32)


def tn(a, b):
    return lax.dot_general(a, b, (((0,), (0,)), ((), ())), preferred_element_type=F32)


def cat(ref):
    return jnp.concatenate([ref[i] for i in range(ref.shape[0])], axis=1)


def put(ref, values):
    width = ref.shape[-1]
    for i in range(ref.shape[0]):
        ref[i] = values[:, i * width : (i + 1) * width].astype(ref.dtype)


def centred(values):
    centre = values - jnp.mean(values, axis=0, keepdims=True)
    rstd = lax.rsqrt(jnp.mean(centre * centre, axis=0, keepdims=True) + EPS)
    return centre * rstd, rstd


def norm_back(values, gain, grad, sums):
    hat, rstd = centred(values)
    scaled = grad * hat
    for k in range(values.shape[1] // 128):
        sums[0] += scaled[:, k * 128 : (k + 1) * 128]
        sums[1] += grad[:, k * 128 : (k + 1) * 128]
    inner = grad * gain
    return rstd * (
        inner
        - jnp.mean(inner, axis=0, keepdims=True)
        - hat * jnp.mean(inner * hat, axis=0, keepdims=True)
    )


def put_sums(ref, sums):
    ref[0:1, :] = jnp.sum(sums[0].T, axis=0, keepdims=True)
    ref[1:2, :] = jnp.sum(sums[1].T, axis=0, keepdims=True)


def gelu_pair(u):
    c0, c1 = 2 * 0.7978845608028654, 2 * 0.7978845608028654 * 0.044715
    square = u * u
    half = jax.nn.sigmoid(u * (c0 + c1 * square))
    g = u * half
    return g, half + (g * (1.0 - half)) * (c0 + (3 * c1) * square)


def spots(part, cols, width):
    found = []
    done = row = 0
    while cols - done >= width:
        found.append(((0, done), (part, width), (row, 0)))
        done += width
        row += part
    if done < cols:
        half, rest = part // 2, cols - done
        found.append(((0, done), (half, rest), (row, 0)))
        found.append(((half, done), (half, rest), (row, rest)))
    return found


def packed_rows(part, cols, width):
    return part * cols // width


def pack(block, width):
    part, cols = block.shape
    pieces = [block[:, c : c + width] for c in range(0, cols - width + 1, width)]
    rest = block[:, cols - cols % width :]
    if rest.shape[1]:
        pieces.append(jnp.concatenate([rest[: part // 2], rest[part // 2 :]], axis=1))
    return jnp.concatenate(pieces, axis=0)


def weight_copies(place, layer, first, second, near, far, first_v, second_v, sem):
    rows, width = first.shape[1], first.shape[2]
    part, cols = second.shape[1] // 4, second.shape[2]
    copies = [
        (first.at[layer], first_v.at[0:rows, :]),
        (second.at[layer], second_v.at[:, 0:cols]),
    ]
    for dc, pieces in enumerate((near, far)):
        for y in range(2):
            index = 2 * y + (place[1] ^ dc)
            start = pl.multiple_of(rows + index * (rows // 4), rows // 4)
            target = first_v.at[pl.ds(start, rows // 4), :]
            if len(pieces) == 2:
                copies.append((pieces[0].at[y], target))
                start = pl.multiple_of(index * part, part)
                copies.append(
                    (pieces[1].at[y], second_v.at[pl.ds(start, part), cols : 2 * cols])
                )
                continue
            (piece,) = pieces
            copies.append((piece.at[y, 0 : rows // 4, :], target))
            for (r, c), (h, w), (pr, pc) in spots(part, cols, width):
                start = pl.multiple_of(index * part + r, part // 2)
                pr += rows // 4
                copies.append(
                    (
                        piece.at[y, pr : pr + h, pc : pc + w],
                        second_v.at[pl.ds(start, h), cols + c : cols + c + w],
                    )
                )
    return [pltpu.make_async_copy(a, b, sem.at[i]) for i, (a, b) in enumerate(copies)]


def load_weights(*args):
    copies = weight_copies(*args)
    for copy in copies:
        copy.start()
    for copy in copies:
        copy.wait()


def put_blocks(place, keep, send, blocks, x_first):
    for core in range(2):

        @pl.when(place[1] == core)
        def _(core=core):
            for kind, dx, quarter, z, values, rows in blocks:
                dy, dz = place[0] ^ (quarter // 2), place[2] ^ z
                lead = (dx, dy) if x_first else (dy, dx)
                target = keep if quarter % 2 == core else send
                target[(kind, *lead, dz, rows)] = values.astype(BF)


def spatial_forward_kernel(
    layer, place, x_ref, bias_ref, norm_ref, wq, wo, near_o, near_q, far_o, far_q,
    p_ref, w_ref, inv_ref, o_ref, r_ref, a_ref, a2_ref, bias_v, wq_v, wo_v, sem,
):
    @pl.when(pl.program_id(0) == 0)
    def _():
        near, far = (near_o, near_q), (far_o, far_q)
        load_weights(place, layer, wo, wq, near, far, wo_v, wq_v, sem)

    patches = p_ref.shape[2]
    heads = wq_v.shape[1] // (3 * HEAD_DIM)
    bias_v[...] = jnp.broadcast_to(bias_ref[0], bias_v.shape)
    frames = range(p_ref.shape[0])
    xs = []
    for f in frames:
        x = x_ref[f * patches : (f + 1) * patches, :].astype(F32).T
        hat, _ = centred(x)
        a = (hat * norm_ref[:, 0:1] + norm_ref[:, 1:2]).astype(BF)
        a_ref[f] = a
        p_ref[f] = tn(wq_v[...], a).astype(BF)
        xs.append(x)

    def scores(f, h):
        base = h * 3 * HEAD_DIM
        q = (p_ref[f, base : base + HEAD_DIM, :] * SCALE).astype(BF)
        return tn(p_ref[f, base + HEAD_DIM : base + 2 * HEAD_DIM, :], q)

    def softmax(f, h, s):
        inverse = []
        for c in range(0, patches, 128):
            part = s[:, c : c + 128] + bias_v[...]
            e = jnp.exp(part - jnp.max(part, axis=0, keepdims=True))
            inverse.append(1.0 / jnp.sum(e, axis=0, keepdims=True))
            w_ref[f, h, :, c : c + 128] = e.astype(BF)
        inv_ref[f, h : h + 1, :] = jnp.concatenate(inverse, axis=1)

    def mix(f, h):
        base = h * 3 * HEAD_DIM
        v = p_ref[f, base + 2 * HEAD_DIM : base + 3 * HEAD_DIM, :]
        o = nn(v, w_ref[f, h]) * inv_ref[f, h : h + 1, :]
        o_ref[f, h * HEAD_DIM : (h + 1) * HEAD_DIM, :] = o.astype(BF)

    order = [(f, h) for f in frames for h in range(heads)]
    ahead = scores(*order[0])
    for i, at in enumerate(order):
        s = ahead
        if i + 1 < len(order):
            ahead = scores(*order[i + 1])
        if i:
            mix(*order[i - 1])
        softmax(*at, s)
    mix(*order[-1])
    for f in frames:
        r = xs[f] + tn(wo_v[...], o_ref[f])
        r_ref[f] = r.astype(r_ref.dtype)
        hat, _ = centred(r)
        a2_ref[f] = (hat * norm_ref[:, 2:3] + norm_ref[:, 3:4]).astype(BF)


def mlp_forward_kernel(
    layer, chunk, place, r_ref, a2_ref, wu, wd, near, far,
    x_ref, g_ref, slope_ref, wu_v, wd_v, sem,
):
    @pl.when(pl.program_id(0) == 0)
    def _():
        load_weights(place, layer, wd, wu, (near,), (far,), wd_v, wu_v, sem)

    a2 = cat(a2_ref)
    hidden = wu_v.shape[1]
    half = chunk // 2
    ahead = tn(wu_v[:, 0:half], a2)
    for j in range(0, hidden, half):
        u = ahead
        if j + half < hidden:
            ahead = tn(wu_v[:, j + half : j + 2 * half], a2)
        g, slope = gelu_pair(u)
        g_ref[j : j + half, :] = g.astype(BF)
        slope_ref[j : j + half, :] = slope.astype(BF)
    put(x_ref, cat(r_ref).astype(F32) + tn(wd_v[...], g_ref[...]))


def temporal_weights(p_ref, h, cols, clip_ref, stream):
    base = h * 3 * HEAD_DIM
    take = lambda f, c: p_ref[
        f, base + c * HEAD_DIM : base + (c + 1) * HEAD_DIM, cols
    ].astype(F32)
    q = [take(f, 0) for f in range(FRAMES)]
    k = [take(f, 1) for f in range(FRAMES)]
    v = [take(f, 2) for f in range(FRAMES)]
    weights = []
    for f in range(FRAMES):
        scores = []
        for g in range(f + 1):
            bias = jnp.where(clip_ref[stream, g] == clip_ref[stream, f], 0.0, -1000000000.0)
            scores.append(jnp.sum(q[f] * k[g], axis=0, keepdims=True) * SCALE + bias)
        top = functools.reduce(jnp.maximum, scores)
        e = [jnp.exp(s - top) for s in scores]
        inverse = 1.0 / functools.reduce(jnp.add, e)
        weights.append([x * inverse for x in e])
    return q, k, v, weights


def low(v):
    return v.astype(BF).astype(F32)


def temporal_forward_kernel(
    layer, place, clip_ref, x_ref, norm_ref, wq, wo, near, far,
    p_ref, o_ref, r_ref, a_ref, a2_ref, wq_v, wo_v, sem,
):
    @pl.when(pl.program_id(0) == 0)
    def _():
        load_weights(place, layer, wo, wq, (near,), (far,), wo_v, wq_v, sem)

    stream = pl.program_id(0)
    heads = wq_v.shape[1] // (3 * HEAD_DIM)
    patches = x_ref.shape[2]
    halves = [slice(c, c + 128) for c in range(0, patches, 128)]

    def project(cols):
        x = jnp.concatenate([x_ref[f, :, cols] for f in range(FRAMES)], axis=1).astype(F32)
        hat, _ = centred(x)
        a = (hat * norm_ref[:, 4:5] + norm_ref[:, 5:6]).astype(BF)
        p = tn(wq_v[...], a).astype(BF)
        for f in range(FRAMES):
            a_ref[f, :, cols] = a[:, f * 128 : (f + 1) * 128]
            p_ref[f, :, cols] = p[:, f * 128 : (f + 1) * 128]

    def mix(cols, h):
        _, _, v, weights = temporal_weights(p_ref, h, cols, clip_ref, stream)
        for f in range(FRAMES):
            o = functools.reduce(jnp.add, [low(w) * v[g] for g, w in enumerate(weights[f])])
            o_ref[f, h * HEAD_DIM : (h + 1) * HEAD_DIM, cols] = o.astype(BF)

    def finish(cols):
        o = jnp.concatenate([o_ref[f, :, cols] for f in range(FRAMES)], axis=1)
        x = jnp.concatenate([x_ref[f, :, cols] for f in range(FRAMES)], axis=1).astype(F32)
        r = x + tn(wo_v[...], o)
        hat, _ = centred(r)
        a2 = (hat * norm_ref[:, 6:7] + norm_ref[:, 7:8]).astype(BF)
        r = r.astype(BF)
        for f in range(FRAMES):
            r_ref[f, :, cols] = r[:, f * 128 : (f + 1) * 128]
            a2_ref[f, :, cols] = a2[:, f * 128 : (f + 1) * 128]

    project(halves[0])
    for i, cols in enumerate(halves):
        if i + 1 < len(halves):
            project(halves[i + 1])
        for h in range(heads):
            mix(cols, h)
        finish(cols)


def mlp_turn_kernel(
    layer, chunk, place, r_ref, a2_ref, y_ref, norm_ref, wu, wd, near, far,
    out_ref, dr_ref, dm_ref, g_ref, du_ref, ln_ref, sums, wu_v, wd_v, sem,
):
    @pl.when(pl.program_id(0) == 0)
    def _():
        load_weights(place, layer, wd, wu, (near,), (far,), wd_v, wu_v, sem)
        sums[...] = jnp.zeros_like(sums)

    a2 = cat(a2_ref)
    dm = y_ref[...].T
    put(dm_ref, dm)
    hidden = wu_v.shape[1]
    half = chunk // 2
    ahead = lambda j: (tn(wu_v[:, j : j + half], a2), nn(wd_v[j : j + half, :], dm))
    after = ahead(0)
    for j in range(0, hidden, half):
        u, dg = after
        if j + half < hidden:
            after = ahead(j + half)
        g, slope = gelu_pair(u)
        g_ref[j : j + half, :] = g.astype(BF)
        du_ref[j : j + half, :] = (dg * slope).astype(BF)
    r = cat(r_ref).astype(F32)
    back = nn(wu_v[...], du_ref[...])
    out = tn(wd_v[...], g_ref[...])
    put(dr_ref, dm.astype(F32) + norm_back(r, norm_ref[:, 6:7], back, sums))
    out_ref[...] = (r + out).astype(BF).T

    @pl.when(pl.program_id(0) == pl.num_programs(0) - 1)
    def _():
        put_sums(ln_ref, sums)


def mlp_back_kernel(
    layer, chunk, place, r_ref, y_ref, slope_ref, norm_ref, wu, wd, near, far,
    dr_ref, du_ref, ln_ref, sums, wu_v, wd_v, sem,
):
    @pl.when(pl.program_id(0) == 0)
    def _():
        load_weights(place, layer, wd, wu, (near,), (far,), wd_v, wu_v, sem)
        sums[...] = jnp.zeros_like(sums)

    dm = cat(y_ref)
    hidden = wu_v.shape[1]
    half = chunk // 2
    after = nn(wd_v[0:half, :], dm)
    for j in range(0, hidden, half):
        dg = after
        if j + half < hidden:
            after = nn(wd_v[j + half : j + 2 * half, :], dm)
        slope = slope_ref[j : j + half, :].astype(F32)
        du_ref[j : j + half, :] = (dg * slope).astype(BF)
    back = nn(wu_v[...], du_ref[...])
    r = cat(r_ref).astype(F32)
    put(dr_ref, dm.astype(F32) + norm_back(r, norm_ref[:, 2:3], back, sums))

    @pl.when(pl.program_id(0) == pl.num_programs(0) - 1)
    def _():
        put_sums(ln_ref, sums)


def mlp_grad_kernel(place, a2_ref, dm_ref, g_ref, du_ref, keep, send):
    step, steps = pl.program_id(0), pl.num_programs(0)
    dx, part = step // (steps // 2), lax.rem(step, steps // 2)
    chunk, width = g_ref.shape[0], dm_ref.shape[1]
    rows = keep.shape[4]
    quarters = chunk // (4 * rows)
    down = nt(g_ref[...], cat(dm_ref))
    up = nt(cat(a2_ref), du_ref[...])
    unit = width // 16
    spot = pl.ds(pl.multiple_of(part * unit, unit), unit)
    for core in range(2):

        @pl.when(place[1] == core)
        def _(core=core):
            for i in range(quarters):
                for z in range(4):
                    at = (4 * i + z) * rows
                    dy = place[0] ^ (part * (quarters // 2) + i // 2)
                    target = keep if i % 2 == core else send
                    target[0, dx, dy, place[2] ^ z] = down[at : at + rows].astype(BF)
            for quarter in range(4):
                for z in range(4):
                    at = (4 * quarter + z) * unit
                    dy = place[0] ^ (quarter // 2)
                    target = keep if quarter % 2 == core else send
                    target[1, dy, dx, place[2] ^ z, spot] = up[at : at + unit].astype(BF)


def temporal_back_kernel(
    layer, place, clip_ref, x_ref, y_ref, p_ref, norm_ref, wq, wo, near, far,
    dx_ref, dp_ref, ln_ref, sums, do_v, wq_v, wo_v, sem,
):
    @pl.when(pl.program_id(0) == 0)
    def _():
        load_weights(place, layer, wo, wq, (near,), (far,), wo_v, wq_v, sem)
        sums[...] = jnp.zeros_like(sums)

    stream = pl.program_id(0)
    heads = wq_v.shape[1] // (3 * HEAD_DIM)
    patches = x_ref.shape[2]
    halves = [slice(c, c + 128) for c in range(0, patches, 128)]
    gather = lambda ref, cols: jnp.concatenate([ref[f, :, cols] for f in range(FRAMES)], axis=1)

    def grad_heads(cols):
        do = nn(wo_v[...], gather(y_ref, cols)).astype(BF)
        for f in range(FRAMES):
            do_v[f, :, cols] = do[:, f * 128 : (f + 1) * 128]

    def one_head(cols, h):
        q, k, v, weights = temporal_weights(p_ref, h, cols, clip_ref, stream)
        base = h * 3 * HEAD_DIM
        rows = slice(h * HEAD_DIM, (h + 1) * HEAD_DIM)
        do = [do_v[f, rows, cols].astype(F32) for f in range(FRAMES)]
        dk = [0.0] * FRAMES
        dv = [0.0] * FRAMES
        for f in range(FRAMES):
            dw = [jnp.sum(do[f] * v[g], axis=0, keepdims=True) for g in range(f + 1)]
            inner = functools.reduce(jnp.add, [w * d for w, d in zip(weights[f], dw)])
            dq = 0.0
            for g in range(f + 1):
                ds = low(weights[f][g] * (dw[g] - inner)) * SCALE
                dq = dq + ds * k[g]
                dk[g] = dk[g] + ds * q[f]
                dv[g] = dv[g] + low(weights[f][g]) * do[f]
            dp_ref[f, base : base + HEAD_DIM, cols] = dq.astype(BF)
        for g in range(FRAMES):
            dp_ref[g, base + HEAD_DIM : base + 2 * HEAD_DIM, cols] = dk[g].astype(BF)
            dp_ref[g, base + 2 * HEAD_DIM : base + 3 * HEAD_DIM, cols] = dv[g].astype(BF)

    def finish(cols):
        inner = nn(wq_v[...], gather(dp_ref, cols))
        x, y = gather(x_ref, cols).astype(F32), gather(y_ref, cols).astype(F32)
        dx = (y + norm_back(x, norm_ref[:, 4:5], inner, sums)).astype(BF)
        for f in range(FRAMES):
            dx_ref[f, :, cols] = dx[:, f * 128 : (f + 1) * 128]

    grad_heads(halves[0])
    for i, cols in enumerate(halves):
        if i + 1 < len(halves):
            grad_heads(halves[i + 1])
        for h in range(heads):
            one_head(cols, h)
        finish(cols)

    @pl.when(pl.program_id(0) == pl.num_programs(0) - 1)
    def _():
        put_sums(ln_ref, sums)


def spatial_back_kernel(
    layer, place, y_ref, p_ref, w_ref, inv_ref, o_ref, wq, wo, near_o, near_q, far_o, far_q,
    dp_ref, do_v, inner_v, ds_v, wq_v, wo_v, sem,
):
    @pl.when(pl.program_id(0) == 0)
    def _():
        near, far = (near_o, near_q), (far_o, far_q)
        load_weights(place, layer, wo, wq, near, far, wo_v, wq_v, sem)

    heads = wq_v.shape[1] // (3 * HEAD_DIM)
    frames = range(p_ref.shape[0])
    for f in frames:
        do = nn(wo_v[...], y_ref[f]).astype(BF).astype(F32)
        for h in range(heads):
            rows = slice(h * HEAD_DIM, (h + 1) * HEAD_DIM)
            scaled = do[rows] * inv_ref[f, h : h + 1, :]
            inner = jnp.sum(scaled * o_ref[f, rows, :].astype(F32), axis=0, keepdims=True)
            inner_v[f, h : h + 1, :] = inner
            do_v[f, rows, :] = scaled.astype(BF)

    def grad_w(f, h):
        v = p_ref[f, (3 * h + 2) * HEAD_DIM : (3 * h + 3) * HEAD_DIM, :]
        return tn(v, do_v[f, h * HEAD_DIM : (h + 1) * HEAD_DIM, :])

    def grad_s(f, h, slot, dw):
        for c in range(0, dw.shape[1], 128):
            cols = slice(c, c + 128)
            w = w_ref[f, h, :, cols].astype(F32)
            ds_v[slot, :, cols] = (w * (dw[:, cols] - inner_v[f, h : h + 1, cols])).astype(BF)

    def grad_qkv(f, h, slot):
        base = h * 3 * HEAD_DIM
        q = (p_ref[f, base : base + HEAD_DIM, :] * SCALE).astype(BF)
        k = p_ref[f, base + HEAD_DIM : base + 2 * HEAD_DIM, :]
        ds = ds_v[slot]
        do = do_v[f, h * HEAD_DIM : (h + 1) * HEAD_DIM, :]
        dp_ref[f, base : base + HEAD_DIM, :] = (nn(k, ds) * SCALE).astype(BF)
        dp_ref[f, base + HEAD_DIM : base + 2 * HEAD_DIM, :] = nt(q, ds).astype(BF)
        dp_ref[f, base + 2 * HEAD_DIM : base + 3 * HEAD_DIM, :] = nt(do, w_ref[f, h]).astype(BF)

    order = [(f, h) for f in frames for h in range(heads)]
    ahead = grad_w(*order[0])
    for i, at in enumerate(order):
        dw = ahead
        if i + 1 < len(order):
            ahead = grad_w(*order[i + 1])
        if i:
            grad_qkv(*order[i - 1], (i - 1) % 2)
        grad_s(*at, i % 2, dw)
    grad_qkv(*order[-1], (len(order) - 1) % 2)


def input_grad_kernel(
    layer, place, x_ref, y_ref, dp_ref, norm_ref, wq, wo, near_o, near_q, far_o, far_q,
    dx_ref, ln_ref, sums, wq_v, wo_v, sem,
):
    @pl.when(pl.program_id(0) == 0)
    def _():
        near, far = (near_o, near_q), (far_o, far_q)
        load_weights(place, layer, wo, wq, near, far, wo_v, wq_v, sem)
        sums[...] = jnp.zeros_like(sums)

    patches = dp_ref.shape[2]
    inner = [nn(wq_v[...], dp_ref[f]) for f in range(dp_ref.shape[0])]
    for f in range(dp_ref.shape[0]):
        tokens = slice(f * patches, (f + 1) * patches)
        x = x_ref[tokens, :].astype(F32).T
        dx = y_ref[f].astype(F32) + norm_back(x, norm_ref[:, 0:1], inner[f], sums)
        dx_ref[tokens, :] = dx.T

    @pl.when(pl.program_id(0) == pl.num_programs(0) - 1)
    def _():
        put_sums(ln_ref, sums)


def attn_grad_kernel(place, a_ref, da_ref, o_ref, dp_ref, keep, send):
    dx = pl.program_id(0)
    width = da_ref.shape[1]
    out = nt(cat(o_ref), cat(da_ref))
    rows = out.shape[0] // 16
    blocks = []
    for quarter in range(4):
        for z in range(4):
            at = (4 * quarter + z) * rows
            blocks.append((0, dx, quarter, z, out[at : at + rows], slice(0, rows)))
    qkv = nt(cat(a_ref), cat(dp_ref))
    unit = qkv.shape[0] // 16
    for quarter in range(4):
        for z in range(4):
            at = (4 * quarter + z) * unit
            rows_of = {}
            for (r, c), (h, w), (pr, pc) in spots(unit, qkv.shape[1], width):
                rows_of.setdefault(pr, []).append(qkv[at + r : at + r + h, c : c + w])
            block = jnp.concatenate(
                [jnp.concatenate(rows_of[pr], axis=1) for pr in sorted(rows_of)], axis=0
            )
            spot = slice(rows, rows + block.shape[0])
            blocks.append((0, dx, quarter, z, block, spot))
    put_blocks(place, keep, send, blocks, True)


ANY = pl.BlockSpec(memory_space=pl.ANY)
SMEM = pl.BlockSpec(memory_space=pltpu.SMEM)
SEMS = pltpu.SemaphoreType.DMA((32,))


def whole(shape):
    zeros = (0,) * len(shape)
    return pl.BlockSpec(shape, lambda *_: zeros, pipeline_mode=pl.Buffered(1))


def call(body, name, grid, ins, outs, scratch, cost, after=()):
    flops, exps = cost
    count, inner = len(ins), body
    if after:
        body = lambda *refs: inner(*refs[:count], *refs[count + len(after) :])
    moved = sum(a.size * a.dtype.itemsize for a, _ in ins)
    shapes = [jax.ShapeDtypeStruct(shape, dtype) for shape, dtype, _ in outs]
    moved += sum(s.size * s.dtype.itemsize for s in shapes)
    return pl.pallas_call(
        body,
        grid=grid,
        in_specs=[spec for _, spec in ins] + [ANY] * len(after),
        out_specs=[spec for _, _, spec in outs],
        out_shape=shapes,
        scratch_shapes=scratch,
        compiler_params=pltpu.CompilerParams(
            vmem_limit_bytes=VMEM_BYTES, dimension_semantics=("arbitrary",) * len(grid)
        ),
        cost_estimate=pl.CostEstimate(
            flops=int(flops), transcendentals=int(exps), bytes_accessed=int(moved)
        ),
        name=name,
    )(*[a for a, _ in ins], *after)


def held(mine, by_rows):
    rows, cols = mine.shape[1:]
    return pltpu.VMEM((2 * rows, cols) if by_rows else (rows, 2 * cols), BF)


def later(value, *others):
    return lax.optimization_barrier((value,) + others)[0]


def own_rows(weight, layer, core):
    part, cols = weight.shape[1] // 4, weight.shape[2]
    split = weight.reshape(weight.shape[0], 2, 2, part, cols)
    return lax.dynamic_slice(split, (layer, 0, core, 0, 0), (1, 2, 1, part, cols))[0, :, 0]


def own_quarters(first, second, layer, core):
    own = []
    for y in range(2):
        index = 2 * y + core
        parts = []
        for weight in (first, second):
            part = weight.shape[1] // 4
            spot = (layer, index * part, 0)
            block = lax.dynamic_slice(weight, spot, (1, part, weight.shape[2]))[0]
            parts.append(pack(block, first.shape[2]))
        own.append(jnp.concatenate(parts, axis=0))
    return jnp.stack(own)


def swap(value, axis):
    return lax.ppermute(value, axis, SWAP)


def swap_z(value, dz):
    return lax.ppermute(value, "z", [(i, i ^ dz) for i in range(4)])


def glue_kernel(jobs, count, *refs):
    ins, outs = refs[:count], refs[count:]
    for out, stack in zip(outs, jobs):
        for i, terms in enumerate(stack):
            total = functools.reduce(
                jnp.add, [ins[a][at].astype(F32) for a, at in terms]
            )
            spot = (i,) if len(stack) > 1 else (...,)
            out[spot] = total.astype(out.dtype)


def glue(name, arrays, jobs, after=()):
    outs = []
    for stack in jobs:
        a, at = stack[0][0]
        shape = arrays[a].shape[len(at) :] if at != (...,) else arrays[a].shape
        outs.append(((len(stack),) + shape if len(stack) > 1 else shape, arrays[a].dtype))
    return call(
        functools.partial(glue_kernel, jobs, len(arrays)), name, (1,),
        [(a, whole(a.shape)) for a in arrays],
        [(shape, dtype, whole(shape)) for shape, dtype in outs], [], (0, 0), after,
    )


class Sum:
    def __init__(self, name, keep, send):
        self.name, self.keep = name, keep
        self.kinds = keep.shape[0]
        self.out = send

    def start(self, *wait):
        self.got = swap(later(self.out, *wait), "core")

    def over_core(self, *wait):
        jobs = [[[(0, (k, side)), (1, (k, side))]] for side in (0, 1) for k in range(self.kinds)]
        outs = glue(self.name + "_core", [self.keep, self.got], jobs, wait)
        self.near, far = outs[: self.kinds], outs[self.kinds :]
        self.sent = far
        self.got = [swap(f, axis) for f, axis in zip(far, ("mp", "y"))]

    def over_first(self, *wait):
        kinds = self.kinds
        jobs = [
            [[(k, (side,)), (kinds + k, (side,))]] for side in (0, 1) for k in range(kinds)
        ]
        outs = glue(self.name + "_first", list(self.near) + self.got, jobs, wait)
        self.near, far = outs[:kinds], outs[kinds:]
        self.sent = far
        self.got = [swap(f, axis) for f, axis in zip(far, ("y", "mp"))]


class Joint:
    def __init__(self, sums, *wait):
        self.name = sums[0].name
        arrays, pairs = [], []
        for part in sums:
            base = len(arrays)
            arrays += list(part.near) + part.got
            pairs += [(base + k, base + part.kinds + k) for k in range(part.kinds)]
        jobs = [[[(a, (dz,)), (b, (dz,))] for a, b in pairs] for dz in range(4)]
        outs = glue(self.name + "_second", arrays, jobs, wait)
        self.near, self.sent = outs[0], outs[1:]
        self.got = [swap_z(outs[dz], dz) for dz in (1, 2, 3)]

    def over_z(self, *wait):
        jobs = [[[(i, (...,)) for i in range(4)]]]
        (self.near,) = glue(self.name + "_z", [self.near] + self.got, jobs, wait)
        self.sent = [self.near]
        self.got = [swap_z(self.near, dz) for dz in (1, 2, 3)]

    def back_z(self, *wait):
        jobs = [[[(i, (...,))] for i in range(4)]]
        (self.near,) = glue(self.name + "_back", [self.near] + self.got, jobs, wait)
        self.sent = [self.near]
        self.got = swap(self.near, "y")

    def back_y(self, *wait):
        side = later(self.got, *wait)
        self.sent = [side]
        self.pieces = [self.near, swap(self.near, "core"), side, swap(side, "core")]


def finish_kernel(place, *refs):
    pieces, (first, second) = refs[:-2], refs[-2:]
    width = first.shape[2]
    rows, unit, cols = first.shape[1] // 16, second.shape[1] // 16, second.shape[2]
    pair = len(pieces[0].shape) == 4
    for layer in range(2):
        for dy in range(2):
            for dc in range(2):
                piece = pieces[4 * layer + 2 * dy + dc]
                for dz in range(4):
                    z = place[2] ^ dz
                    index = ((place[0] ^ dy) * 2 + (place[1] ^ dc)) * 4 + z
                    if layer:
                        at = lambda kind: (dz, kind if pair else 2)
                    else:
                        at = lambda kind: (dz, kind) if pair else (dz,)
                    lead = at(0)
                    start = pl.multiple_of(index * rows, rows)
                    first[layer, pl.ds(start, rows), :] = piece[
                        (*lead, slice(0, rows))
                    ].astype(F32)
                    lead, base = (at(1), 0) if pair else (at(0), rows)
                    for (r, c), (h, w), (pr, pc) in spots(unit, cols, width):
                        start = pl.multiple_of(index * unit + r, unit // 2)
                        pr += base
                        second[layer, pl.ds(start, h), c : c + w] = piece[
                            (*lead, slice(pr, pr + h), slice(pc, pc + w))
                        ].astype(F32)


def finish(name, place, layers, shapes):
    pieces = [p for layer in layers for p in layer.pieces]
    ins = [(place, SMEM)] + [(p, whole(p.shape)) for p in pieces]
    outs = [(s, F32, whole(s)) for s in shapes]
    return call(finish_kernel, name, (1,), ins, outs, [], (0, 0))


def shards(tokens, out_grad, patch_valid, clip_ids, ln_gain, ln_bias, w_qkv, w_out, w_up, w_down):
    z, y, core, mp = (lax.axis_index(a) for a in ("z", "y", "core", "mp"))
    place = jnp.stack([y, core, z]).astype(jnp.int32)
    n, width = tokens.shape
    patches = patch_valid.shape[1]
    frames = n // patches
    streams = frames // FRAMES
    hidden = 2 * w_up.shape[2]
    heads = 2 * w_qkv.shape[2] // (3 * HEAD_DIM)
    qkv = 2 * w_qkv.shape[2]
    inner = 2 * w_out.shape[1]

    attn, mlp = (w_out, w_qkv), (w_down, w_up)
    near_a0 = [swap(own_rows(w, 0, core), "mp") for w in attn]
    own_m0, own_a1, own_m1 = (
        own_quarters(*mlp, 0, core), own_quarters(*attn, 1, core), own_quarters(*mlp, 1, core)
    )
    near_m0 = swap(later(own_m0, *near_a0), "mp")
    got_a0 = near_a0 + [swap(near, "core") for near in near_a0]

    def attn_ins(got):
        return [(array, ANY) for array in (w_qkv, w_out, *got)]

    def mlp_ins(got):
        return [(array, ANY) for array in (w_up, w_down, *got)]

    valid = lax.dynamic_slice(patch_valid, (mp * streams, 0), (streams, patches))
    bias = jnp.where(valid == 1, 0.0, -1000000000.0).astype(F32)[:, :, None]
    clips = lax.dynamic_slice(clip_ids, (mp * streams, 0), (streams, FRAMES))
    norms = jnp.stack([ln_gain, ln_bias], axis=2).reshape(8, width).T

    attn_held = [held(w_qkv, False), held(w_out, True), SEMS]
    mlp_held = [held(w_up, False), held(w_down, True), SEMS]
    norm_in = (norms, whole(norms.shape))
    place_in = (place, SMEM)
    both = 2
    span = both * patches
    tiles = frames // both
    chunk = hidden // 4

    def rows(features):
        return pl.BlockSpec((both, features, patches), lambda i: (i, 0, 0))

    def columns(features):
        return pl.BlockSpec((FRAMES, features, patches), lambda i: (i, 0, 0))

    def flat(features):
        return pl.BlockSpec((features, span), lambda i: (0, i))

    act = lambda features: (frames, features, patches)
    full = lambda features: whole(act(features))
    token_rows = pl.BlockSpec((span, width), lambda i: (i, 0))
    bias_rows = pl.BlockSpec((1, patches, 1), lambda i: (i * both // FRAMES, 0, 0))
    ln_out = ((8, width), F32, whole((8, width)))
    sums = pltpu.VMEM((2, width, 128), F32)
    spatial_flops = 4 * n * patches * inner
    attn_flops = 2 * n * width * (qkv + inner)
    mlp_flops = 4 * n * width * hidden
    grad_shape = lambda kinds, size: (kinds, 2, 2, 4, size, width)
    mlp_grad = grad_shape(2, w_down.shape[1] // 16)
    attn_grad = grad_shape(1, w_out.shape[1] // 16 + w_qkv.shape[1] * w_qkv.shape[2] // width // 16)

    p0, w0, inv0, o0, r0, a0, b0 = call(
        functools.partial(spatial_forward_kernel, 0), "spatial_forward", (tiles,),
        [place_in, (tokens, token_rows), (bias, bias_rows), norm_in] + attn_ins(got_a0),
        [(act(qkv), BF, rows(qkv)),
         ((frames, heads, patches, patches), BF,
          pl.BlockSpec((both, heads, patches, patches), lambda i: (i, 0, 0, 0))),
         (act(heads), F32, rows(heads)),
         (act(inner), BF, rows(inner)), (act(width), BF, rows(width)),
         (act(width), BF, rows(width)), (act(width), BF, rows(width))],
        [pltpu.VMEM((patches, 128), F32)] + attn_held,
        (attn_flops + spatial_flops, n * patches * heads),
    )
    near_m0 = later(near_m0, r0)
    got_m0 = [near_m0, swap(near_m0, "core")]
    near_a1 = swap(later(own_a1, near_m0), "mp")
    near_m1 = swap(later(own_m1, near_m0), "mp")
    hid = (hidden, n)
    x1, g0, slope0 = call(
        functools.partial(mlp_forward_kernel, 0, chunk), "mlp_forward", (tiles,),
        [place_in, (r0, rows(width)), (b0, rows(width))] + mlp_ins(got_m0),
        [(act(width), BF, rows(width)), (hid, BF, flat(hidden)), (hid, BF, flat(hidden))],
        mlp_held, (mlp_flops, n * hidden),
    )

    near_a1 = later(near_a1, x1)
    got_a1 = [near_a1, swap(near_a1, "core")]
    clip_in = (clips, SMEM)
    grid1 = (streams,)
    p1, o1, r1, a1, b1 = call(
        functools.partial(temporal_forward_kernel, 1), "temporal_forward", grid1,
        [place_in, clip_in, (x1, columns(width)), norm_in] + attn_ins(got_a1),
        [(act(qkv), BF, columns(qkv)), (act(inner), BF, columns(inner)),
         (act(width), BF, columns(width)), (act(width), BF, columns(width)),
         (act(width), BF, columns(width))],
        attn_held, (attn_flops * 1.2, 0),
    )
    near_m1 = later(near_m1, r1)
    got_m1 = [near_m1, swap(near_m1, "core")]
    layer_out, dr1, dm1, g1, du1, ln11 = call(
        functools.partial(mlp_turn_kernel, 1, chunk), "mlp_turn", (tiles,),
        [place_in, (r1, rows(width)), (b1, rows(width)), (out_grad, token_rows), norm_in]
        + mlp_ins(got_m1),
        [((n, width), BF, token_rows), (act(width), BF, rows(width)),
         (act(width), BF, rows(width)), (hid, BF, flat(hidden)), (hid, BF, flat(hidden)), ln_out],
        [sums] + mlp_held, (2 * mlp_flops, n * hidden),
    )

    def mlp_grads(name, place, b, dm, g, du, after=()):
        block = pl.BlockSpec((chunk, n), lambda i: (i, 0))
        keep, send = call(
            mlp_grad_kernel, name, (hidden // chunk,),
            [(place, SMEM), (b, full(width)), (dm, full(width)), (g, block), (du, block)],
            [(mlp_grad, BF, whole(mlp_grad))] * 2, [], (mlp_flops, 0), after,
        )
        return keep, send

    def attn_grads(name, place, a, da, o, dp, after=()):
        half = lambda f: pl.BlockSpec((frames, f // 2, patches), lambda i: (0, i, 0))
        keep, send = call(
            attn_grad_kernel, name, (2,),
            [(place, SMEM), (a, full(width)), (da, full(width)), (o, half(inner)), (dp, half(qkv))],
            [(attn_grad, BF, whole(attn_grad))] * 2, [], (attn_flops, 0), after,
        )
        return keep, send

    mlp1 = Sum("mlp1", *mlp_grads("mlp1", place, b1, dm1, g1, du1))
    mlp1.start()
    dx1, dp1, ln10 = call(
        functools.partial(temporal_back_kernel, 1), "temporal_back", grid1,
        [place_in, clip_in, (x1, columns(width)), (dr1, columns(width)), (p1, columns(qkv)),
         norm_in] + attn_ins(got_a1),
        [(act(width), BF, columns(width)), (act(qkv), BF, columns(qkv)), ln_out],
        [sums, pltpu.VMEM((FRAMES, inner, patches), BF)] + attn_held, (1.4 * attn_flops, 0),
        [mlp1.keep],
    )
    mlp1.over_core(dx1)
    attn1 = Sum("attn1", *attn_grads("attn1", place, a1, dr1, o1, dp1, mlp1.sent))
    attn1.start()
    attn1.over_core()
    dr0, du0, ln01 = call(
        functools.partial(mlp_back_kernel, 0, chunk), "mlp_back", (tiles,),
        [place_in, (r0, rows(width)), (dx1, rows(width)), (slope0, flat(hidden)), norm_in]
        + mlp_ins(got_m0),
        [(act(width), BF, rows(width)), (hid, BF, flat(hidden)), ln_out],
        [sums] + mlp_held, (mlp_flops, 0), attn1.sent,
    )
    mlp1.over_first(dr0)
    attn1.over_first(*mlp1.sent)
    mlp0 = Sum("mlp0", *mlp_grads("mlp0", place, b0, dx1, g0, du0, attn1.sent))
    late = Joint([mlp1, attn1], mlp0.keep)
    mlp0.start(*late.sent)
    (dp0,) = call(
        functools.partial(spatial_back_kernel, 0), "spatial_back", (tiles,),
        [place_in, (dr0, rows(width)), (p0, rows(qkv)),
         (w0, pl.BlockSpec((both, heads, patches, patches), lambda i: (i, 0, 0, 0))),
         (inv0, rows(heads)), (o0, rows(inner))] + attn_ins(got_a0),
        [(act(qkv), BF, rows(qkv))],
        [pltpu.VMEM((both, inner, patches), BF), pltpu.VMEM((both, heads, patches), F32),
         pltpu.VMEM((2, patches, patches), BF)] + attn_held,
        (attn_flops + 2.5 * spatial_flops, 0), late.sent,
    )
    mlp0.over_core(dp0)
    attn0 = Sum("attn0", *attn_grads("attn0", place, a0, dr0, o0, dp0, mlp0.sent))
    late.over_z(attn0.keep)
    attn0.start(*late.sent)
    attn0.over_core()
    input_grad, ln00 = call(
        functools.partial(input_grad_kernel, 0), "input_grad", (tiles,),
        [place_in, (tokens, token_rows), (dr0, rows(width)), (dp0, rows(qkv)), norm_in]
        + attn_ins(got_a0),
        [((n, width), F32, token_rows), ln_out],
        [sums] + attn_held, (attn_flops, 0), [*attn0.sent],
    )
    small = jnp.stack([ln00[:2], ln01[:2], ln10[:2], ln11[:2]])
    small = small + swap(small, "core")
    mlp0.over_first(input_grad)
    attn0.over_first(*mlp0.sent)
    late.back_z(*attn0.sent)
    mlp0 = Joint([mlp0], *late.sent)
    small = small + later(swap(later(small, *mlp0.sent), "mp"), *mlp0.sent)
    attn0 = Joint([attn0], *mlp0.sent, small)
    mlp0.over_z(*attn0.sent)
    attn0.over_z(*mlp0.sent)
    late.back_y(*attn0.sent)
    mlp0.back_z(*attn0.sent)
    attn0.back_z(*mlp0.sent)
    for dz in (1, 2):
        small = small + swap_z(later(small, *attn0.sent), dz)
    mlp0.back_y(*attn0.sent)
    small = small + swap(later(small, *mlp0.sent), "y")
    attn0.back_y(*mlp0.sent)

    small = small.reshape(2, 2, 2, width)
    grad_down, grad_up = finish("finish_mlp", place, (mlp0, late), (w_down.shape, w_up.shape))
    grad_out, grad_qkv = finish("finish_attn", place, (attn0, late), (w_out.shape, w_qkv.shape))
    return (
        layer_out,
        input_grad,
        small[:, :, 0],
        small[:, :, 1],
        grad_qkv,
        grad_out,
        grad_up,
        grad_down,
    )


SPATIAL_FORMS = ("sfphe,sfqhe->sfhpq", "sfhpq,sfqhe->sfphe", "sfhpq,sfphe->sfqhe")
TEMPORAL_FORMS = ("sfphe,sgphe->sphfg", "sphfg,sgphe->sfphe", "sphfg,sfphe->sgphe")
ROWS_ONLY = (((0,), (0,)), ((), ()))
COLS_ONLY = (((1,), (1,)), ((), ()))


def layer_norm(values, ln_gain, ln_bias):
    centre = values - jnp.mean(values, axis=-1, keepdims=True)
    spread = jnp.mean(centre * centre, axis=-1, keepdims=True)
    return centre * lax.rsqrt(spread + 1e-05) * ln_gain + ln_bias


def mask_biases(patch_valid, clip_ids):
    space_bias = jnp.where(patch_valid == 1, 0.0, -1000000000.0).astype(jnp.float32)[
        :, None, None, None, :
    ]
    frame_row = jnp.arange(FRAMES)[:, None]
    frame_col = jnp.arange(FRAMES)[None, :]
    allowed = (clip_ids[:, :, None] == clip_ids[:, None, :]) & (frame_col <= frame_row)
    time_bias = jnp.where(allowed, 0.0, -1000000000.0).astype(jnp.float32)[:, None, None, :, :]
    return (space_bias, time_bias)


def norm_gather(normed):
    return lax.all_gather(normed, "mp", axis=0, tiled=True)


def grad_gather(grad_rows):
    return lax.all_gather(grad_rows, "mp", axis=0, tiled=True)


def branch_scatter(values_bf, weight):
    return lax.psum_scatter(
        jnp.dot(values_bf, weight, preferred_element_type=jnp.float32).astype(jnp.bfloat16),
        "mp",
        scatter_dimension=0,
        tiled=True,
    ).astype(jnp.float32)


def input_scatter(grads_bf, weight):
    return lax.psum_scatter(
        lax.dot_general(grads_bf, weight, COLS_ONLY, preferred_element_type=jnp.float32).astype(
            jnp.bfloat16
        ),
        "mp",
        scatter_dimension=0,
        tiled=True,
    ).astype(jnp.float32)


def weight_grad(stored, grads_bf):
    return lax.dot_general(stored, grads_bf, ROWS_ONLY, preferred_element_type=jnp.float32)


def split_heads(projected, streams, frames):
    heads_dev = projected.shape[1] // (3 * HEAD_DIM)
    split = projected.reshape(streams, frames, -1, heads_dev, 3, HEAD_DIM)
    return (split[..., 0, :], split[..., 1, :], split[..., 2, :], heads_dev)


def attend_forward(projected, mask_bias, einsum_forms, streams, frames):
    queries, key_rows, value_rows, heads_dev = split_heads(projected, streams, frames)
    scores = (
        jnp.einsum(einsum_forms[0], queries, key_rows, preferred_element_type=jnp.float32)
        * HEAD_DIM ** (-0.5)
        + mask_bias
    )
    top_score = jnp.max(scores, axis=-1, keepdims=True)
    exponent = jnp.exp(scores - top_score)
    total = jnp.sum(exponent, axis=-1, keepdims=True)
    weights = exponent / total
    log_total = top_score + jnp.log(total)
    mixed_heads = jnp.einsum(
        einsum_forms[1],
        weights.astype(jnp.bfloat16),
        value_rows,
        preferred_element_type=jnp.float32,
    )
    return (mixed_heads.astype(jnp.bfloat16).reshape(-1, heads_dev * HEAD_DIM), log_total)


def attend_backward(projected, log_total, heads_grad, mask_bias, einsum_forms, streams, frames):
    queries, key_rows, value_rows, heads_dev = split_heads(projected, streams, frames)
    grad_heads = heads_grad.reshape(streams, frames, -1, heads_dev, HEAD_DIM)
    scale = HEAD_DIM ** (-0.5)
    scores = (
        jnp.einsum(einsum_forms[0], queries, key_rows, preferred_element_type=jnp.float32) * scale
        + mask_bias
    )
    weights = jnp.exp(scores - log_total)
    weights_grad = jnp.einsum(
        einsum_forms[0], grad_heads, value_rows, preferred_element_type=jnp.float32
    )
    inner = jnp.sum(weights * weights_grad, axis=-1, keepdims=True)
    score_grad = (weights * (weights_grad - inner)).astype(jnp.bfloat16)
    query_grad = (
        jnp.einsum(einsum_forms[1], score_grad, key_rows, preferred_element_type=jnp.float32)
        * scale
    ).astype(jnp.bfloat16)
    key_grad = (
        jnp.einsum(einsum_forms[2], score_grad, queries, preferred_element_type=jnp.float32) * scale
    ).astype(jnp.bfloat16)
    value_grad = jnp.einsum(
        einsum_forms[2],
        weights.astype(jnp.bfloat16),
        grad_heads,
        preferred_element_type=jnp.float32,
    ).astype(jnp.bfloat16)
    return jnp.stack([query_grad, key_grad, value_grad], axis=-2).reshape(projected.shape)


def block_forward(
    stream_in,
    ln_gain,
    ln_bias,
    w_qkv,
    w_out,
    w_up,
    w_down,
    mask_bias,
    einsum_forms,
    streams,
    frames,
):
    normed = layer_norm(stream_in, ln_gain[0], ln_bias[0]).astype(jnp.bfloat16)
    full_rows = norm_gather(normed)
    projected = jnp.dot(full_rows, w_qkv, preferred_element_type=jnp.float32).astype(jnp.bfloat16)
    mixed_heads, log_total = attend_forward(projected, mask_bias, einsum_forms, streams, frames)
    middle = stream_in + branch_scatter(mixed_heads, w_out)
    second = layer_norm(middle, ln_gain[1], ln_bias[1]).astype(jnp.bfloat16)
    second_full = norm_gather(second)
    hidden_pre = jnp.dot(second_full, w_up, preferred_element_type=jnp.float32)
    activated = jax.nn.gelu(hidden_pre).astype(jnp.bfloat16)
    result = middle + branch_scatter(activated, w_down)
    kept = (
        stream_in,
        full_rows,
        projected,
        mixed_heads,
        log_total,
        middle,
        second_full,
        hidden_pre,
        activated,
    )
    return (result, kept)


def block_backward(
    result_grad,
    kept,
    ln_gain,
    ln_bias,
    w_qkv,
    w_out,
    w_up,
    w_down,
    mask_bias,
    einsum_forms,
    streams,
    frames,
):
    (
        stream_in,
        first_store,
        projected,
        mixed_heads,
        log_total,
        middle,
        second_store,
        hidden_pre,
        activated,
    ) = kept
    result_low = result_grad.astype(jnp.bfloat16)
    gelu_pull = jax.vjp(jax.nn.gelu, hidden_pre)[1]
    down_in = grad_gather(result_low)
    grad_down = lax.dot_general(activated, down_in, ROWS_ONLY, preferred_element_type=jnp.float32)
    act_grad = lax.dot_general(down_in, w_down, COLS_ONLY, preferred_element_type=jnp.float32)
    hidden_grad = gelu_pull(act_grad)[0].astype(jnp.bfloat16)
    grad_up = weight_grad(second_store, hidden_grad)
    second_grad = input_scatter(hidden_grad, w_up)
    second_pull = jax.vjp(layer_norm, middle, ln_gain[1], ln_bias[1])[1]
    middle_part, gain_two, shift_two = second_pull(second_grad)
    middle_grad = result_grad + middle_part
    middle_low = middle_grad.astype(jnp.bfloat16)
    out_in = grad_gather(middle_low)
    grad_out = lax.dot_general(mixed_heads, out_in, ROWS_ONLY, preferred_element_type=jnp.float32)
    heads_grad = lax.dot_general(
        out_in, w_out, COLS_ONLY, preferred_element_type=jnp.float32
    ).astype(jnp.bfloat16)
    proj_grad = attend_backward(
        projected, log_total, heads_grad, mask_bias, einsum_forms, streams, frames
    )
    grad_qkv = weight_grad(first_store, proj_grad)
    first_grad = input_scatter(proj_grad, w_qkv)
    first_pull = jax.vjp(layer_norm, stream_in, ln_gain[0], ln_bias[0])[1]
    input_part, gain_one, shift_one = first_pull(first_grad)
    matrices = (grad_qkv, grad_out, grad_up, grad_down)
    return (
        middle_grad + input_part,
        matrices,
        jnp.stack([gain_one, gain_two]),
        jnp.stack([shift_one, shift_two]),
    )


def split_shards(tokens, out_grad, patch_valid, clip_ids, ln_gain, ln_bias, w_qkv, w_out, w_up, w_down):
    streams = patch_valid.shape[0]
    space_bias, time_bias = mask_biases(patch_valid, clip_ids)
    up_use, down_use = (w_up, w_down)
    weights = (w_qkv, w_out, up_use, down_use)
    layouts = ((streams, FRAMES, space_bias), (streams, FRAMES, time_bias))
    form_pair = (SPATIAL_FORMS, TEMPORAL_FORMS)
    state = tokens.astype(jnp.float32)
    kept_blocks = []
    for layer_index in range(2):
        group_count, frame_count, mask_bias = layouts[layer_index]
        state, kept = block_forward(
            state,
            ln_gain[layer_index],
            ln_bias[layer_index],
            weights[0][layer_index],
            weights[1][layer_index],
            weights[2][layer_index],
            weights[3][layer_index],
            mask_bias,
            form_pair[layer_index],
            group_count,
            frame_count,
        )
        kept_blocks.append(kept)
    layer_out = state.astype(jnp.bfloat16)
    grad_state = out_grad.astype(jnp.float32)
    matrix_grads = [None, None]
    gain_grads = [None, None]
    shift_grads = [None, None]
    for layer_index in (1, 0):
        group_count, frame_count, mask_bias = layouts[layer_index]
        grad_state, matrices, gain_part, shift_part = block_backward(
            grad_state,
            kept_blocks[layer_index],
            ln_gain[layer_index],
            ln_bias[layer_index],
            weights[0][layer_index],
            weights[1][layer_index],
            weights[2][layer_index],
            weights[3][layer_index],
            mask_bias,
            form_pair[layer_index],
            group_count,
            frame_count,
        )
        matrix_grads[layer_index] = matrices
        gain_grads[layer_index] = gain_part
        shift_grads[layer_index] = shift_part
    stacked = tuple(
        (jnp.stack([matrix_grads[0][item], matrix_grads[1][item]]) for item in range(4))
    )
    stacked = (
        lax.psum(stacked[0].astype(jnp.bfloat16), "dp").astype(jnp.float32),
        lax.psum(stacked[1].astype(jnp.bfloat16), "dp").astype(jnp.float32),
        lax.psum(stacked[2].astype(jnp.bfloat16), "dp").astype(jnp.float32),
        lax.psum(stacked[3].astype(jnp.bfloat16), "dp").astype(jnp.float32),
    )
    norm_sums = lax.psum((jnp.stack(gain_grads), jnp.stack(shift_grads)), ("dp", "mp"))
    return (
        layer_out,
        grad_state,
        norm_sums[0],
        norm_sums[1],
        stacked[0],
        stacked[1],
        stacked[2],
        stacked[3],
    )


def solution(mesh):
    dp, mp = mesh.shape["dp"], mesh.shape["mp"]
    if (dp, mp) != (16, 2):
        return on_mesh(split_shards, mesh, ("dp",), "mp")
    fine = Mesh(mesh.devices.reshape(4, 2, 2, 2), ("z", "y", "core", "mp"))
    return on_mesh(shards, fine, ("z", "y", "core"), "mp")


def on_mesh(body, mesh, dp, mp):
    both = dp + (mp,)
    return jax.shard_map(
        body,
        mesh=mesh,
        in_specs=(
            P(both, None),
            P(both, None),
            P(dp, None),
            P(dp, None),
            P(),
            P(),
            P(None, None, mp),
            P(None, mp, None),
            P(None, None, mp),
            P(None, mp, None),
        ),
        out_specs=(
            P(both, None),
            P(both, None),
            P(),
            P(),
            P(None, None, mp),
            P(None, mp, None),
            P(None, None, mp),
            P(None, mp, None),
        ),
        check_vma=False,
    )
```

```python
import functools

import jax
import jax.numpy as jnp
from jax import lax
from jax.experimental import pallas as pl
from jax.experimental.pallas import tpu as pltpu
from jax.sharding import Mesh
from jax.sharding import PartitionSpec as P

HEAD_DIM = 64
FRAMES = 4
EPS = 1e-05
SCALE = HEAD_DIM ** (-0.5)
F32 = jnp.float32
BF = jnp.bfloat16
VMEM_BYTES = 50 * 2**20
SMALL_BYTES = 44 * 2**20
SWAP = [(0, 1), (1, 0)]


def nn(a, b):
    return lax.dot_general(a, b, (((1,), (0,)), ((), ())), preferred_element_type=F32)


def nt(a, b):
    return lax.dot_general(a, b, (((1,), (1,)), ((), ())), preferred_element_type=F32)


def tn(a, b):
    return lax.dot_general(a, b, (((0,), (0,)), ((), ())), preferred_element_type=F32)


def cat(ref):
    return jnp.concatenate([ref[i] for i in range(ref.shape[0])], axis=1)


def put(ref, values):
    width = ref.shape[-1]
    for i in range(ref.shape[0]):
        ref[i] = values[:, i * width : (i + 1) * width].astype(ref.dtype)


def centred(values):
    centre = values - jnp.mean(values, axis=0, keepdims=True)
    rstd = lax.rsqrt(jnp.mean(centre * centre, axis=0, keepdims=True) + EPS)
    return centre * rstd, rstd


def norm_back(values, gain, grad, sums):
    hat, rstd = centred(values)
    scaled = grad * hat
    for k in range(values.shape[1] // 128):
        sums[0] += scaled[:, k * 128 : (k + 1) * 128]
        sums[1] += grad[:, k * 128 : (k + 1) * 128]
    inner = grad * gain
    return rstd * (
        inner
        - jnp.mean(inner, axis=0, keepdims=True)
        - hat * jnp.mean(inner * hat, axis=0, keepdims=True)
    )


def put_sums(ref, sums):
    ref[0:1, :] = jnp.sum(sums[0].T, axis=0, keepdims=True)
    ref[1:2, :] = jnp.sum(sums[1].T, axis=0, keepdims=True)


def gelu_pair(u):
    c0, c1 = 2 * 0.7978845608028654, 2 * 0.7978845608028654 * 0.044715
    square = u * u
    half = jax.nn.sigmoid(u * (c0 + c1 * square))
    g = u * half
    return g, half + (g * (1.0 - half)) * (c0 + (3 * c1) * square)


def spots(part, cols, width):
    found = []
    done = row = 0
    while cols - done >= width:
        found.append(((0, done), (part, width), (row, 0)))
        done += width
        row += part
    if done < cols:
        half, rest = part // 2, cols - done
        found.append(((0, done), (half, rest), (row, 0)))
        found.append(((half, done), (half, rest), (row, rest)))
    return found


def packed_rows(part, cols, width):
    return part * cols // width


def pack(block, width):
    part, cols = block.shape
    pieces = [block[:, c : c + width] for c in range(0, cols - width + 1, width)]
    rest = block[:, cols - cols % width :]
    if rest.shape[1]:
        pieces.append(jnp.concatenate([rest[: part // 2], rest[part // 2 :]], axis=1))
    return jnp.concatenate(pieces, axis=0)


def weight_copies(place, layer, first, second, near, far, first_v, second_v, sem):
    rows, width = first.shape[1], first.shape[2]
    part, cols = second.shape[1] // 4, second.shape[2]
    copies = [
        (first.at[layer], first_v.at[0:rows, :]),
        (second.at[layer], second_v.at[:, 0:cols]),
    ]
    for dc, pieces in enumerate((near, far)):
        for y in range(2):
            index = 2 * y + (place[1] ^ dc)
            start = pl.multiple_of(rows + index * (rows // 4), rows // 4)
            target = first_v.at[pl.ds(start, rows // 4), :]
            if len(pieces) == 2:
                copies.append((pieces[0].at[y], target))
                start = pl.multiple_of(index * part, part)
                copies.append(
                    (pieces[1].at[y], second_v.at[pl.ds(start, part), cols : 2 * cols])
                )
                continue
            (piece,) = pieces
            copies.append((piece.at[y, 0 : rows // 4, :], target))
            for (r, c), (h, w), (pr, pc) in spots(part, cols, width):
                start = pl.multiple_of(index * part + r, part // 2)
                pr += rows // 4
                copies.append(
                    (
                        piece.at[y, pr : pr + h, pc : pc + w],
                        second_v.at[pl.ds(start, h), cols + c : cols + c + w],
                    )
                )
    return [pltpu.make_async_copy(a, b, sem.at[i]) for i, (a, b) in enumerate(copies)]


def load_weights(*args):
    copies = weight_copies(*args)
    for copy in copies:
        copy.start()
    for copy in copies:
        copy.wait()


def put_blocks(place, keep, send, blocks, x_first):
    for core in range(2):

        @pl.when(place[1] == core)
        def _(core=core):
            for kind, dx, quarter, z, values, rows in blocks:
                dy, dz = place[0] ^ (quarter // 2), place[2] ^ z
                lead = (dx, dy) if x_first else (dy, dx)
                target = keep if quarter % 2 == core else send
                target[(kind, *lead, dz, rows)] = values.astype(BF)


def spatial_forward_kernel(
    layer, place, x_ref, bias_ref, norm_ref, wq, wo, near_o, near_q, far_o, far_q,
    p_ref, w_ref, inv_ref, o_ref, r_ref, a_ref, a2_ref, bias_v, wq_v, wo_v, sem,
):
    @pl.when(pl.program_id(0) == 0)
    def _():
        near, far = (near_o, near_q), (far_o, far_q)
        load_weights(place, layer, wo, wq, near, far, wo_v, wq_v, sem)

    patches = p_ref.shape[2]
    heads = wq_v.shape[1] // (3 * HEAD_DIM)
    bias_v[...] = jnp.broadcast_to(bias_ref[0], bias_v.shape)
    frames = range(p_ref.shape[0])
    xs = []
    for f in frames:
        x = x_ref[f * patches : (f + 1) * patches, :].astype(F32).T
        hat, _ = centred(x)
        a = (hat * norm_ref[:, 0:1] + norm_ref[:, 1:2]).astype(BF)
        a_ref[f] = a
        p_ref[f] = tn(wq_v[...], a).astype(BF)
        xs.append(x)

    def scores(f, h):
        base = h * 3 * HEAD_DIM
        q = (p_ref[f, base : base + HEAD_DIM, :] * SCALE).astype(BF)
        return tn(p_ref[f, base + HEAD_DIM : base + 2 * HEAD_DIM, :], q)

    def softmax(f, h, s):
        inverse = []
        for c in range(0, patches, 128):
            part = s[:, c : c + 128] + bias_v[...]
            e = jnp.exp(part - jnp.max(part, axis=0, keepdims=True))
            inverse.append(1.0 / jnp.sum(e, axis=0, keepdims=True))
            w_ref[f, h, :, c : c + 128] = e.astype(BF)
        inv_ref[f, h : h + 1, :] = jnp.concatenate(inverse, axis=1)

    def mix(f, h):
        base = h * 3 * HEAD_DIM
        v = p_ref[f, base + 2 * HEAD_DIM : base + 3 * HEAD_DIM, :]
        o = nn(v, w_ref[f, h]) * inv_ref[f, h : h + 1, :]
        o_ref[f, h * HEAD_DIM : (h + 1) * HEAD_DIM, :] = o.astype(BF)

    order = [(f, h) for f in frames for h in range(heads)]
    ahead = scores(*order[0])
    for i, at in enumerate(order):
        s = ahead
        if i + 1 < len(order):
            ahead = scores(*order[i + 1])
        if i:
            mix(*order[i - 1])
        softmax(*at, s)
    mix(*order[-1])
    for f in frames:
        r = xs[f] + tn(wo_v[...], o_ref[f])
        r_ref[f] = r.astype(r_ref.dtype)
        hat, _ = centred(r)
        a2_ref[f] = (hat * norm_ref[:, 2:3] + norm_ref[:, 3:4]).astype(BF)


def mlp_forward_kernel(
    layer, chunk, place, r_ref, a2_ref, wu, wd, near, far,
    x_ref, g_ref, slope_ref, wu_v, wd_v, sem,
):
    @pl.when(pl.program_id(0) == 0)
    def _():
        load_weights(place, layer, wd, wu, (near,), (far,), wd_v, wu_v, sem)

    a2 = cat(a2_ref)
    hidden = wu_v.shape[1]
    half = chunk // 2
    ahead = tn(wu_v[:, 0:half], a2)
    for j in range(0, hidden, half):
        u = ahead
        if j + half < hidden:
            ahead = tn(wu_v[:, j + half : j + 2 * half], a2)
        g, slope = gelu_pair(u)
        g_ref[j : j + half, :] = g.astype(BF)
        slope_ref[j : j + half, :] = slope.astype(BF)
    put(x_ref, cat(r_ref).astype(F32) + tn(wd_v[...], g_ref[...]))


def temporal_weights(p_ref, h, cols, clip_ref, stream):
    base = h * 3 * HEAD_DIM
    take = lambda f, c: p_ref[
        f, base + c * HEAD_DIM : base + (c + 1) * HEAD_DIM, cols
    ].astype(F32)
    q = [take(f, 0) for f in range(FRAMES)]
    k = [take(f, 1) for f in range(FRAMES)]
    v = [take(f, 2) for f in range(FRAMES)]
    weights = []
    for f in range(FRAMES):
        scores = []
        for g in range(f + 1):
            bias = jnp.where(clip_ref[stream, g] == clip_ref[stream, f], 0.0, -1000000000.0)
            scores.append(jnp.sum(q[f] * k[g], axis=0, keepdims=True) * SCALE + bias)
        top = functools.reduce(jnp.maximum, scores)
        e = [jnp.exp(s - top) for s in scores]
        inverse = 1.0 / functools.reduce(jnp.add, e)
        weights.append([x * inverse for x in e])
    return q, k, v, weights


def low(v):
    return v.astype(BF).astype(F32)


def temporal_forward_kernel(
    layer, place, clip_ref, x_ref, norm_ref, wq, wo, near, far,
    p_ref, o_ref, r_ref, a_ref, a2_ref, wq_v, wo_v, sem,
):
    @pl.when(pl.program_id(0) == 0)
    def _():
        load_weights(place, layer, wo, wq, (near,), (far,), wo_v, wq_v, sem)

    stream = pl.program_id(0)
    heads = wq_v.shape[1] // (3 * HEAD_DIM)
    patches = x_ref.shape[2]
    halves = [slice(c, c + 128) for c in range(0, patches, 128)]

    def project(cols):
        x = jnp.concatenate([x_ref[f, :, cols] for f in range(FRAMES)], axis=1).astype(F32)
        hat, _ = centred(x)
        a = (hat * norm_ref[:, 4:5] + norm_ref[:, 5:6]).astype(BF)
        p = tn(wq_v[...], a).astype(BF)
        for f in range(FRAMES):
            a_ref[f, :, cols] = a[:, f * 128 : (f + 1) * 128]
            p_ref[f, :, cols] = p[:, f * 128 : (f + 1) * 128]

    def mix(cols, h):
        _, _, v, weights = temporal_weights(p_ref, h, cols, clip_ref, stream)
        for f in range(FRAMES):
            o = functools.reduce(jnp.add, [low(w) * v[g] for g, w in enumerate(weights[f])])
            o_ref[f, h * HEAD_DIM : (h + 1) * HEAD_DIM, cols] = o.astype(BF)

    def finish(cols):
        o = jnp.concatenate([o_ref[f, :, cols] for f in range(FRAMES)], axis=1)
        x = jnp.concatenate([x_ref[f, :, cols] for f in range(FRAMES)], axis=1).astype(F32)
        r = x + tn(wo_v[...], o)
        hat, _ = centred(r)
        a2 = (hat * norm_ref[:, 6:7] + norm_ref[:, 7:8]).astype(BF)
        r = r.astype(BF)
        for f in range(FRAMES):
            r_ref[f, :, cols] = r[:, f * 128 : (f + 1) * 128]
            a2_ref[f, :, cols] = a2[:, f * 128 : (f + 1) * 128]

    project(halves[0])
    for i, cols in enumerate(halves):
        if i + 1 < len(halves):
            project(halves[i + 1])
        for h in range(heads):
            mix(cols, h)
        finish(cols)


def mlp_turn_kernel(
    layer, chunk, place, r_ref, a2_ref, y_ref, norm_ref, wu, wd, near, far,
    out_ref, dr_ref, dm_ref, g_ref, du_ref, ln_ref, sums, wu_v, wd_v, sem,
):
    @pl.when(pl.program_id(0) == 0)
    def _():
        load_weights(place, layer, wd, wu, (near,), (far,), wd_v, wu_v, sem)
        sums[...] = jnp.zeros_like(sums)

    a2 = cat(a2_ref)
    dm = y_ref[...].T
    put(dm_ref, dm)
    hidden = wu_v.shape[1]
    half = chunk // 2
    ahead = lambda j: (tn(wu_v[:, j : j + half], a2), nn(wd_v[j : j + half, :], dm))
    after = ahead(0)
    for j in range(0, hidden, half):
        u, dg = after
        if j + half < hidden:
            after = ahead(j + half)
        g, slope = gelu_pair(u)
        g_ref[j : j + half, :] = g.astype(BF)
        du_ref[j : j + half, :] = (dg * slope).astype(BF)
    r = cat(r_ref).astype(F32)
    back = nn(wu_v[...], du_ref[...])
    out = tn(wd_v[...], g_ref[...])
    put(dr_ref, dm.astype(F32) + norm_back(r, norm_ref[:, 6:7], back, sums))
    out_ref[...] = (r + out).astype(BF).T

    @pl.when(pl.program_id(0) == pl.num_programs(0) - 1)
    def _():
        put_sums(ln_ref, sums)


def mlp_back_kernel(
    layer, chunk, place, r_ref, y_ref, slope_ref, norm_ref, wu, wd, near, far,
    dr_ref, du_ref, ln_ref, sums, wu_v, wd_v, sem,
):
    @pl.when(pl.program_id(0) == 0)
    def _():
        load_weights(place, layer, wd, wu, (near,), (far,), wd_v, wu_v, sem)
        sums[...] = jnp.zeros_like(sums)

    dm = cat(y_ref)
    hidden = wu_v.shape[1]
    half = chunk // 2
    after = nn(wd_v[0:half, :], dm)
    for j in range(0, hidden, half):
        dg = after
        if j + half < hidden:
            after = nn(wd_v[j + half : j + 2 * half, :], dm)
        slope = slope_ref[j : j + half, :].astype(F32)
        du_ref[j : j + half, :] = (dg * slope).astype(BF)
    back = nn(wu_v[...], du_ref[...])
    r = cat(r_ref).astype(F32)
    put(dr_ref, dm.astype(F32) + norm_back(r, norm_ref[:, 2:3], back, sums))

    @pl.when(pl.program_id(0) == pl.num_programs(0) - 1)
    def _():
        put_sums(ln_ref, sums)


def mlp_grad_kernel(place, a2_ref, dm_ref, g_ref, du_ref, keep, send):
    step, steps = pl.program_id(0), pl.num_programs(0)
    dx, part = step // (steps // 2), lax.rem(step, steps // 2)
    chunk, width = g_ref.shape[0], dm_ref.shape[1]
    rows = keep.shape[4]
    quarters = chunk // (4 * rows)
    down = nt(g_ref[...], cat(dm_ref))
    up = nt(cat(a2_ref), du_ref[...])
    unit = width // 16
    spot = pl.ds(pl.multiple_of(part * unit, unit), unit)
    for core in range(2):

        @pl.when(place[1] == core)
        def _(core=core):
            for i in range(quarters):
                for z in range(4):
                    at = (4 * i + z) * rows
                    dy = place[0] ^ (part * (quarters // 2) + i // 2)
                    target = keep if i % 2 == core else send
                    target[0, dx, dy, place[2] ^ z] = down[at : at + rows].astype(BF)
            for quarter in range(4):
                for z in range(4):
                    at = (4 * quarter + z) * unit
                    dy = place[0] ^ (quarter // 2)
                    target = keep if quarter % 2 == core else send
                    target[1, dy, dx, place[2] ^ z, spot] = up[at : at + unit].astype(BF)


def temporal_back_kernel(
    layer, place, clip_ref, x_ref, y_ref, p_ref, norm_ref, wq, wo, near, far,
    dx_ref, dp_ref, ln_ref, sums, do_v, wq_v, wo_v, sem,
):
    @pl.when(pl.program_id(0) == 0)
    def _():
        load_weights(place, layer, wo, wq, (near,), (far,), wo_v, wq_v, sem)
        sums[...] = jnp.zeros_like(sums)

    stream = pl.program_id(0)
    heads = wq_v.shape[1] // (3 * HEAD_DIM)
    patches = x_ref.shape[2]
    halves = [slice(c, c + 128) for c in range(0, patches, 128)]
    gather = lambda ref, cols: jnp.concatenate([ref[f, :, cols] for f in range(FRAMES)], axis=1)

    def grad_heads(cols):
        do = nn(wo_v[...], gather(y_ref, cols)).astype(BF)
        for f in range(FRAMES):
            do_v[f, :, cols] = do[:, f * 128 : (f + 1) * 128]

    def one_head(cols, h):
        q, k, v, weights = temporal_weights(p_ref, h, cols, clip_ref, stream)
        base = h * 3 * HEAD_DIM
        rows = slice(h * HEAD_DIM, (h + 1) * HEAD_DIM)
        do = [do_v[f, rows, cols].astype(F32) for f in range(FRAMES)]
        dk = [0.0] * FRAMES
        dv = [0.0] * FRAMES
        for f in range(FRAMES):
            dw = [jnp.sum(do[f] * v[g], axis=0, keepdims=True) for g in range(f + 1)]
            inner = functools.reduce(jnp.add, [w * d for w, d in zip(weights[f], dw)])
            dq = 0.0
            for g in range(f + 1):
                ds = low(weights[f][g] * (dw[g] - inner)) * SCALE
                dq = dq + ds * k[g]
                dk[g] = dk[g] + ds * q[f]
                dv[g] = dv[g] + low(weights[f][g]) * do[f]
            dp_ref[f, base : base + HEAD_DIM, cols] = dq.astype(BF)
        for g in range(FRAMES):
            dp_ref[g, base + HEAD_DIM : base + 2 * HEAD_DIM, cols] = dk[g].astype(BF)
            dp_ref[g, base + 2 * HEAD_DIM : base + 3 * HEAD_DIM, cols] = dv[g].astype(BF)

    def finish(cols):
        inner = nn(wq_v[...], gather(dp_ref, cols))
        x, y = gather(x_ref, cols).astype(F32), gather(y_ref, cols).astype(F32)
        dx = (y + norm_back(x, norm_ref[:, 4:5], inner, sums)).astype(BF)
        for f in range(FRAMES):
            dx_ref[f, :, cols] = dx[:, f * 128 : (f + 1) * 128]

    grad_heads(halves[0])
    for i, cols in enumerate(halves):
        if i + 1 < len(halves):
            grad_heads(halves[i + 1])
        for h in range(heads):
            one_head(cols, h)
        finish(cols)

    @pl.when(pl.program_id(0) == pl.num_programs(0) - 1)
    def _():
        put_sums(ln_ref, sums)


def spatial_back_kernel(
    layer, place, y_ref, p_ref, w_ref, inv_ref, o_ref, wq, wo, near_o, near_q, far_o, far_q,
    dp_ref, do_v, inner_v, ds_v, wq_v, wo_v, sem,
):
    @pl.when(pl.program_id(0) == 0)
    def _():
        near, far = (near_o, near_q), (far_o, far_q)
        load_weights(place, layer, wo, wq, near, far, wo_v, wq_v, sem)

    heads = wq_v.shape[1] // (3 * HEAD_DIM)
    frames = range(p_ref.shape[0])
    for f in frames:
        do = nn(wo_v[...], y_ref[f]).astype(BF).astype(F32)
        for h in range(heads):
            rows = slice(h * HEAD_DIM, (h + 1) * HEAD_DIM)
            scaled = do[rows] * inv_ref[f, h : h + 1, :]
            inner = jnp.sum(scaled * o_ref[f, rows, :].astype(F32), axis=0, keepdims=True)
            inner_v[f, h : h + 1, :] = inner
            do_v[f, rows, :] = scaled.astype(BF)

    def grad_w(f, h):
        v = p_ref[f, (3 * h + 2) * HEAD_DIM : (3 * h + 3) * HEAD_DIM, :]
        return tn(v, do_v[f, h * HEAD_DIM : (h + 1) * HEAD_DIM, :])

    def grad_s(f, h, slot, dw):
        for c in range(0, dw.shape[1], 128):
            cols = slice(c, c + 128)
            w = w_ref[f, h, :, cols].astype(F32)
            ds_v[slot, :, cols] = (w * (dw[:, cols] - inner_v[f, h : h + 1, cols])).astype(BF)

    def grad_qkv(f, h, slot):
        base = h * 3 * HEAD_DIM
        q = (p_ref[f, base : base + HEAD_DIM, :] * SCALE).astype(BF)
        k = p_ref[f, base + HEAD_DIM : base + 2 * HEAD_DIM, :]
        ds = ds_v[slot]
        do = do_v[f, h * HEAD_DIM : (h + 1) * HEAD_DIM, :]
        dp_ref[f, base : base + HEAD_DIM, :] = (nn(k, ds) * SCALE).astype(BF)
        dp_ref[f, base + HEAD_DIM : base + 2 * HEAD_DIM, :] = nt(q, ds).astype(BF)
        dp_ref[f, base + 2 * HEAD_DIM : base + 3 * HEAD_DIM, :] = nt(do, w_ref[f, h]).astype(BF)

    order = [(f, h) for f in frames for h in range(heads)]
    ahead = grad_w(*order[0])
    for i, at in enumerate(order):
        dw = ahead
        if i + 1 < len(order):
            ahead = grad_w(*order[i + 1])
        if i:
            grad_qkv(*order[i - 1], (i - 1) % 2)
        grad_s(*at, i % 2, dw)
    grad_qkv(*order[-1], (len(order) - 1) % 2)


def input_grad_kernel(
    layer, place, x_ref, y_ref, dp_ref, norm_ref, wq, wo, near_o, near_q, far_o, far_q,
    dx_ref, ln_ref, sums, wq_v, wo_v, sem,
):
    @pl.when(pl.program_id(0) == 0)
    def _():
        near, far = (near_o, near_q), (far_o, far_q)
        load_weights(place, layer, wo, wq, near, far, wo_v, wq_v, sem)
        sums[...] = jnp.zeros_like(sums)

    patches = dp_ref.shape[2]
    inner = [nn(wq_v[...], dp_ref[f]) for f in range(dp_ref.shape[0])]
    for f in range(dp_ref.shape[0]):
        tokens = slice(f * patches, (f + 1) * patches)
        x = x_ref[tokens, :].astype(F32).T
        dx = y_ref[f].astype(F32) + norm_back(x, norm_ref[:, 0:1], inner[f], sums)
        dx_ref[tokens, :] = dx.T

    @pl.when(pl.program_id(0) == pl.num_programs(0) - 1)
    def _():
        put_sums(ln_ref, sums)


def attn_grad_kernel(place, a_ref, da_ref, o_ref, dp_ref, keep, send):
    dx = pl.program_id(0)
    width = da_ref.shape[1]
    out = nt(cat(o_ref), cat(da_ref))
    rows = out.shape[0] // 16
    blocks = []
    for quarter in range(4):
        for z in range(4):
            at = (4 * quarter + z) * rows
            blocks.append((0, dx, quarter, z, out[at : at + rows], slice(0, rows)))
    qkv = nt(cat(a_ref), cat(dp_ref))
    unit = qkv.shape[0] // 16
    for quarter in range(4):
        for z in range(4):
            at = (4 * quarter + z) * unit
            rows_of = {}
            for (r, c), (h, w), (pr, pc) in spots(unit, qkv.shape[1], width):
                rows_of.setdefault(pr, []).append(qkv[at + r : at + r + h, c : c + w])
            block = jnp.concatenate(
                [jnp.concatenate(rows_of[pr], axis=1) for pr in sorted(rows_of)], axis=0
            )
            spot = slice(rows, rows + block.shape[0])
            blocks.append((0, dx, quarter, z, block, spot))
    put_blocks(place, keep, send, blocks, True)


ANY = pl.BlockSpec(memory_space=pl.ANY)
SMEM = pl.BlockSpec(memory_space=pltpu.SMEM)
SEMS = pltpu.SemaphoreType.DMA((32,))


def whole(shape):
    zeros = (0,) * len(shape)
    return pl.BlockSpec(shape, lambda *_: zeros, pipeline_mode=pl.Buffered(1))


MARKS = {}


def call(body, name, grid, ins, outs, scratch, cost, after=(), aliases=None, vmem=None):
    flops, exps = cost
    count, inner = len(ins), body
    after = [MARKS[id(a)][1] if id(a) in MARKS else a for a in after]
    after = list({id(a): a for a in after}.values())
    end = count + len(after) + len(outs)
    body = lambda *refs: inner(*refs[:count], *refs[count + len(after) : end], *refs[end + 1 :])
    moved = sum(a.size * a.dtype.itemsize for a, _ in ins)
    shapes = [jax.ShapeDtypeStruct(shape, dtype) for shape, dtype, _ in outs]
    moved += sum(s.size * s.dtype.itemsize for s in shapes)
    shapes.append(jax.ShapeDtypeStruct((8, 128), F32))
    results = pl.pallas_call(
        body,
        grid=grid,
        in_specs=[spec for _, spec in ins] + [ANY] * len(after),
        out_specs=[spec for _, _, spec in outs] + [ANY],
        out_shape=shapes,
        scratch_shapes=scratch,
        compiler_params=pltpu.CompilerParams(
            vmem_limit_bytes=vmem or (VMEM_BYTES if scratch else SMALL_BYTES), dimension_semantics=("arbitrary",) * len(grid)
        ),
        cost_estimate=pl.CostEstimate(
            flops=int(flops), transcendentals=int(exps), bytes_accessed=int(moved)
        ),
        name=name,
        input_output_aliases=aliases or {},
    )(*[a for a, _ in ins], *after)
    *results, mark = results
    MARKS.update((id(r), (r, mark)) for r in results)
    return results


def held(mine, by_rows):
    rows, cols = mine.shape[1:]
    return pltpu.VMEM((2 * rows, cols) if by_rows else (rows, 2 * cols), BF)


def later(value, *others):
    return lax.optimization_barrier((value,) + others)[0]


def own_rows(weight, layer, core):
    part, cols = weight.shape[1] // 4, weight.shape[2]
    split = weight.reshape(weight.shape[0], 2, 2, part, cols)
    return lax.dynamic_slice(split, (layer, 0, core, 0, 0), (1, 2, 1, part, cols))[0, :, 0]


def own_quarters(first, second, layer, core):
    own = []
    for y in range(2):
        index = 2 * y + core
        parts = []
        for weight in (first, second):
            part = weight.shape[1] // 4
            spot = (layer, index * part, 0)
            block = lax.dynamic_slice(weight, spot, (1, part, weight.shape[2]))[0]
            parts.append(pack(block, first.shape[2]))
        own.append(jnp.concatenate(parts, axis=0))
    return jnp.stack(own)


def swap(value, axis):
    return lax.ppermute(value, axis, SWAP)


def swap_z(value, dz):
    return lax.ppermute(value, "z", [(i, i ^ dz) for i in range(4)])


def glue_kernel(jobs, count, *refs):
    ins, outs = refs[:count], refs[count:]
    for out, stack in zip(outs, jobs):
        for i, terms in enumerate(stack):
            total = functools.reduce(
                jnp.add, [ins[a][at].astype(F32) for a, at in terms]
            )
            spot = (i,) if len(stack) > 1 else (...,)
            out[spot] = total.astype(out.dtype)


def glue(name, arrays, jobs, after=()):
    outs = []
    for stack in jobs:
        a, at = stack[0][0]
        shape = arrays[a].shape[len(at) :] if at != (...,) else arrays[a].shape
        outs.append(((len(stack),) + shape if len(stack) > 1 else shape, arrays[a].dtype))
    return call(
        functools.partial(glue_kernel, jobs, len(arrays)), name, (1,),
        [(a, whole(a.shape)) for a in arrays],
        [(shape, dtype, whole(shape)) for shape, dtype in outs], [], (0, 0), after,
    )


class Sum:
    def __init__(self, name, keep, send):
        self.name, self.keep = name, keep
        self.kinds = keep.shape[0]
        self.out = send

    def start(self, *wait):
        self.got = swap(later(self.out, *wait), "core")

    def over_core(self, *wait):
        jobs = [[[(0, (k, side)), (1, (k, side))]] for side in (0, 1) for k in range(self.kinds)]
        outs = glue(self.name + "_core", [self.keep, self.got], jobs, wait)
        self.near, far = outs[: self.kinds], outs[self.kinds :]
        self.sent = far
        self.got = [swap(f, axis) for f, axis in zip(far, ("mp", "y"))]

    def over_first(self, *wait):
        kinds = self.kinds
        jobs = [
            [[(k, (side,)), (kinds + k, (side,))]] for side in (0, 1) for k in range(kinds)
        ]
        outs = glue(self.name + "_first", list(self.near) + self.got, jobs, wait)
        self.near, far = outs[:kinds], outs[kinds:]
        self.sent = far
        self.got = [swap(f, axis) for f, axis in zip(far, ("y", "mp"))]


def put_extra(message, rows, small):
    high = small.astype(BF)
    low_part = (small - high.astype(F32)).astype(BF)
    message[rows : rows + 16] = jnp.concatenate([high, low_part], axis=0)


def get_extra(message, rows):
    return message[rows : rows + 8].astype(F32) + message[rows + 8 : rows + 16].astype(F32)


def ride_core_kernel(keep, got, small, near, message):
    size = near.shape[2]
    rows = near.shape[0] * near.shape[1] * size
    near[...] = (keep[0, 0].astype(F32) + got[0, 0].astype(F32)).astype(BF)
    for dy in range(near.shape[0]):
        for dz in range(near.shape[1]):
            at = (dy * near.shape[1] + dz) * size
            total = keep[0, 1, dy, dz].astype(F32) + got[0, 1, dy, dz].astype(F32)
            message[at : at + size] = total.astype(BF)
    put_extra(message, rows, small[...])


def ride_first_kernel(near_in, got, small, near, message, total):
    size = near.shape[1]
    half = near.shape[0] * size
    total[...] = small[...] + get_extra(got, 2 * half)
    for dz in range(near.shape[0]):
        for dy in range(2):
            at = dz * size
            here = slice(dy * half + at, dy * half + at + size)
            value = (near_in[dy, dz].astype(F32) + got[here].astype(F32)).astype(BF)
            if dy:
                message[at : at + size] = value
            else:
                near[dz] = value
    put_extra(message, half, total[...])


def ride_second_kernel(near, got, small, *outs):
    size = near.shape[1]
    outs, total = outs[:4], outs[4]
    total[...] = small[...] + get_extra(got, 4 * size)
    for dz, out in enumerate(outs):
        here = slice(dz * size, (dz + 1) * size)
        out[0:size] = (near[dz].astype(F32) + got[here].astype(F32)).astype(BF)
        put_extra(out, size, total[...])


def joint_sum_kernel(own, a, b, c, small, near, total):
    rows = near.shape[0]
    terms = [r[0:rows].astype(F32) for r in (own, a, b, c)]
    near[...] = functools.reduce(jnp.add, terms).astype(BF)
    total[...] = functools.reduce(jnp.add, [get_extra(r, rows) for r in (a, b, c)], small[...])


def ride(body, name, ins, outs, after):
    specs = [(a, whole(a.shape)) for a in ins]
    return call(body, name, (1,), specs, [(s, d, whole(s)) for s, d in outs], [], (0, 0), after)


class Ride:
    def __init__(self, keep, send, small, *wait):
        self.keep, self.small = keep, small
        self.got = swap(later(send, *wait), "core")

    def over_core(self, *wait):
        shape = self.keep.shape[2:]
        flat = (shape[0] * shape[1] * shape[2] + 16, shape[3])
        self.near, message = ride(
            ride_core_kernel, "attn0_core", [self.keep, self.got, self.small],
            [(shape, BF), (flat, BF)], wait,
        )
        self.sent, self.got = [message], swap(message, "mp")

    def over_first(self, *wait):
        shape = self.near.shape[1:]
        flat = (shape[0] * shape[1] + 16, shape[2])
        self.near, message, self.small = ride(
            ride_first_kernel, "attn0_first", [self.near, self.got, self.small],
            [(shape, BF), (flat, BF), (self.small.shape, F32)], wait,
        )
        self.sent, self.got = [message], swap(message, "y")

    def over_second(self, *wait):
        flat = (self.near.shape[1] + 16, self.near.shape[2])
        *outs, self.small = ride(
            ride_second_kernel, "attn0_second", [self.near, self.got, self.small],
            [(flat, BF)] * 4 + [(self.small.shape, F32)], wait,
        )
        self.near, self.sent = outs[0], outs[1:]
        self.got = [swap_z(outs[dz], dz) for dz in (1, 2, 3)]

    def over_z(self, *wait):
        shape = (self.near.shape[0] - 16, self.near.shape[1])
        self.near, self.small = ride(
            joint_sum_kernel, "attn0_z", [self.near, *self.got, self.small],
            [(shape, BF), (self.small.shape, F32)], wait,
        )
        self.sent = [self.near]
        self.got = [swap_z(self.near, dz) for dz in (1, 2, 3)]

    def back_z(self, *wait):
        jobs = [[[(i, (...,))] for i in range(4)]]
        (self.near,) = glue("attn0_back", [self.near] + self.got, jobs, wait)
        self.sent = [self.near]
        self.got = swap(self.near, "y")

    def back_y(self, *wait):
        side = later(self.got, *wait)
        self.pieces = [self.near, swap(self.near, "core"), side, swap(side, "core")]


class Joint:
    def __init__(self, sums, *wait):
        self.name = sums[0].name
        arrays, pairs = [], []
        for part in sums:
            base = len(arrays)
            arrays += list(part.near) + part.got
            pairs += [(base + k, base + part.kinds + k) for k in range(part.kinds)]
        jobs = [[[(a, (dz,)), (b, (dz,))] for a, b in pairs] for dz in range(4)]
        outs = glue(self.name + "_second", arrays, jobs, wait)
        self.near, self.sent = outs[0], outs[1:]
        self.got = [swap_z(outs[dz], dz) for dz in (1, 2, 3)]

    def over_z(self, *wait):
        jobs = [[[(i, (...,)) for i in range(4)]]]
        (self.near,) = glue(self.name + "_z", [self.near] + self.got, jobs, wait)
        self.sent = [self.near]
        self.got = [swap_z(self.near, dz) for dz in (1, 2, 3)]

    def back_z(self, *wait):
        jobs = [[[(i, (...,))] for i in range(4)]]
        (self.near,) = glue(self.name + "_back", [self.near] + self.got, jobs, wait)
        self.sent = [self.near]
        self.got = swap(self.near, "y")

    def back_y(self, *wait):
        side = later(self.got, *wait)
        self.sent = [side]
        self.pieces = [self.near, swap(self.near, "core"), side, swap(side, "core")]


def finish_kernel(layer, kind, place, *refs):
    pieces, (first, second) = refs[:4], refs[-2:]
    width = first.shape[2]
    rows, unit, cols = first.shape[1] // 16, second.shape[1] // 16, second.shape[2]
    pair = kind == 0
    for dy in range(2):
        for dc in range(2):
            piece = pieces[2 * dy + dc]
            for dz in range(4):
                index = ((place[0] ^ dy) * 2 + (place[1] ^ dc)) * 4 + (place[2] ^ dz)
                at = lambda k: (dz, k) if len(piece.shape) == 4 else (dz,)
                start = pl.multiple_of(index * rows, rows)
                first[0, pl.ds(start, rows), :] = piece[(*at(kind), slice(0, rows))].astype(F32)
                lead, base = (at(1), 0) if pair else (at(kind), rows)
                for (r, c), (h, w), (pr, pc) in spots(unit, cols, width):
                    start = pl.multiple_of(index * unit + r, unit // 2)
                    pr += base
                    second[0, pl.ds(start, h), c : c + w] = piece[
                        (*lead, slice(pr, pr + h), slice(pc, pc + w))
                    ].astype(F32)


def finish(name, place, layer, kind, pieces, shapes, filled=(), after=()):
    ins = [(place, SMEM)] + [(p, whole(p.shape)) for p in pieces] + [(f, ANY) for f in filled]
    block = lambda s: pl.BlockSpec((1,) + s[1:], lambda i: (layer, 0, 0))
    outs = [(s, F32, block(s)) for s in shapes]
    aliases = {5 + i: i for i in range(len(filled))}
    body = functools.partial(finish_kernel, layer, kind)
    return call(body, name, (1,), ins, outs, [], (0, 0), after, aliases)


def shards(tokens, out_grad, patch_valid, clip_ids, ln_gain, ln_bias, w_qkv, w_out, w_up, w_down):
    MARKS.clear()
    z, y, core, mp = (lax.axis_index(a) for a in ("z", "y", "core", "mp"))
    place = jnp.stack([y, core, z]).astype(jnp.int32)
    n, width = tokens.shape
    patches = patch_valid.shape[1]
    frames = n // patches
    streams = frames // FRAMES
    hidden = 2 * w_up.shape[2]
    heads = 2 * w_qkv.shape[2] // (3 * HEAD_DIM)
    qkv = 2 * w_qkv.shape[2]
    inner = 2 * w_out.shape[1]

    attn, mlp = (w_out, w_qkv), (w_down, w_up)
    near_a0 = [swap(own_rows(w, 0, core), "mp") for w in attn]
    own_m0, own_a1, own_m1 = (
        own_quarters(*mlp, 0, core), own_quarters(*attn, 1, core), own_quarters(*mlp, 1, core)
    )
    near_m0 = swap(later(own_m0, *near_a0), "mp")
    got_a0 = near_a0 + [swap(near, "core") for near in near_a0]

    def attn_ins(got):
        return [(array, ANY) for array in (w_qkv, w_out, *got)]

    def mlp_ins(got):
        return [(array, ANY) for array in (w_up, w_down, *got)]

    valid = lax.dynamic_slice(patch_valid, (mp * streams, 0), (streams, patches))
    bias = jnp.where(valid == 1, 0.0, -1000000000.0).astype(F32)[:, :, None]
    clips = lax.dynamic_slice(clip_ids, (mp * streams, 0), (streams, FRAMES))
    norms = jnp.stack([ln_gain, ln_bias], axis=2).reshape(8, width).T

    attn_held = [held(w_qkv, False), held(w_out, True), SEMS]
    mlp_held = [held(w_up, False), held(w_down, True), SEMS]
    norm_in = (norms, whole(norms.shape))
    place_in = (place, SMEM)
    both = 2
    span = both * patches
    tiles = frames // both
    chunk = hidden // 4

    def rows(features):
        return pl.BlockSpec((both, features, patches), lambda i: (i, 0, 0))

    def columns(features):
        return pl.BlockSpec((FRAMES, features, patches), lambda i: (i, 0, 0))

    def flat(features):
        return pl.BlockSpec((features, span), lambda i: (0, i))

    act = lambda features: (frames, features, patches)
    full = lambda features: whole(act(features))
    token_rows = pl.BlockSpec((span, width), lambda i: (i, 0))
    bias_rows = pl.BlockSpec((1, patches, 1), lambda i: (i * both // FRAMES, 0, 0))
    ln_out = ((8, width), F32, whole((8, width)))
    sums = pltpu.VMEM((2, width, 128), F32)
    spatial_flops = 4 * n * patches * inner
    attn_flops = 2 * n * width * (qkv + inner)
    mlp_flops = 4 * n * width * hidden
    grad_shape = lambda kinds, size: (kinds, 2, 2, 4, size, width)
    mlp_grad = grad_shape(2, w_down.shape[1] // 16)
    attn_grad = grad_shape(1, w_out.shape[1] // 16 + w_qkv.shape[1] * w_qkv.shape[2] // width // 16)

    p0, w0, inv0, o0, r0, a0, b0 = call(
        functools.partial(spatial_forward_kernel, 0), "spatial_forward", (tiles,),
        [place_in, (tokens, token_rows), (bias, bias_rows), norm_in] + attn_ins(got_a0),
        [(act(qkv), BF, rows(qkv)),
         ((frames, heads, patches, patches), BF,
          pl.BlockSpec((both, heads, patches, patches), lambda i: (i, 0, 0, 0))),
         (act(heads), F32, rows(heads)),
         (act(inner), BF, rows(inner)), (act(width), BF, rows(width)),
         (act(width), BF, rows(width)), (act(width), BF, rows(width))],
        [pltpu.VMEM((patches, 128), F32)] + attn_held,
        (attn_flops + spatial_flops, n * patches * heads),
    )
    near_m0 = later(near_m0, r0)
    got_m0 = [near_m0, swap(near_m0, "core")]
    near_a1 = swap(later(own_a1, near_m0), "mp")
    near_m1 = swap(later(own_m1, near_m0), "mp")
    hid = (hidden, n)
    x1, g0, slope0 = call(
        functools.partial(mlp_forward_kernel, 0, chunk), "mlp_forward", (tiles,),
        [place_in, (r0, rows(width)), (b0, rows(width))] + mlp_ins(got_m0),
        [(act(width), BF, rows(width)), (hid, BF, flat(hidden)), (hid, BF, flat(hidden))],
        mlp_held, (mlp_flops, n * hidden),
    )

    near_a1 = later(near_a1, x1)
    got_a1 = [near_a1, swap(near_a1, "core")]
    clip_in = (clips, SMEM)
    grid1 = (streams,)
    p1, o1, r1, a1, b1 = call(
        functools.partial(temporal_forward_kernel, 1), "temporal_forward", grid1,
        [place_in, clip_in, (x1, columns(width)), norm_in] + attn_ins(got_a1),
        [(act(qkv), BF, columns(qkv)), (act(inner), BF, columns(inner)),
         (act(width), BF, columns(width)), (act(width), BF, columns(width)),
         (act(width), BF, columns(width))],
        attn_held, (attn_flops * 1.2, 0),
    )
    near_m1 = later(near_m1, r1)
    got_m1 = [near_m1, swap(near_m1, "core")]
    layer_out, dr1, dm1, g1, du1, ln11 = call(
        functools.partial(mlp_turn_kernel, 1, chunk), "mlp_turn", (tiles,),
        [place_in, (r1, rows(width)), (b1, rows(width)), (out_grad, token_rows), norm_in]
        + mlp_ins(got_m1),
        [((n, width), BF, token_rows), (act(width), BF, rows(width)),
         (act(width), BF, rows(width)), (hid, BF, flat(hidden)), (hid, BF, flat(hidden)), ln_out],
        [sums] + mlp_held, (2 * mlp_flops, n * hidden),
    )

    def mlp_grads(name, place, b, dm, g, du, after=()):
        block = pl.BlockSpec((chunk, n), lambda i: (i, 0))
        keep, send = call(
            mlp_grad_kernel, name, (hidden // chunk,),
            [(place, SMEM), (b, full(width)), (dm, full(width)), (g, block), (du, block)],
            [(mlp_grad, BF, whole(mlp_grad))] * 2, [], (mlp_flops, 0), after,
        )
        return keep, send

    def attn_grads(name, place, a, da, o, dp, after=()):
        half = lambda f: pl.BlockSpec((frames, f // 2, patches), lambda i: (0, i, 0))
        keep, send = call(
            attn_grad_kernel, name, (2,),
            [(place, SMEM), (a, full(width)), (da, full(width)), (o, half(inner)), (dp, half(qkv))],
            [(attn_grad, BF, whole(attn_grad))] * 2, [], (attn_flops, 0), after,
        )
        return keep, send

    mlp1 = Sum("mlp1", *mlp_grads("mlp1", place, b1, dm1, g1, du1))
    mlp1.start()
    dx1, dp1, ln10 = call(
        functools.partial(temporal_back_kernel, 1), "temporal_back", grid1,
        [place_in, clip_in, (x1, columns(width)), (dr1, columns(width)), (p1, columns(qkv)),
         norm_in] + attn_ins(got_a1),
        [(act(width), BF, columns(width)), (act(qkv), BF, columns(qkv)), ln_out],
        [sums, pltpu.VMEM((FRAMES, inner, patches), BF)] + attn_held, (1.4 * attn_flops, 0),
        [mlp1.keep],
    )
    mlp1.over_core(dx1)
    attn1 = Sum("attn1", *attn_grads("attn1", place, a1, dr1, o1, dp1, mlp1.sent))
    attn1.start()
    attn1.over_core()
    dr0, du0, ln01 = call(
        functools.partial(mlp_back_kernel, 0, chunk), "mlp_back", (tiles,),
        [place_in, (r0, rows(width)), (dx1, rows(width)), (slope0, flat(hidden)), norm_in]
        + mlp_ins(got_m0),
        [(act(width), BF, rows(width)), (hid, BF, flat(hidden)), ln_out],
        [sums] + mlp_held, (mlp_flops, 0), attn1.sent,
    )
    mlp1.over_first(dr0)
    attn1.over_first(*mlp1.sent)
    mlp0 = Sum("mlp0", *mlp_grads("mlp0", place, b0, dx1, g0, du0, attn1.sent))
    late = Joint([mlp1, attn1], mlp0.keep)
    mlp0.start(*late.sent)
    (dp0,) = call(
        functools.partial(spatial_back_kernel, 0), "spatial_back", (tiles,),
        [place_in, (dr0, rows(width)), (p0, rows(qkv)),
         (w0, pl.BlockSpec((both, heads, patches, patches), lambda i: (i, 0, 0, 0))),
         (inv0, rows(heads)), (o0, rows(inner))] + attn_ins(got_a0),
        [(act(qkv), BF, rows(qkv))],
        [pltpu.VMEM((both, inner, patches), BF), pltpu.VMEM((both, heads, patches), F32),
         pltpu.VMEM((2, patches, patches), BF)] + attn_held,
        (attn_flops + 2.5 * spatial_flops, 0), late.sent,
    )
    late.over_z(dp0)
    mlp0.over_core(*late.sent)
    input_grad, ln00 = call(
        functools.partial(input_grad_kernel, 0), "input_grad", (tiles,),
        [place_in, (tokens, token_rows), (dr0, rows(width)), (dp0, rows(qkv)), norm_in]
        + attn_ins(got_a0),
        [((n, width), F32, token_rows), ln_out],
        [sums] + attn_held, (attn_flops, 0), [*late.sent, *mlp0.sent],
    )
    mlp0.over_first(input_grad)
    keep, send = attn_grads("attn0", place, a0, dr0, o0, dp0, mlp0.sent)
    late.back_z(keep)
    mlp0 = Joint([mlp0], *late.sent)
    small = later(jnp.stack([ln00[:2], ln01[:2], ln10[:2], ln11[:2]]), *mlp0.sent)
    small = (small + swap(small, "core")).reshape(8, width)
    attn0 = Ride(keep, send, small, *mlp0.sent)
    attn0.over_core()
    attn0.over_first(*attn0.sent, *mlp0.got)
    mlp0.over_z(*attn0.sent)
    late.back_y(*mlp0.sent)
    attn0.over_second(*late.sent)
    mlp_shapes, attn_shapes = (w_down.shape, w_up.shape), (w_out.shape, w_qkv.shape)
    attn_filled = finish("finish_attn1", place, 1, 2, late.pieces, attn_shapes, (), attn0.sent)
    attn0.over_z(*mlp0.got, attn_filled[0])
    mlp0.back_z(*attn0.sent)
    mlp_filled = finish("finish_mlp1", place, 1, 0, late.pieces, mlp_shapes, (), mlp0.sent)
    attn0.back_z(*mlp0.sent, mlp_filled[0])
    mlp0.back_y(*attn0.sent)
    grad_down, grad_up = finish("finish_mlp0", place, 0, 0, mlp0.pieces, mlp_shapes, mlp_filled)
    attn0.back_y(grad_up)
    grad_out, grad_qkv = finish(
        "finish_attn0", place, 0, 2, attn0.pieces, attn_shapes, attn_filled
    )
    small = attn0.small.reshape(2, 2, 2, width)
    return (
        layer_out,
        input_grad,
        small[:, :, 0],
        small[:, :, 1],
        grad_qkv,
        grad_out,
        grad_up,
        grad_down,
    )


SPATIAL_FORMS = ("sfphe,sfqhe->sfhpq", "sfhpq,sfqhe->sfphe", "sfhpq,sfphe->sfqhe")
TEMPORAL_FORMS = ("sfphe,sgphe->sphfg", "sphfg,sgphe->sfphe", "sphfg,sfphe->sgphe")
ROWS_ONLY = (((0,), (0,)), ((), ()))
COLS_ONLY = (((1,), (1,)), ((), ()))


def layer_norm(values, ln_gain, ln_bias):
    centre = values - jnp.mean(values, axis=-1, keepdims=True)
    spread = jnp.mean(centre * centre, axis=-1, keepdims=True)
    return centre * lax.rsqrt(spread + 1e-05) * ln_gain + ln_bias


def mask_biases(patch_valid, clip_ids):
    space_bias = jnp.where(patch_valid == 1, 0.0, -1000000000.0).astype(jnp.float32)[
        :, None, None, None, :
    ]
    frame_row = jnp.arange(FRAMES)[:, None]
    frame_col = jnp.arange(FRAMES)[None, :]
    allowed = (clip_ids[:, :, None] == clip_ids[:, None, :]) & (frame_col <= frame_row)
    time_bias = jnp.where(allowed, 0.0, -1000000000.0).astype(jnp.float32)[:, None, None, :, :]
    return (space_bias, time_bias)


def norm_gather(normed):
    return lax.all_gather(normed, "mp", axis=0, tiled=True)


def grad_gather(grad_rows):
    return lax.all_gather(grad_rows, "mp", axis=0, tiled=True)


def branch_scatter(values_bf, weight):
    return lax.psum_scatter(
        jnp.dot(values_bf, weight, preferred_element_type=jnp.float32).astype(jnp.bfloat16),
        "mp",
        scatter_dimension=0,
        tiled=True,
    ).astype(jnp.float32)


def input_scatter(grads_bf, weight):
    return lax.psum_scatter(
        lax.dot_general(grads_bf, weight, COLS_ONLY, preferred_element_type=jnp.float32).astype(
            jnp.bfloat16
        ),
        "mp",
        scatter_dimension=0,
        tiled=True,
    ).astype(jnp.float32)


def weight_grad(stored, grads_bf):
    return lax.dot_general(stored, grads_bf, ROWS_ONLY, preferred_element_type=jnp.float32)


def split_heads(projected, streams, frames):
    heads_dev = projected.shape[1] // (3 * HEAD_DIM)
    split = projected.reshape(streams, frames, -1, heads_dev, 3, HEAD_DIM)
    return (split[..., 0, :], split[..., 1, :], split[..., 2, :], heads_dev)


def attend_forward(projected, mask_bias, einsum_forms, streams, frames):
    queries, key_rows, value_rows, heads_dev = split_heads(projected, streams, frames)
    scores = (
        jnp.einsum(einsum_forms[0], queries, key_rows, preferred_element_type=jnp.float32)
        * HEAD_DIM ** (-0.5)
        + mask_bias
    )
    top_score = jnp.max(scores, axis=-1, keepdims=True)
    exponent = jnp.exp(scores - top_score)
    total = jnp.sum(exponent, axis=-1, keepdims=True)
    weights = exponent / total
    log_total = top_score + jnp.log(total)
    mixed_heads = jnp.einsum(
        einsum_forms[1],
        weights.astype(jnp.bfloat16),
        value_rows,
        preferred_element_type=jnp.float32,
    )
    return (mixed_heads.astype(jnp.bfloat16).reshape(-1, heads_dev * HEAD_DIM), log_total)


def attend_backward(projected, log_total, heads_grad, mask_bias, einsum_forms, streams, frames):
    queries, key_rows, value_rows, heads_dev = split_heads(projected, streams, frames)
    grad_heads = heads_grad.reshape(streams, frames, -1, heads_dev, HEAD_DIM)
    scale = HEAD_DIM ** (-0.5)
    scores = (
        jnp.einsum(einsum_forms[0], queries, key_rows, preferred_element_type=jnp.float32) * scale
        + mask_bias
    )
    weights = jnp.exp(scores - log_total)
    weights_grad = jnp.einsum(
        einsum_forms[0], grad_heads, value_rows, preferred_element_type=jnp.float32
    )
    inner = jnp.sum(weights * weights_grad, axis=-1, keepdims=True)
    score_grad = (weights * (weights_grad - inner)).astype(jnp.bfloat16)
    query_grad = (
        jnp.einsum(einsum_forms[1], score_grad, key_rows, preferred_element_type=jnp.float32)
        * scale
    ).astype(jnp.bfloat16)
    key_grad = (
        jnp.einsum(einsum_forms[2], score_grad, queries, preferred_element_type=jnp.float32) * scale
    ).astype(jnp.bfloat16)
    value_grad = jnp.einsum(
        einsum_forms[2],
        weights.astype(jnp.bfloat16),
        grad_heads,
        preferred_element_type=jnp.float32,
    ).astype(jnp.bfloat16)
    return jnp.stack([query_grad, key_grad, value_grad], axis=-2).reshape(projected.shape)


def block_forward(
    stream_in,
    ln_gain,
    ln_bias,
    w_qkv,
    w_out,
    w_up,
    w_down,
    mask_bias,
    einsum_forms,
    streams,
    frames,
):
    normed = layer_norm(stream_in, ln_gain[0], ln_bias[0]).astype(jnp.bfloat16)
    full_rows = norm_gather(normed)
    projected = jnp.dot(full_rows, w_qkv, preferred_element_type=jnp.float32).astype(jnp.bfloat16)
    mixed_heads, log_total = attend_forward(projected, mask_bias, einsum_forms, streams, frames)
    middle = stream_in + branch_scatter(mixed_heads, w_out)
    second = layer_norm(middle, ln_gain[1], ln_bias[1]).astype(jnp.bfloat16)
    second_full = norm_gather(second)
    hidden_pre = jnp.dot(second_full, w_up, preferred_element_type=jnp.float32)
    activated = jax.nn.gelu(hidden_pre).astype(jnp.bfloat16)
    result = middle + branch_scatter(activated, w_down)
    kept = (
        stream_in,
        full_rows,
        projected,
        mixed_heads,
        log_total,
        middle,
        second_full,
        hidden_pre,
        activated,
    )
    return (result, kept)


def block_backward(
    result_grad,
    kept,
    ln_gain,
    ln_bias,
    w_qkv,
    w_out,
    w_up,
    w_down,
    mask_bias,
    einsum_forms,
    streams,
    frames,
):
    (
        stream_in,
        first_store,
        projected,
        mixed_heads,
        log_total,
        middle,
        second_store,
        hidden_pre,
        activated,
    ) = kept
    result_low = result_grad.astype(jnp.bfloat16)
    gelu_pull = jax.vjp(jax.nn.gelu, hidden_pre)[1]
    down_in = grad_gather(result_low)
    grad_down = lax.dot_general(activated, down_in, ROWS_ONLY, preferred_element_type=jnp.float32)
    act_grad = lax.dot_general(down_in, w_down, COLS_ONLY, preferred_element_type=jnp.float32)
    hidden_grad = gelu_pull(act_grad)[0].astype(jnp.bfloat16)
    grad_up = weight_grad(second_store, hidden_grad)
    second_grad = input_scatter(hidden_grad, w_up)
    second_pull = jax.vjp(layer_norm, middle, ln_gain[1], ln_bias[1])[1]
    middle_part, gain_two, shift_two = second_pull(second_grad)
    middle_grad = result_grad + middle_part
    middle_low = middle_grad.astype(jnp.bfloat16)
    out_in = grad_gather(middle_low)
    grad_out = lax.dot_general(mixed_heads, out_in, ROWS_ONLY, preferred_element_type=jnp.float32)
    heads_grad = lax.dot_general(
        out_in, w_out, COLS_ONLY, preferred_element_type=jnp.float32
    ).astype(jnp.bfloat16)
    proj_grad = attend_backward(
        projected, log_total, heads_grad, mask_bias, einsum_forms, streams, frames
    )
    grad_qkv = weight_grad(first_store, proj_grad)
    first_grad = input_scatter(proj_grad, w_qkv)
    first_pull = jax.vjp(layer_norm, stream_in, ln_gain[0], ln_bias[0])[1]
    input_part, gain_one, shift_one = first_pull(first_grad)
    matrices = (grad_qkv, grad_out, grad_up, grad_down)
    return (
        middle_grad + input_part,
        matrices,
        jnp.stack([gain_one, gain_two]),
        jnp.stack([shift_one, shift_two]),
    )


def split_shards(tokens, out_grad, patch_valid, clip_ids, ln_gain, ln_bias, w_qkv, w_out, w_up, w_down):
    streams = patch_valid.shape[0]
    space_bias, time_bias = mask_biases(patch_valid, clip_ids)
    up_use, down_use = (w_up, w_down)
    weights = (w_qkv, w_out, up_use, down_use)
    layouts = ((streams, FRAMES, space_bias), (streams, FRAMES, time_bias))
    form_pair = (SPATIAL_FORMS, TEMPORAL_FORMS)
    state = tokens.astype(jnp.float32)
    kept_blocks = []
    for layer_index in range(2):
        group_count, frame_count, mask_bias = layouts[layer_index]
        state, kept = block_forward(
            state,
            ln_gain[layer_index],
            ln_bias[layer_index],
            weights[0][layer_index],
            weights[1][layer_index],
            weights[2][layer_index],
            weights[3][layer_index],
            mask_bias,
            form_pair[layer_index],
            group_count,
            frame_count,
        )
        kept_blocks.append(kept)
    layer_out = state.astype(jnp.bfloat16)
    grad_state = out_grad.astype(jnp.float32)
    matrix_grads = [None, None]
    gain_grads = [None, None]
    shift_grads = [None, None]
    for layer_index in (1, 0):
        group_count, frame_count, mask_bias = layouts[layer_index]
        grad_state, matrices, gain_part, shift_part = block_backward(
            grad_state,
            kept_blocks[layer_index],
            ln_gain[layer_index],
            ln_bias[layer_index],
            weights[0][layer_index],
            weights[1][layer_index],
            weights[2][layer_index],
            weights[3][layer_index],
            mask_bias,
            form_pair[layer_index],
            group_count,
            frame_count,
        )
        matrix_grads[layer_index] = matrices
        gain_grads[layer_index] = gain_part
        shift_grads[layer_index] = shift_part
    stacked = tuple(
        (jnp.stack([matrix_grads[0][item], matrix_grads[1][item]]) for item in range(4))
    )
    stacked = (
        lax.psum(stacked[0].astype(jnp.bfloat16), "dp").astype(jnp.float32),
        lax.psum(stacked[1].astype(jnp.bfloat16), "dp").astype(jnp.float32),
        lax.psum(stacked[2].astype(jnp.bfloat16), "dp").astype(jnp.float32),
        lax.psum(stacked[3].astype(jnp.bfloat16), "dp").astype(jnp.float32),
    )
    norm_sums = lax.psum((jnp.stack(gain_grads), jnp.stack(shift_grads)), ("dp", "mp"))
    return (
        layer_out,
        grad_state,
        norm_sums[0],
        norm_sums[1],
        stacked[0],
        stacked[1],
        stacked[2],
        stacked[3],
    )


def solution(mesh):
    dp, mp = mesh.shape["dp"], mesh.shape["mp"]
    if (dp, mp) != (16, 2):
        return on_mesh(split_shards, mesh, ("dp",), "mp")
    fine = Mesh(mesh.devices.reshape(4, 2, 2, 2), ("z", "y", "core", "mp"))
    return on_mesh(shards, fine, ("z", "y", "core"), "mp")


def on_mesh(body, mesh, dp, mp):
    both = dp + (mp,)
    return jax.shard_map(
        body,
        mesh=mesh,
        in_specs=(
            P(both, None),
            P(both, None),
            P(dp, None),
            P(dp, None),
            P(),
            P(),
            P(None, None, mp),
            P(None, mp, None),
            P(None, None, mp),
            P(None, mp, None),
        ),
        out_specs=(
            P(both, None),
            P(both, None),
            P(),
            P(),
            P(None, None, mp),
            P(None, mp, None),
            P(None, None, mp),
            P(None, mp, None),
        ),
        check_vma=False,
    )
```

```python
import functools

import jax
import jax.numpy as jnp
from jax import lax
from jax.experimental import pallas as pl
from jax.experimental.pallas import tpu as pltpu
from jax.sharding import Mesh
from jax.sharding import PartitionSpec as P

HEAD_DIM = 64
FRAMES = 4
EPS = 1e-05
SCALE = HEAD_DIM ** (-0.5)
F32 = jnp.float32
BF = jnp.bfloat16
VMEM_BYTES = 50 * 2**20
SMALL_BYTES = 44 * 2**20
SWAP = [(0, 1), (1, 0)]


def nn(a, b):
    return lax.dot_general(a, b, (((1,), (0,)), ((), ())), preferred_element_type=F32)


def nt(a, b):
    return lax.dot_general(a, b, (((1,), (1,)), ((), ())), preferred_element_type=F32)


def tn(a, b):
    return lax.dot_general(a, b, (((0,), (0,)), ((), ())), preferred_element_type=F32)


def cat(ref):
    return jnp.concatenate([ref[i] for i in range(ref.shape[0])], axis=1)


def put(ref, values):
    width = ref.shape[-1]
    for i in range(ref.shape[0]):
        ref[i] = values[:, i * width : (i + 1) * width].astype(ref.dtype)


def centred(values):
    centre = values - jnp.mean(values, axis=0, keepdims=True)
    rstd = lax.rsqrt(jnp.mean(centre * centre, axis=0, keepdims=True) + EPS)
    return centre * rstd, rstd


def norm_back(values, gain, grad, sums):
    hat, rstd = centred(values)
    scaled = grad * hat
    for k in range(values.shape[1] // 128):
        sums[0] += scaled[:, k * 128 : (k + 1) * 128]
        sums[1] += grad[:, k * 128 : (k + 1) * 128]
    inner = grad * gain
    return rstd * (
        inner
        - jnp.mean(inner, axis=0, keepdims=True)
        - hat * jnp.mean(inner * hat, axis=0, keepdims=True)
    )


def put_sums(ref, sums):
    ref[0:1, :] = jnp.sum(sums[0].T, axis=0, keepdims=True)
    ref[1:2, :] = jnp.sum(sums[1].T, axis=0, keepdims=True)


def gelu_pair(u):
    c0, c1 = 2 * 0.7978845608028654, 2 * 0.7978845608028654 * 0.044715
    square = u * u
    half = jax.nn.sigmoid(u * (c0 + c1 * square))
    g = u * half
    return g, half + (g * (1.0 - half)) * (c0 + (3 * c1) * square)


def spots(part, cols, width):
    found = []
    done = row = 0
    while cols - done >= width:
        found.append(((0, done), (part, width), (row, 0)))
        done += width
        row += part
    if done < cols:
        half, rest = part // 2, cols - done
        found.append(((0, done), (half, rest), (row, 0)))
        found.append(((half, done), (half, rest), (row, rest)))
    return found


def packed_rows(part, cols, width):
    return part * cols // width


def pack(block, width):
    part, cols = block.shape
    pieces = [block[:, c : c + width] for c in range(0, cols - width + 1, width)]
    rest = block[:, cols - cols % width :]
    if rest.shape[1]:
        pieces.append(jnp.concatenate([rest[: part // 2], rest[part // 2 :]], axis=1))
    return jnp.concatenate(pieces, axis=0)


def weight_copies(place, layer, first, second, near, far, first_v, second_v, sem):
    rows, width = first.shape[1], first.shape[2]
    part, cols = second.shape[1] // 4, second.shape[2]
    copies = [
        (first.at[layer], first_v.at[0:rows, :]),
        (second.at[layer], second_v.at[:, 0:cols]),
    ]
    for dc, pieces in enumerate((near, far)):
        for y in range(2):
            index = 2 * y + (place[1] ^ dc)
            start = pl.multiple_of(rows + index * (rows // 4), rows // 4)
            target = first_v.at[pl.ds(start, rows // 4), :]
            if len(pieces) == 2:
                copies.append((pieces[0].at[y], target))
                start = pl.multiple_of(index * part, part)
                copies.append(
                    (pieces[1].at[y], second_v.at[pl.ds(start, part), cols : 2 * cols])
                )
                continue
            (piece,) = pieces
            copies.append((piece.at[y, 0 : rows // 4, :], target))
            for (r, c), (h, w), (pr, pc) in spots(part, cols, width):
                start = pl.multiple_of(index * part + r, part // 2)
                pr += rows // 4
                copies.append(
                    (
                        piece.at[y, pr : pr + h, pc : pc + w],
                        second_v.at[pl.ds(start, h), cols + c : cols + c + w],
                    )
                )
    return [pltpu.make_async_copy(a, b, sem.at[i]) for i, (a, b) in enumerate(copies)]


def begin_weights(*args):
    for copy in weight_copies(*args):
        copy.start()


def end_weights(*args):
    for copy in weight_copies(*args):
        copy.wait()


def load_weights(*args):
    begin_weights(*args)
    end_weights(*args)


def put_blocks(place, keep, send, blocks, x_first):
    for core in range(2):

        @pl.when(place[1] == core)
        def _(core=core):
            for kind, dx, quarter, z, values, rows in blocks:
                dy, dz = place[0] ^ (quarter // 2), place[2] ^ z
                lead = (dx, dy) if x_first else (dy, dx)
                target = keep if quarter % 2 == core else send
                target[(kind, *lead, dz, rows)] = values.astype(BF)


def spatial_forward_kernel(
    layer, place, x_ref, bias_ref, norm_ref, wq, wo, near_o, near_q, far_o, far_q,
    p_ref, w_ref, inv_ref, o_ref, r_ref, a_ref, a2_ref, bias_v, wq_v, wo_v, sem,
):
    args = (place, layer, wo, wq, (near_o, near_q), (far_o, far_q), wo_v, wq_v, sem)

    @pl.when(pl.program_id(0) == 0)
    def _():
        begin_weights(*args)

    patches = p_ref.shape[2]
    heads = wq_v.shape[1] // (3 * HEAD_DIM)
    bias_v[...] = jnp.broadcast_to(bias_ref[0], bias_v.shape)
    frames = range(p_ref.shape[0])
    xs = []
    for f in frames:
        x = x_ref[f * patches : (f + 1) * patches, :].astype(F32).T
        hat, _ = centred(x)
        a = (hat * norm_ref[:, 0:1] + norm_ref[:, 1:2]).astype(BF)
        a_ref[f] = a
        if f == 0:

            @pl.when(pl.program_id(0) == 0)
            def _():
                end_weights(*args)

        p_ref[f] = tn(wq_v[...], a).astype(BF)
        xs.append(x)

    def scores(f, h):
        base = h * 3 * HEAD_DIM
        q = (p_ref[f, base : base + HEAD_DIM, :] * SCALE).astype(BF)
        return tn(p_ref[f, base + HEAD_DIM : base + 2 * HEAD_DIM, :], q)

    def softmax(f, h, s):
        inverse = []
        for c in range(0, patches, 128):
            part = s[:, c : c + 128] + bias_v[...]
            e = jnp.exp(part - jnp.max(part, axis=0, keepdims=True))
            inverse.append(1.0 / jnp.sum(e, axis=0, keepdims=True))
            w_ref[f, h, :, c : c + 128] = e.astype(BF)
        inv_ref[f, h : h + 1, :] = jnp.concatenate(inverse, axis=1)

    def mix(f, h):
        base = h * 3 * HEAD_DIM
        v = p_ref[f, base + 2 * HEAD_DIM : base + 3 * HEAD_DIM, :]
        o = nn(v, w_ref[f, h]) * inv_ref[f, h : h + 1, :]
        o_ref[f, h * HEAD_DIM : (h + 1) * HEAD_DIM, :] = o.astype(BF)

    order = [(f, h) for f in frames for h in range(heads)]
    ahead = scores(*order[0])
    for i, at in enumerate(order):
        s = ahead
        if i + 1 < len(order):
            ahead = scores(*order[i + 1])
        if i:
            mix(*order[i - 1])
        softmax(*at, s)
    mix(*order[-1])
    for f in frames:
        r = xs[f] + tn(wo_v[...], o_ref[f])
        r_ref[f] = r.astype(r_ref.dtype)
        hat, _ = centred(r)
        a2_ref[f] = (hat * norm_ref[:, 2:3] + norm_ref[:, 3:4]).astype(BF)


def mlp_forward_kernel(
    layer, chunk, place, r_ref, a2_ref, wu, wd, near, far,
    x_ref, g_ref, slope_ref, wu_v, wd_v, sem,
):
    @pl.when(pl.program_id(0) == 0)
    def _():
        load_weights(place, layer, wd, wu, (near,), (far,), wd_v, wu_v, sem)

    a2 = cat(a2_ref)
    hidden = wu_v.shape[1]
    half = chunk // 2
    ahead = tn(wu_v[:, 0:half], a2)
    for j in range(0, hidden, half):
        u = ahead
        if j + half < hidden:
            ahead = tn(wu_v[:, j + half : j + 2 * half], a2)
        g, slope = gelu_pair(u)
        g_ref[j : j + half, :] = g.astype(BF)
        slope_ref[j : j + half, :] = slope.astype(BF)
    put(x_ref, cat(r_ref).astype(F32) + tn(wd_v[...], g_ref[...]))


def temporal_weights(p_ref, h, cols, clip_ref, stream):
    base = h * 3 * HEAD_DIM
    take = lambda f, c: p_ref[
        f, base + c * HEAD_DIM : base + (c + 1) * HEAD_DIM, cols
    ].astype(F32)
    q = [take(f, 0) for f in range(FRAMES)]
    k = [take(f, 1) for f in range(FRAMES)]
    v = [take(f, 2) for f in range(FRAMES)]
    weights = []
    for f in range(FRAMES):
        scores = []
        for g in range(f + 1):
            bias = jnp.where(clip_ref[stream, g] == clip_ref[stream, f], 0.0, -1000000000.0)
            scores.append(jnp.sum(q[f] * k[g], axis=0, keepdims=True) * SCALE + bias)
        top = functools.reduce(jnp.maximum, scores)
        e = [jnp.exp(s - top) for s in scores]
        inverse = 1.0 / functools.reduce(jnp.add, e)
        weights.append([x * inverse for x in e])
    return q, k, v, weights


def low(v):
    return v.astype(BF).astype(F32)


def temporal_forward_kernel(
    layer, place, clip_ref, x_ref, norm_ref, wq, wo, near, far,
    p_ref, o_ref, r_ref, a_ref, a2_ref, wq_v, wo_v, sem,
):
    args = (place, layer, wo, wq, (near,), (far,), wo_v, wq_v, sem)

    @pl.when(pl.program_id(0) == 0)
    def _():
        begin_weights(*args)

    stream = pl.program_id(0)
    heads = wq_v.shape[1] // (3 * HEAD_DIM)
    patches = x_ref.shape[2]
    halves = [slice(c, c + 128) for c in range(0, patches, 128)]

    def project(cols, ready=None):
        x = jnp.concatenate([x_ref[f, :, cols] for f in range(FRAMES)], axis=1).astype(F32)
        hat, _ = centred(x)
        a = (hat * norm_ref[:, 4:5] + norm_ref[:, 5:6]).astype(BF)
        if ready:
            pl.when(pl.program_id(0) == 0)(ready)
        p = tn(wq_v[...], a).astype(BF)
        for f in range(FRAMES):
            a_ref[f, :, cols] = a[:, f * 128 : (f + 1) * 128]
            p_ref[f, :, cols] = p[:, f * 128 : (f + 1) * 128]

    def mix(cols, h):
        _, _, v, weights = temporal_weights(p_ref, h, cols, clip_ref, stream)
        for f in range(FRAMES):
            o = functools.reduce(jnp.add, [low(w) * v[g] for g, w in enumerate(weights[f])])
            o_ref[f, h * HEAD_DIM : (h + 1) * HEAD_DIM, cols] = o.astype(BF)

    def finish(cols):
        o = jnp.concatenate([o_ref[f, :, cols] for f in range(FRAMES)], axis=1)
        x = jnp.concatenate([x_ref[f, :, cols] for f in range(FRAMES)], axis=1).astype(F32)
        r = x + tn(wo_v[...], o)
        hat, _ = centred(r)
        a2 = (hat * norm_ref[:, 6:7] + norm_ref[:, 7:8]).astype(BF)
        r = r.astype(BF)
        for f in range(FRAMES):
            r_ref[f, :, cols] = r[:, f * 128 : (f + 1) * 128]
            a2_ref[f, :, cols] = a2[:, f * 128 : (f + 1) * 128]

    project(halves[0], lambda: end_weights(*args))
    for i, cols in enumerate(halves):
        if i + 1 < len(halves):
            project(halves[i + 1])
        for h in range(heads):
            mix(cols, h)
        finish(cols)


def mlp_turn_kernel(
    layer, chunk, place, r_ref, a2_ref, y_ref, norm_ref, wu, wd, near, far,
    out_ref, dr_ref, dm_ref, g_ref, du_ref, ln_ref, sums, wu_v, wd_v, sem,
):
    args = (place, layer, wd, wu, (near,), (far,), wd_v, wu_v, sem)

    @pl.when(pl.program_id(0) == 0)
    def _():
        begin_weights(*args)
        sums[...] = jnp.zeros_like(sums)

    a2 = cat(a2_ref)
    dm = y_ref[...].T
    put(dm_ref, dm)

    @pl.when(pl.program_id(0) == 0)
    def _():
        end_weights(*args)

    hidden = wu_v.shape[1]
    half = chunk // 4
    ahead = lambda j: (tn(wu_v[:, j : j + half], a2), nn(wd_v[j : j + half, :], dm))
    after = ahead(0)
    for j in range(0, hidden, half):
        u, dg = after
        if j + half < hidden:
            after = ahead(j + half)
        g, slope = gelu_pair(u)
        g_ref[j : j + half, :] = g.astype(BF)
        du_ref[j : j + half, :] = (dg * slope).astype(BF)
    r = cat(r_ref).astype(F32)
    back = nn(wu_v[...], du_ref[...])
    out = tn(wd_v[...], g_ref[...])
    put(dr_ref, dm.astype(F32) + norm_back(r, norm_ref[:, 6:7], back, sums))
    out_ref[...] = (r + out).astype(BF).T

    @pl.when(pl.program_id(0) == pl.num_programs(0) - 1)
    def _():
        put_sums(ln_ref, sums)


def mlp_back_kernel(
    layer, chunk, place, r_ref, y_ref, slope_ref, norm_ref, wu, wd, near, far,
    dr_ref, du_ref, ln_ref, sums, wu_v, wd_v, sem,
):
    @pl.when(pl.program_id(0) == 0)
    def _():
        load_weights(place, layer, wd, wu, (near,), (far,), wd_v, wu_v, sem)
        sums[...] = jnp.zeros_like(sums)

    dm = cat(y_ref)
    hidden = wu_v.shape[1]
    half = chunk // 2
    after = nn(wd_v[0:half, :], dm)
    for j in range(0, hidden, half):
        dg = after
        if j + half < hidden:
            after = nn(wd_v[j + half : j + 2 * half, :], dm)
        slope = slope_ref[j : j + half, :].astype(F32)
        du_ref[j : j + half, :] = (dg * slope).astype(BF)
    back = nn(wu_v[...], du_ref[...])
    r = cat(r_ref).astype(F32)
    put(dr_ref, dm.astype(F32) + norm_back(r, norm_ref[:, 2:3], back, sums))

    @pl.when(pl.program_id(0) == pl.num_programs(0) - 1)
    def _():
        put_sums(ln_ref, sums)


def mlp_grad_kernel(place, a2_ref, dm_ref, g_ref, du_ref, keep, send):
    step, steps = pl.program_id(0), pl.num_programs(0)
    dx, part = step // (steps // 2), lax.rem(step, steps // 2)
    chunk, width = g_ref.shape[0], dm_ref.shape[1]
    rows = keep.shape[4]
    quarters = chunk // (4 * rows)
    down = nt(g_ref[...], cat(dm_ref))
    up = nt(cat(a2_ref), du_ref[...])
    unit = width // 16
    spot = pl.ds(pl.multiple_of(part * unit, unit), unit)
    for core in range(2):

        @pl.when(place[1] == core)
        def _(core=core):
            for i in range(quarters):
                for z in range(4):
                    at = (4 * i + z) * rows
                    dy = place[0] ^ (part * (quarters // 2) + i // 2)
                    target = keep if i % 2 == core else send
                    target[0, dx, dy, place[2] ^ z] = down[at : at + rows].astype(BF)
            for quarter in range(4):
                for z in range(4):
                    at = (4 * quarter + z) * unit
                    dy = place[0] ^ (quarter // 2)
                    target = keep if quarter % 2 == core else send
                    target[1, dy, dx, place[2] ^ z, spot] = up[at : at + unit].astype(BF)


def temporal_back_kernel(
    layer, place, clip_ref, x_ref, y_ref, p_ref, norm_ref, wq, wo, near, far,
    dx_ref, dp_ref, ln_ref, sums, do_v, wq_v, wo_v, sem,
):
    @pl.when(pl.program_id(0) == 0)
    def _():
        load_weights(place, layer, wo, wq, (near,), (far,), wo_v, wq_v, sem)
        sums[...] = jnp.zeros_like(sums)

    stream = pl.program_id(0)
    heads = wq_v.shape[1] // (3 * HEAD_DIM)
    patches = x_ref.shape[2]
    halves = [slice(c, c + 128) for c in range(0, patches, 128)]
    gather = lambda ref, cols: jnp.concatenate([ref[f, :, cols] for f in range(FRAMES)], axis=1)

    def grad_heads(cols):
        do = nn(wo_v[...], gather(y_ref, cols)).astype(BF)
        for f in range(FRAMES):
            do_v[f, :, cols] = do[:, f * 128 : (f + 1) * 128]

    def one_head(cols, h):
        q, k, v, weights = temporal_weights(p_ref, h, cols, clip_ref, stream)
        base = h * 3 * HEAD_DIM
        rows = slice(h * HEAD_DIM, (h + 1) * HEAD_DIM)
        do = [do_v[f, rows, cols].astype(F32) for f in range(FRAMES)]
        dk = [0.0] * FRAMES
        dv = [0.0] * FRAMES
        for f in range(FRAMES):
            dw = [jnp.sum(do[f] * v[g], axis=0, keepdims=True) for g in range(f + 1)]
            inner = functools.reduce(jnp.add, [w * d for w, d in zip(weights[f], dw)])
            dq = 0.0
            for g in range(f + 1):
                ds = low(weights[f][g] * (dw[g] - inner)) * SCALE
                dq = dq + ds * k[g]
                dk[g] = dk[g] + ds * q[f]
                dv[g] = dv[g] + low(weights[f][g]) * do[f]
            dp_ref[f, base : base + HEAD_DIM, cols] = dq.astype(BF)
        for g in range(FRAMES):
            dp_ref[g, base + HEAD_DIM : base + 2 * HEAD_DIM, cols] = dk[g].astype(BF)
            dp_ref[g, base + 2 * HEAD_DIM : base + 3 * HEAD_DIM, cols] = dv[g].astype(BF)

    def finish(cols):
        inner = nn(wq_v[...], gather(dp_ref, cols))
        x, y = gather(x_ref, cols).astype(F32), gather(y_ref, cols).astype(F32)
        dx = (y + norm_back(x, norm_ref[:, 4:5], inner, sums)).astype(BF)
        for f in range(FRAMES):
            dx_ref[f, :, cols] = dx[:, f * 128 : (f + 1) * 128]

    grad_heads(halves[0])
    for i, cols in enumerate(halves):
        if i + 1 < len(halves):
            grad_heads(halves[i + 1])
        for h in range(heads):
            one_head(cols, h)
        finish(cols)

    @pl.when(pl.program_id(0) == pl.num_programs(0) - 1)
    def _():
        put_sums(ln_ref, sums)


def spatial_back_kernel(
    layer, place, y_ref, p_ref, w_ref, inv_ref, o_ref, wq, wo, near_o, near_q, far_o, far_q,
    dp_ref, do_v, inner_v, ds_v, wq_v, wo_v, sem,
):
    @pl.when(pl.program_id(0) == 0)
    def _():
        near, far = (near_o, near_q), (far_o, far_q)
        load_weights(place, layer, wo, wq, near, far, wo_v, wq_v, sem)

    heads = wq_v.shape[1] // (3 * HEAD_DIM)
    frames = range(p_ref.shape[0])
    for f in frames:
        do = nn(wo_v[...], y_ref[f]).astype(BF).astype(F32)
        for h in range(heads):
            rows = slice(h * HEAD_DIM, (h + 1) * HEAD_DIM)
            scaled = do[rows] * inv_ref[f, h : h + 1, :]
            inner = jnp.sum(scaled * o_ref[f, rows, :].astype(F32), axis=0, keepdims=True)
            inner_v[f, h : h + 1, :] = inner
            do_v[f, rows, :] = scaled.astype(BF)

    def grad_w(f, h):
        v = p_ref[f, (3 * h + 2) * HEAD_DIM : (3 * h + 3) * HEAD_DIM, :]
        return tn(v, do_v[f, h * HEAD_DIM : (h + 1) * HEAD_DIM, :])

    def grad_s(f, h, slot, dw):
        for c in range(0, dw.shape[1], 128):
            cols = slice(c, c + 128)
            w = w_ref[f, h, :, cols].astype(F32)
            ds_v[slot, :, cols] = (w * (dw[:, cols] - inner_v[f, h : h + 1, cols])).astype(BF)

    def grad_qkv(f, h, slot):
        base = h * 3 * HEAD_DIM
        q = (p_ref[f, base : base + HEAD_DIM, :] * SCALE).astype(BF)
        k = p_ref[f, base + HEAD_DIM : base + 2 * HEAD_DIM, :]
        ds = ds_v[slot]
        do = do_v[f, h * HEAD_DIM : (h + 1) * HEAD_DIM, :]
        dp_ref[f, base : base + HEAD_DIM, :] = (nn(k, ds) * SCALE).astype(BF)
        dp_ref[f, base + HEAD_DIM : base + 2 * HEAD_DIM, :] = nt(q, ds).astype(BF)
        dp_ref[f, base + 2 * HEAD_DIM : base + 3 * HEAD_DIM, :] = nt(do, w_ref[f, h]).astype(BF)

    order = [(f, h) for f in frames for h in range(heads)]
    ahead = grad_w(*order[0])
    for i, at in enumerate(order):
        dw = ahead
        if i + 1 < len(order):
            ahead = grad_w(*order[i + 1])
        if i:
            grad_qkv(*order[i - 1], (i - 1) % 2)
        grad_s(*at, i % 2, dw)
    grad_qkv(*order[-1], (len(order) - 1) % 2)


def input_grad_kernel(
    layer, place, x_ref, y_ref, dp_ref, norm_ref, wq, wo, near_o, near_q, far_o, far_q,
    dx_ref, ln_ref, sums, wq_v, wo_v, sem,
):
    args = (place, layer, wo, wq, (near_o, near_q), (far_o, far_q), wo_v, wq_v, sem)

    @pl.when(pl.program_id(0) == 0)
    def _():
        begin_weights(*args)
        sums[...] = jnp.zeros_like(sums)

    patches = dp_ref.shape[2]
    xs = []
    for f in range(dp_ref.shape[0]):
        xs.append(x_ref[f * patches : (f + 1) * patches, :].astype(F32).T)

    @pl.when(pl.program_id(0) == 0)
    def _():
        end_weights(*args)

    inner = [nn(wq_v[...], dp_ref[f]) for f in range(dp_ref.shape[0])]
    for f in range(dp_ref.shape[0]):
        tokens = slice(f * patches, (f + 1) * patches)
        dx = y_ref[f].astype(F32) + norm_back(xs[f], norm_ref[:, 0:1], inner[f], sums)
        dx_ref[tokens, :] = dx.T

    @pl.when(pl.program_id(0) == pl.num_programs(0) - 1)
    def _():
        put_sums(ln_ref, sums)


def attn_grad_kernel(place, a_ref, da_ref, o_ref, dp_ref, keep, send):
    dx = pl.program_id(0)
    width = da_ref.shape[1]
    out = nt(cat(o_ref), cat(da_ref))
    rows = out.shape[0] // 16
    blocks = []
    for quarter in range(4):
        for z in range(4):
            at = (4 * quarter + z) * rows
            blocks.append((0, dx, quarter, z, out[at : at + rows], slice(0, rows)))
    qkv = nt(cat(a_ref), cat(dp_ref))
    unit = qkv.shape[0] // 16
    for quarter in range(4):
        for z in range(4):
            at = (4 * quarter + z) * unit
            rows_of = {}
            for (r, c), (h, w), (pr, pc) in spots(unit, qkv.shape[1], width):
                rows_of.setdefault(pr, []).append(qkv[at + r : at + r + h, c : c + w])
            block = jnp.concatenate(
                [jnp.concatenate(rows_of[pr], axis=1) for pr in sorted(rows_of)], axis=0
            )
            spot = slice(rows, rows + block.shape[0])
            blocks.append((0, dx, quarter, z, block, spot))
    put_blocks(place, keep, send, blocks, True)


ANY = pl.BlockSpec(memory_space=pl.ANY)
SMEM = pl.BlockSpec(memory_space=pltpu.SMEM)
SEMS = pltpu.SemaphoreType.DMA((32,))


def whole(shape):
    zeros = (0,) * len(shape)
    return pl.BlockSpec(shape, lambda *_: zeros, pipeline_mode=pl.Buffered(1))


MARKS = {}


def call(body, name, grid, ins, outs, scratch, cost, after=(), aliases=None, vmem=None):
    flops, exps = cost
    count, inner = len(ins), body
    after = [MARKS[id(a)][1] if id(a) in MARKS else a for a in after]
    after = list({id(a): a for a in after}.values())
    end = count + len(after) + len(outs)
    body = lambda *refs: inner(*refs[:count], *refs[count + len(after) : end], *refs[end + 1 :])
    moved = sum(a.size * a.dtype.itemsize for a, _ in ins)
    shapes = [jax.ShapeDtypeStruct(shape, dtype) for shape, dtype, _ in outs]
    moved += sum(s.size * s.dtype.itemsize for s in shapes)
    shapes.append(jax.ShapeDtypeStruct((8, 128), F32))
    results = pl.pallas_call(
        body,
        grid=grid,
        in_specs=[spec for _, spec in ins] + [ANY] * len(after),
        out_specs=[spec for _, _, spec in outs] + [ANY],
        out_shape=shapes,
        scratch_shapes=scratch,
        compiler_params=pltpu.CompilerParams(
            vmem_limit_bytes=vmem or (VMEM_BYTES if scratch else SMALL_BYTES), dimension_semantics=("arbitrary",) * len(grid)
        ),
        cost_estimate=pl.CostEstimate(
            flops=int(flops), transcendentals=int(exps), bytes_accessed=int(moved)
        ),
        name=name,
        input_output_aliases=aliases or {},
    )(*[a for a, _ in ins], *after)
    *results, mark = results
    MARKS.update((id(r), (r, mark)) for r in results)
    return results


def held(mine, by_rows):
    rows, cols = mine.shape[1:]
    return pltpu.VMEM((2 * rows, cols) if by_rows else (rows, 2 * cols), BF)


def later(value, *others):
    return lax.optimization_barrier((value,) + others)[0]


def own_rows(weight, layer, core):
    part, cols = weight.shape[1] // 4, weight.shape[2]
    split = weight.reshape(weight.shape[0], 2, 2, part, cols)
    return lax.dynamic_slice(split, (layer, 0, core, 0, 0), (1, 2, 1, part, cols))[0, :, 0]


def own_quarters(first, second, layer, core):
    own = []
    for y in range(2):
        index = 2 * y + core
        parts = []
        for weight in (first, second):
            part = weight.shape[1] // 4
            spot = (layer, index * part, 0)
            block = lax.dynamic_slice(weight, spot, (1, part, weight.shape[2]))[0]
            parts.append(pack(block, first.shape[2]))
        own.append(jnp.concatenate(parts, axis=0))
    return jnp.stack(own)


def swap(value, axis):
    return lax.ppermute(value, axis, SWAP)


def swap_z(value, dz):
    return lax.ppermute(value, "z", [(i, i ^ dz) for i in range(4)])


def glue_kernel(jobs, count, *refs):
    ins, outs = refs[:count], refs[count:]
    for out, stack in zip(outs, jobs):
        for i, terms in enumerate(stack):
            total = functools.reduce(
                jnp.add, [ins[a][at].astype(F32) for a, at in terms]
            )
            spot = (i,) if len(stack) > 1 else (...,)
            out[spot] = total.astype(out.dtype)


def glue(name, arrays, jobs, after=()):
    outs = []
    for stack in jobs:
        a, at = stack[0][0]
        shape = arrays[a].shape[len(at) :] if at != (...,) else arrays[a].shape
        outs.append(((len(stack),) + shape if len(stack) > 1 else shape, arrays[a].dtype))
    return call(
        functools.partial(glue_kernel, jobs, len(arrays)), name, (1,),
        [(a, whole(a.shape)) for a in arrays],
        [(shape, dtype, whole(shape)) for shape, dtype in outs], [], (0, 0), after,
    )


class Sum:
    def __init__(self, name, keep, send):
        self.name, self.keep = name, keep
        self.kinds = keep.shape[0]
        self.out = send

    def start(self, *wait):
        self.got = swap(later(self.out, *wait), "core")

    def over_core(self, *wait):
        jobs = [[[(0, (k, side)), (1, (k, side))]] for side in (0, 1) for k in range(self.kinds)]
        outs = glue(self.name + "_core", [self.keep, self.got], jobs, wait)
        self.near, far = outs[: self.kinds], outs[self.kinds :]
        self.sent = far
        self.got = [swap(f, axis) for f, axis in zip(far, ("mp", "y"))]

    def over_first(self, *wait):
        kinds = self.kinds
        jobs = [
            [[(k, (side,)), (kinds + k, (side,))]] for side in (0, 1) for k in range(kinds)
        ]
        outs = glue(self.name + "_first", list(self.near) + self.got, jobs, wait)
        self.near, far = outs[:kinds], outs[kinds:]
        self.sent = far
        self.got = [swap(f, axis) for f, axis in zip(far, ("y", "mp"))]


def put_extra(message, rows, small):
    high = small.astype(BF)
    low_part = (small - high.astype(F32)).astype(BF)
    message[rows : rows + 16] = jnp.concatenate([high, low_part], axis=0)


def get_extra(message, rows):
    return message[rows : rows + 8].astype(F32) + message[rows + 8 : rows + 16].astype(F32)


def ride_core_kernel(keep, got, small, near, message):
    size = near.shape[2]
    rows = near.shape[0] * near.shape[1] * size
    near[...] = (keep[0, 0].astype(F32) + got[0, 0].astype(F32)).astype(BF)
    for dy in range(near.shape[0]):
        for dz in range(near.shape[1]):
            at = (dy * near.shape[1] + dz) * size
            total = keep[0, 1, dy, dz].astype(F32) + got[0, 1, dy, dz].astype(F32)
            message[at : at + size] = total.astype(BF)
    put_extra(message, rows, small[...])


def ride_first_kernel(near_in, got, small, near, message, total):
    size = near.shape[1]
    half = near.shape[0] * size
    total[...] = small[...] + get_extra(got, 2 * half)
    for dz in range(near.shape[0]):
        for dy in range(2):
            at = dz * size
            here = slice(dy * half + at, dy * half + at + size)
            value = (near_in[dy, dz].astype(F32) + got[here].astype(F32)).astype(BF)
            if dy:
                message[at : at + size] = value
            else:
                near[dz] = value
    put_extra(message, half, total[...])


def ride_second_kernel(near, got, small, *outs):
    size = near.shape[1]
    outs, total = outs[:4], outs[4]
    total[...] = small[...] + get_extra(got, 4 * size)
    for dz, out in enumerate(outs):
        here = slice(dz * size, (dz + 1) * size)
        out[0:size] = (near[dz].astype(F32) + got[here].astype(F32)).astype(BF)
        put_extra(out, size, total[...])


def joint_sum_kernel(own, a, b, c, small, near, total):
    rows = near.shape[0]
    terms = [r[0:rows].astype(F32) for r in (own, a, b, c)]
    near[...] = functools.reduce(jnp.add, terms).astype(BF)
    total[...] = functools.reduce(jnp.add, [get_extra(r, rows) for r in (a, b, c)], small[...])


def ride(body, name, ins, outs, after):
    specs = [(a, whole(a.shape)) for a in ins]
    return call(body, name, (1,), specs, [(s, d, whole(s)) for s, d in outs], [], (0, 0), after)


class Ride:
    def __init__(self, keep, send, small, *wait):
        self.keep, self.small = keep, small
        self.got = swap(later(send, *wait), "core")

    def over_core(self, *wait):
        shape = self.keep.shape[2:]
        flat = (shape[0] * shape[1] * shape[2] + 16, shape[3])
        self.near, message = ride(
            ride_core_kernel, "attn0_core", [self.keep, self.got, self.small],
            [(shape, BF), (flat, BF)], wait,
        )
        self.sent, self.got = [message], swap(message, "mp")

    def over_first(self, *wait):
        shape = self.near.shape[1:]
        flat = (shape[0] * shape[1] + 16, shape[2])
        self.near, message, self.small = ride(
            ride_first_kernel, "attn0_first", [self.near, self.got, self.small],
            [(shape, BF), (flat, BF), (self.small.shape, F32)], wait,
        )
        self.sent, self.got = [message], swap(message, "y")

    def over_second(self, *wait):
        flat = (self.near.shape[1] + 16, self.near.shape[2])
        *outs, self.small = ride(
            ride_second_kernel, "attn0_second", [self.near, self.got, self.small],
            [(flat, BF)] * 4 + [(self.small.shape, F32)], wait,
        )
        self.near, self.sent = outs[0], outs[1:]
        self.got = [swap_z(outs[dz], dz) for dz in (1, 2, 3)]

    def over_z(self, *wait):
        shape = (self.near.shape[0] - 16, self.near.shape[1])
        self.near, self.small = ride(
            joint_sum_kernel, "attn0_z", [self.near, *self.got, self.small],
            [(shape, BF), (self.small.shape, F32)], wait,
        )
        self.sent = [self.near]
        self.got = [swap_z(self.near, dz) for dz in (1, 2, 3)]

    def back_z(self, *wait):
        jobs = [[[(i, (...,))] for i in range(4)]]
        (self.near,) = glue("attn0_back", [self.near] + self.got, jobs, wait)
        self.sent = [self.near]
        self.got = swap(self.near, "y")

    def back_y(self, *wait):
        side = later(self.got, *wait)
        self.pieces = [self.near, swap(self.near, "core"), side, swap(side, "core")]


class Joint:
    def __init__(self, sums, *wait):
        self.name = sums[0].name
        arrays, pairs = [], []
        for part in sums:
            base = len(arrays)
            arrays += list(part.near) + part.got
            pairs += [(base + k, base + part.kinds + k) for k in range(part.kinds)]
        jobs = [[[(a, (dz,)), (b, (dz,))] for a, b in pairs] for dz in range(4)]
        outs = glue(self.name + "_second", arrays, jobs, wait)
        self.near, self.sent = outs[0], outs[1:]
        self.got = [swap_z(outs[dz], dz) for dz in (1, 2, 3)]

    def over_z(self, *wait):
        jobs = [[[(i, (...,)) for i in range(4)]]]
        (self.near,) = glue(self.name + "_z", [self.near] + self.got, jobs, wait)
        self.sent = [self.near]
        self.got = [swap_z(self.near, dz) for dz in (1, 2, 3)]

    def back_z(self, *wait):
        jobs = [[[(i, (...,))] for i in range(4)]]
        (self.near,) = glue(self.name + "_back", [self.near] + self.got, jobs, wait)
        self.sent = [self.near]
        self.got = swap(self.near, "y")

    def back_y(self, *wait):
        side = later(self.got, *wait)
        self.sent = [side]
        self.pieces = [self.near, swap(self.near, "core"), side, swap(side, "core")]


def finish_kernel(layer, kind, place, *refs):
    pieces, (first, second) = refs[:4], refs[-2:]
    width = first.shape[2]
    rows, unit, cols = first.shape[1] // 16, second.shape[1] // 16, second.shape[2]
    pair = kind == 0
    for dy in range(2):
        for dc in range(2):
            piece = pieces[2 * dy + dc]
            for dz in range(4):
                index = ((place[0] ^ dy) * 2 + (place[1] ^ dc)) * 4 + (place[2] ^ dz)
                at = lambda k: (dz, k) if len(piece.shape) == 4 else (dz,)
                start = pl.multiple_of(index * rows, rows)
                first[0, pl.ds(start, rows), :] = piece[(*at(kind), slice(0, rows))].astype(F32)
                lead, base = (at(1), 0) if pair else (at(kind), rows)
                for (r, c), (h, w), (pr, pc) in spots(unit, cols, width):
                    start = pl.multiple_of(index * unit + r, unit // 2)
                    pr += base
                    second[0, pl.ds(start, h), c : c + w] = piece[
                        (*lead, slice(pr, pr + h), slice(pc, pc + w))
                    ].astype(F32)


def finish(name, place, layer, kind, pieces, shapes, filled=(), after=()):
    ins = [(place, SMEM)] + [(p, whole(p.shape)) for p in pieces] + [(f, ANY) for f in filled]
    block = lambda s: pl.BlockSpec((1,) + s[1:], lambda i: (layer, 0, 0))
    outs = [(s, F32, block(s)) for s in shapes]
    aliases = {5 + i: i for i in range(len(filled))}
    body = functools.partial(finish_kernel, layer, kind)
    return call(body, name, (1,), ins, outs, [], (0, 0), after, aliases)


def shards(tokens, out_grad, patch_valid, clip_ids, ln_gain, ln_bias, w_qkv, w_out, w_up, w_down):
    MARKS.clear()
    z, y, core, mp = (lax.axis_index(a) for a in ("z", "y", "core", "mp"))
    place = jnp.stack([y, core, z]).astype(jnp.int32)
    n, width = tokens.shape
    patches = patch_valid.shape[1]
    frames = n // patches
    streams = frames // FRAMES
    hidden = 2 * w_up.shape[2]
    heads = 2 * w_qkv.shape[2] // (3 * HEAD_DIM)
    qkv = 2 * w_qkv.shape[2]
    inner = 2 * w_out.shape[1]

    attn, mlp = (w_out, w_qkv), (w_down, w_up)
    near_a0 = [swap(own_rows(w, 0, core), "mp") for w in attn]
    own_m0, own_a1, own_m1 = (
        own_quarters(*mlp, 0, core), own_quarters(*attn, 1, core), own_quarters(*mlp, 1, core)
    )
    near_m0 = swap(later(own_m0, *near_a0), "mp")
    got_a0 = near_a0 + [swap(near, "core") for near in near_a0]

    def attn_ins(got):
        return [(array, ANY) for array in (w_qkv, w_out, *got)]

    def mlp_ins(got):
        return [(array, ANY) for array in (w_up, w_down, *got)]

    valid = lax.dynamic_slice(patch_valid, (mp * streams, 0), (streams, patches))
    bias = jnp.where(valid == 1, 0.0, -1000000000.0).astype(F32)[:, :, None]
    clips = lax.dynamic_slice(clip_ids, (mp * streams, 0), (streams, FRAMES))
    norms = jnp.stack([ln_gain, ln_bias], axis=2).reshape(8, width).T

    attn_held = [held(w_qkv, False), held(w_out, True), SEMS]
    mlp_held = [held(w_up, False), held(w_down, True), SEMS]
    norm_in = (norms, whole(norms.shape))
    place_in = (place, SMEM)
    both = 2
    span = both * patches
    tiles = frames // both
    chunk = hidden // 4

    def rows(features):
        return pl.BlockSpec((both, features, patches), lambda i: (i, 0, 0))

    def columns(features):
        return pl.BlockSpec((FRAMES, features, patches), lambda i: (i, 0, 0))

    def flat(features):
        return pl.BlockSpec((features, span), lambda i: (0, i))

    act = lambda features: (frames, features, patches)
    full = lambda features: whole(act(features))
    token_rows = pl.BlockSpec((span, width), lambda i: (i, 0))
    bias_rows = pl.BlockSpec((1, patches, 1), lambda i: (i * both // FRAMES, 0, 0))
    ln_out = ((8, width), F32, whole((8, width)))
    sums = pltpu.VMEM((2, width, 128), F32)
    spatial_flops = 4 * n * patches * inner
    attn_flops = 2 * n * width * (qkv + inner)
    mlp_flops = 4 * n * width * hidden
    grad_shape = lambda kinds, size: (kinds, 2, 2, 4, size, width)
    mlp_grad = grad_shape(2, w_down.shape[1] // 16)
    attn_grad = grad_shape(1, w_out.shape[1] // 16 + w_qkv.shape[1] * w_qkv.shape[2] // width // 16)

    p0, w0, inv0, o0, r0, a0, b0 = call(
        functools.partial(spatial_forward_kernel, 0), "spatial_forward", (tiles,),
        [place_in, (tokens, token_rows), (bias, bias_rows), norm_in] + attn_ins(got_a0),
        [(act(qkv), BF, rows(qkv)),
         ((frames, heads, patches, patches), BF,
          pl.BlockSpec((both, heads, patches, patches), lambda i: (i, 0, 0, 0))),
         (act(heads), F32, rows(heads)),
         (act(inner), BF, rows(inner)), (act(width), BF, rows(width)),
         (act(width), BF, rows(width)), (act(width), BF, rows(width))],
        [pltpu.VMEM((patches, 128), F32)] + attn_held,
        (attn_flops + spatial_flops, n * patches * heads),
    )
    near_m0 = later(near_m0, r0)
    got_m0 = [near_m0, swap(near_m0, "core")]
    near_a1 = swap(later(own_a1, near_m0), "mp")
    near_m1 = swap(later(own_m1, near_m0), "mp")
    hid = (hidden, n)
    x1, g0, slope0 = call(
        functools.partial(mlp_forward_kernel, 0, chunk), "mlp_forward", (tiles,),
        [place_in, (r0, rows(width)), (b0, rows(width))] + mlp_ins(got_m0),
        [(act(width), BF, rows(width)), (hid, BF, flat(hidden)), (hid, BF, flat(hidden))],
        mlp_held, (mlp_flops, n * hidden),
    )

    near_a1 = later(near_a1, x1)
    got_a1 = [near_a1, swap(near_a1, "core")]
    clip_in = (clips, SMEM)
    grid1 = (streams,)
    p1, o1, r1, a1, b1 = call(
        functools.partial(temporal_forward_kernel, 1), "temporal_forward", grid1,
        [place_in, clip_in, (x1, columns(width)), norm_in] + attn_ins(got_a1),
        [(act(qkv), BF, columns(qkv)), (act(inner), BF, columns(inner)),
         (act(width), BF, columns(width)), (act(width), BF, columns(width)),
         (act(width), BF, columns(width))],
        attn_held, (attn_flops * 1.2, 0),
    )
    near_m1 = later(near_m1, r1)
    got_m1 = [near_m1, swap(near_m1, "core")]
    layer_out, dr1, dm1, g1, du1, ln11 = call(
        functools.partial(mlp_turn_kernel, 1, chunk), "mlp_turn", (tiles,),
        [place_in, (r1, rows(width)), (b1, rows(width)), (out_grad, token_rows), norm_in]
        + mlp_ins(got_m1),
        [((n, width), BF, token_rows), (act(width), BF, rows(width)),
         (act(width), BF, rows(width)), (hid, BF, flat(hidden)), (hid, BF, flat(hidden)), ln_out],
        [sums] + mlp_held, (2 * mlp_flops, n * hidden),
    )

    def mlp_grads(name, place, b, dm, g, du, after=()):
        block = pl.BlockSpec((chunk, n), lambda i: (i, 0))
        keep, send = call(
            mlp_grad_kernel, name, (hidden // chunk,),
            [(place, SMEM), (b, full(width)), (dm, full(width)), (g, block), (du, block)],
            [(mlp_grad, BF, whole(mlp_grad))] * 2, [], (mlp_flops, 0), after,
        )
        return keep, send

    def attn_grads(name, place, a, da, o, dp, after=()):
        half = lambda f: pl.BlockSpec((frames, f // 2, patches), lambda i: (0, i, 0))
        keep, send = call(
            attn_grad_kernel, name, (2,),
            [(place, SMEM), (a, full(width)), (da, full(width)), (o, half(inner)), (dp, half(qkv))],
            [(attn_grad, BF, whole(attn_grad))] * 2, [], (attn_flops, 0), after,
        )
        return keep, send

    mlp1 = Sum("mlp1", *mlp_grads("mlp1", place, b1, dm1, g1, du1))
    mlp1.start()
    dx1, dp1, ln10 = call(
        functools.partial(temporal_back_kernel, 1), "temporal_back", grid1,
        [place_in, clip_in, (x1, columns(width)), (dr1, columns(width)), (p1, columns(qkv)),
         norm_in] + attn_ins(got_a1),
        [(act(width), BF, columns(width)), (act(qkv), BF, columns(qkv)), ln_out],
        [sums, pltpu.VMEM((FRAMES, inner, patches), BF)] + attn_held, (1.4 * attn_flops, 0),
        [mlp1.keep],
    )
    mlp1.over_core(dx1)
    attn1 = Sum("attn1", *attn_grads("attn1", place, a1, dr1, o1, dp1, mlp1.sent))
    attn1.start()
    attn1.over_core()
    dr0, du0, ln01 = call(
        functools.partial(mlp_back_kernel, 0, chunk), "mlp_back", (tiles,),
        [place_in, (r0, rows(width)), (dx1, rows(width)), (slope0, flat(hidden)), norm_in]
        + mlp_ins(got_m0),
        [(act(width), BF, rows(width)), (hid, BF, flat(hidden)), ln_out],
        [sums] + mlp_held, (mlp_flops, 0), attn1.sent,
    )
    mlp1.over_first(dr0)
    attn1.over_first(*mlp1.sent)
    mlp0 = Sum("mlp0", *mlp_grads("mlp0", place, b0, dx1, g0, du0, attn1.sent))
    late = Joint([mlp1, attn1], mlp0.keep)
    mlp0.start(*late.sent)
    (dp0,) = call(
        functools.partial(spatial_back_kernel, 0), "spatial_back", (tiles,),
        [place_in, (dr0, rows(width)), (p0, rows(qkv)),
         (w0, pl.BlockSpec((both, heads, patches, patches), lambda i: (i, 0, 0, 0))),
         (inv0, rows(heads)), (o0, rows(inner))] + attn_ins(got_a0),
        [(act(qkv), BF, rows(qkv))],
        [pltpu.VMEM((both, inner, patches), BF), pltpu.VMEM((both, heads, patches), F32),
         pltpu.VMEM((2, patches, patches), BF)] + attn_held,
        (attn_flops + 2.5 * spatial_flops, 0), late.sent,
    )
    late.over_z(dp0)
    mlp0.over_core(*late.sent)
    input_grad, ln00 = call(
        functools.partial(input_grad_kernel, 0), "input_grad", (tiles,),
        [place_in, (tokens, token_rows), (dr0, rows(width)), (dp0, rows(qkv)), norm_in]
        + attn_ins(got_a0),
        [((n, width), F32, token_rows), ln_out],
        [sums] + attn_held, (attn_flops, 0), [*late.sent, *mlp0.sent],
    )
    mlp0.over_first(input_grad)
    keep, send = attn_grads("attn0", place, a0, dr0, o0, dp0, mlp0.sent)
    late.back_z(keep)
    mlp0 = Joint([mlp0], *late.sent)
    small = later(jnp.stack([ln00[:2], ln01[:2], ln10[:2], ln11[:2]]), *mlp0.sent)
    small = (small + swap(small, "core")).reshape(8, width)
    attn0 = Ride(keep, send, small, *mlp0.sent)
    attn0.over_core()
    mlp0.over_z(*attn0.sent)
    attn0.over_first(*mlp0.sent)
    late.back_y(*attn0.sent)
    attn0.over_second(*late.sent)
    mlp_shapes, attn_shapes = (w_down.shape, w_up.shape), (w_out.shape, w_qkv.shape)
    attn_filled = finish("finish_attn1", place, 1, 2, late.pieces, attn_shapes, (), attn0.sent)
    attn0.over_z(*mlp0.got, attn_filled[0])
    mlp0.back_z(*attn0.sent)
    mlp_filled = finish("finish_mlp1", place, 1, 0, late.pieces, mlp_shapes, (), mlp0.sent)
    attn0.back_z(*mlp0.sent, mlp_filled[0])
    mlp0.back_y(*attn0.sent)
    grad_down, grad_up = finish("finish_mlp0", place, 0, 0, mlp0.pieces, mlp_shapes, mlp_filled)
    attn0.back_y(grad_up)
    grad_out, grad_qkv = finish(
        "finish_attn0", place, 0, 2, attn0.pieces, attn_shapes, attn_filled
    )
    small = attn0.small.reshape(2, 2, 2, width)
    return (
        layer_out,
        input_grad,
        small[:, :, 0],
        small[:, :, 1],
        grad_qkv,
        grad_out,
        grad_up,
        grad_down,
    )


SPATIAL_FORMS = ("sfphe,sfqhe->sfhpq", "sfhpq,sfqhe->sfphe", "sfhpq,sfphe->sfqhe")
TEMPORAL_FORMS = ("sfphe,sgphe->sphfg", "sphfg,sgphe->sfphe", "sphfg,sfphe->sgphe")
ROWS_ONLY = (((0,), (0,)), ((), ()))
COLS_ONLY = (((1,), (1,)), ((), ()))


def layer_norm(values, ln_gain, ln_bias):
    centre = values - jnp.mean(values, axis=-1, keepdims=True)
    spread = jnp.mean(centre * centre, axis=-1, keepdims=True)
    return centre * lax.rsqrt(spread + 1e-05) * ln_gain + ln_bias


def mask_biases(patch_valid, clip_ids):
    space_bias = jnp.where(patch_valid == 1, 0.0, -1000000000.0).astype(jnp.float32)[
        :, None, None, None, :
    ]
    frame_row = jnp.arange(FRAMES)[:, None]
    frame_col = jnp.arange(FRAMES)[None, :]
    allowed = (clip_ids[:, :, None] == clip_ids[:, None, :]) & (frame_col <= frame_row)
    time_bias = jnp.where(allowed, 0.0, -1000000000.0).astype(jnp.float32)[:, None, None, :, :]
    return (space_bias, time_bias)


def norm_gather(normed):
    return lax.all_gather(normed, "mp", axis=0, tiled=True)


def grad_gather(grad_rows):
    return lax.all_gather(grad_rows, "mp", axis=0, tiled=True)


def branch_scatter(values_bf, weight):
    return lax.psum_scatter(
        jnp.dot(values_bf, weight, preferred_element_type=jnp.float32).astype(jnp.bfloat16),
        "mp",
        scatter_dimension=0,
        tiled=True,
    ).astype(jnp.float32)


def input_scatter(grads_bf, weight):
    return lax.psum_scatter(
        lax.dot_general(grads_bf, weight, COLS_ONLY, preferred_element_type=jnp.float32).astype(
            jnp.bfloat16
        ),
        "mp",
        scatter_dimension=0,
        tiled=True,
    ).astype(jnp.float32)


def weight_grad(stored, grads_bf):
    return lax.dot_general(stored, grads_bf, ROWS_ONLY, preferred_element_type=jnp.float32)


def split_heads(projected, streams, frames):
    heads_dev = projected.shape[1] // (3 * HEAD_DIM)
    split = projected.reshape(streams, frames, -1, heads_dev, 3, HEAD_DIM)
    return (split[..., 0, :], split[..., 1, :], split[..., 2, :], heads_dev)


def attend_forward(projected, mask_bias, einsum_forms, streams, frames):
    queries, key_rows, value_rows, heads_dev = split_heads(projected, streams, frames)
    scores = (
        jnp.einsum(einsum_forms[0], queries, key_rows, preferred_element_type=jnp.float32)
        * HEAD_DIM ** (-0.5)
        + mask_bias
    )
    top_score = jnp.max(scores, axis=-1, keepdims=True)
    exponent = jnp.exp(scores - top_score)
    total = jnp.sum(exponent, axis=-1, keepdims=True)
    weights = exponent / total
    log_total = top_score + jnp.log(total)
    mixed_heads = jnp.einsum(
        einsum_forms[1],
        weights.astype(jnp.bfloat16),
        value_rows,
        preferred_element_type=jnp.float32,
    )
    return (mixed_heads.astype(jnp.bfloat16).reshape(-1, heads_dev * HEAD_DIM), log_total)


def attend_backward(projected, log_total, heads_grad, mask_bias, einsum_forms, streams, frames):
    queries, key_rows, value_rows, heads_dev = split_heads(projected, streams, frames)
    grad_heads = heads_grad.reshape(streams, frames, -1, heads_dev, HEAD_DIM)
    scale = HEAD_DIM ** (-0.5)
    scores = (
        jnp.einsum(einsum_forms[0], queries, key_rows, preferred_element_type=jnp.float32) * scale
        + mask_bias
    )
    weights = jnp.exp(scores - log_total)
    weights_grad = jnp.einsum(
        einsum_forms[0], grad_heads, value_rows, preferred_element_type=jnp.float32
    )
    inner = jnp.sum(weights * weights_grad, axis=-1, keepdims=True)
    score_grad = (weights * (weights_grad - inner)).astype(jnp.bfloat16)
    query_grad = (
        jnp.einsum(einsum_forms[1], score_grad, key_rows, preferred_element_type=jnp.float32)
        * scale
    ).astype(jnp.bfloat16)
    key_grad = (
        jnp.einsum(einsum_forms[2], score_grad, queries, preferred_element_type=jnp.float32) * scale
    ).astype(jnp.bfloat16)
    value_grad = jnp.einsum(
        einsum_forms[2],
        weights.astype(jnp.bfloat16),
        grad_heads,
        preferred_element_type=jnp.float32,
    ).astype(jnp.bfloat16)
    return jnp.stack([query_grad, key_grad, value_grad], axis=-2).reshape(projected.shape)


def block_forward(
    stream_in,
    ln_gain,
    ln_bias,
    w_qkv,
    w_out,
    w_up,
    w_down,
    mask_bias,
    einsum_forms,
    streams,
    frames,
):
    normed = layer_norm(stream_in, ln_gain[0], ln_bias[0]).astype(jnp.bfloat16)
    full_rows = norm_gather(normed)
    projected = jnp.dot(full_rows, w_qkv, preferred_element_type=jnp.float32).astype(jnp.bfloat16)
    mixed_heads, log_total = attend_forward(projected, mask_bias, einsum_forms, streams, frames)
    middle = stream_in + branch_scatter(mixed_heads, w_out)
    second = layer_norm(middle, ln_gain[1], ln_bias[1]).astype(jnp.bfloat16)
    second_full = norm_gather(second)
    hidden_pre = jnp.dot(second_full, w_up, preferred_element_type=jnp.float32)
    activated = jax.nn.gelu(hidden_pre).astype(jnp.bfloat16)
    result = middle + branch_scatter(activated, w_down)
    kept = (
        stream_in,
        full_rows,
        projected,
        mixed_heads,
        log_total,
        middle,
        second_full,
        hidden_pre,
        activated,
    )
    return (result, kept)


def block_backward(
    result_grad,
    kept,
    ln_gain,
    ln_bias,
    w_qkv,
    w_out,
    w_up,
    w_down,
    mask_bias,
    einsum_forms,
    streams,
    frames,
):
    (
        stream_in,
        first_store,
        projected,
        mixed_heads,
        log_total,
        middle,
        second_store,
        hidden_pre,
        activated,
    ) = kept
    result_low = result_grad.astype(jnp.bfloat16)
    gelu_pull = jax.vjp(jax.nn.gelu, hidden_pre)[1]
    down_in = grad_gather(result_low)
    grad_down = lax.dot_general(activated, down_in, ROWS_ONLY, preferred_element_type=jnp.float32)
    act_grad = lax.dot_general(down_in, w_down, COLS_ONLY, preferred_element_type=jnp.float32)
    hidden_grad = gelu_pull(act_grad)[0].astype(jnp.bfloat16)
    grad_up = weight_grad(second_store, hidden_grad)
    second_grad = input_scatter(hidden_grad, w_up)
    second_pull = jax.vjp(layer_norm, middle, ln_gain[1], ln_bias[1])[1]
    middle_part, gain_two, shift_two = second_pull(second_grad)
    middle_grad = result_grad + middle_part
    middle_low = middle_grad.astype(jnp.bfloat16)
    out_in = grad_gather(middle_low)
    grad_out = lax.dot_general(mixed_heads, out_in, ROWS_ONLY, preferred_element_type=jnp.float32)
    heads_grad = lax.dot_general(
        out_in, w_out, COLS_ONLY, preferred_element_type=jnp.float32
    ).astype(jnp.bfloat16)
    proj_grad = attend_backward(
        projected, log_total, heads_grad, mask_bias, einsum_forms, streams, frames
    )
    grad_qkv = weight_grad(first_store, proj_grad)
    first_grad = input_scatter(proj_grad, w_qkv)
    first_pull = jax.vjp(layer_norm, stream_in, ln_gain[0], ln_bias[0])[1]
    input_part, gain_one, shift_one = first_pull(first_grad)
    matrices = (grad_qkv, grad_out, grad_up, grad_down)
    return (
        middle_grad + input_part,
        matrices,
        jnp.stack([gain_one, gain_two]),
        jnp.stack([shift_one, shift_two]),
    )


def split_shards(tokens, out_grad, patch_valid, clip_ids, ln_gain, ln_bias, w_qkv, w_out, w_up, w_down):
    streams = patch_valid.shape[0]
    space_bias, time_bias = mask_biases(patch_valid, clip_ids)
    up_use, down_use = (w_up, w_down)
    weights = (w_qkv, w_out, up_use, down_use)
    layouts = ((streams, FRAMES, space_bias), (streams, FRAMES, time_bias))
    form_pair = (SPATIAL_FORMS, TEMPORAL_FORMS)
    state = tokens.astype(jnp.float32)
    kept_blocks = []
    for layer_index in range(2):
        group_count, frame_count, mask_bias = layouts[layer_index]
        state, kept = block_forward(
            state,
            ln_gain[layer_index],
            ln_bias[layer_index],
            weights[0][layer_index],
            weights[1][layer_index],
            weights[2][layer_index],
            weights[3][layer_index],
            mask_bias,
            form_pair[layer_index],
            group_count,
            frame_count,
        )
        kept_blocks.append(kept)
    layer_out = state.astype(jnp.bfloat16)
    grad_state = out_grad.astype(jnp.float32)
    matrix_grads = [None, None]
    gain_grads = [None, None]
    shift_grads = [None, None]
    for layer_index in (1, 0):
        group_count, frame_count, mask_bias = layouts[layer_index]
        grad_state, matrices, gain_part, shift_part = block_backward(
            grad_state,
            kept_blocks[layer_index],
            ln_gain[layer_index],
            ln_bias[layer_index],
            weights[0][layer_index],
            weights[1][layer_index],
            weights[2][layer_index],
            weights[3][layer_index],
            mask_bias,
            form_pair[layer_index],
            group_count,
            frame_count,
        )
        matrix_grads[layer_index] = matrices
        gain_grads[layer_index] = gain_part
        shift_grads[layer_index] = shift_part
    stacked = tuple(
        (jnp.stack([matrix_grads[0][item], matrix_grads[1][item]]) for item in range(4))
    )
    stacked = (
        lax.psum(stacked[0].astype(jnp.bfloat16), "dp").astype(jnp.float32),
        lax.psum(stacked[1].astype(jnp.bfloat16), "dp").astype(jnp.float32),
        lax.psum(stacked[2].astype(jnp.bfloat16), "dp").astype(jnp.float32),
        lax.psum(stacked[3].astype(jnp.bfloat16), "dp").astype(jnp.float32),
    )
    norm_sums = lax.psum((jnp.stack(gain_grads), jnp.stack(shift_grads)), ("dp", "mp"))
    return (
        layer_out,
        grad_state,
        norm_sums[0],
        norm_sums[1],
        stacked[0],
        stacked[1],
        stacked[2],
        stacked[3],
    )


def solution(mesh):
    dp, mp = mesh.shape["dp"], mesh.shape["mp"]
    if (dp, mp) != (16, 2):
        return on_mesh(split_shards, mesh, ("dp",), "mp")
    fine = Mesh(mesh.devices.reshape(4, 2, 2, 2), ("z", "y", "core", "mp"))
    return on_mesh(shards, fine, ("z", "y", "core"), "mp")


def on_mesh(body, mesh, dp, mp):
    both = dp + (mp,)
    return jax.shard_map(
        body,
        mesh=mesh,
        in_specs=(
            P(both, None),
            P(both, None),
            P(dp, None),
            P(dp, None),
            P(),
            P(),
            P(None, None, mp),
            P(None, mp, None),
            P(None, None, mp),
            P(None, mp, None),
        ),
        out_specs=(
            P(both, None),
            P(both, None),
            P(),
            P(),
            P(None, None, mp),
            P(None, mp, None),
            P(None, None, mp),
            P(None, mp, None),
        ),
        check_vma=False,
    )
```
